32 devices in a mesh: seq: 32 (over z, y, x, core).
Axes of the slice: x: 2, y: 2, z: 4, core: 2. Of those that a mesh axis runs over, the one named last changes fastest.
Arguments:
- tokens: bfloat16 [24576, 1280], P('seq'), may hold values from -6 to 6
- cotangent: bfloat16 [24576, 1280], P('seq'), may hold values from -6 to 6
- protein_lengths: int32 [24, 6], replicated, may hold values from 1 to 512, 1024 in all within a row
- w_in: float32 [1280, 640], P('seq'), may hold values from -0.15625 to 0.15625
- w_conv: float32 [5, 640, 640], P(None, 'seq'), may hold values from -0.109375 to 0.109375
- w_out: float32 [640, 1280], P('seq'), may hold values from -0.25 to 0.25
- vectors: float32 [7680], P('seq'), may hold values from -1.2 to 1.4, as said below
- mom_in: float32 [1280, 640], P('seq'), may hold values from -768 to 768
- mom_conv: float32 [5, 640, 640], P(None, 'seq'), may hold values from -768 to 768
- mom_out: float32 [640, 1280], P('seq'), may hold values from -768 to 768
- vec_mean: float32 [7680], P('seq'), may hold values from -112 to 112
- vec_square: float32 [7680], P('seq'), may hold values from 983.04 to 7372.8
Outputs:
- output: bfloat16 [24576, 1280], P('seq')
- input_grad: bfloat16 [24576, 1280], P('seq')
- grad_in: float32 [1280, 640], P('seq')
- grad_conv: float32 [5, 640, 640], P(None, 'seq')
- grad_out: float32 [640, 1280], P('seq')
- moment_in: float32 [1280, 640], P('seq')
- moment_conv: float32 [5, 640, 640], P(None, 'seq')
- moment_out: float32 [640, 1280], P('seq')
- new_in: float32 [1280, 640], P('seq')
- new_conv: float32 [5, 640, 640], P(None, 'seq')
- new_out: float32 [640, 1280], P('seq')
- vec_grad: float32 [7680], P('seq')
- vec_mean_new: float32 [7680], P('seq')
- vec_square_new: float32 [7680], P('seq')
- vec_new: float32 [7680], P('seq')
The draws below stay inside these ranges and needn't reach their ends.
Inputs may be any that keep to these rules, and one draw needn't show every extreme that they name: `protein_lengths`: in each row the 6 lengths sum to 1024 and the longest is exactly 512. `vectors`: the entries of the three gains lie near one, the biases and shifts are of both signs.
All inputs are finite; a program needn't handle non-finite values.
Results may differ from the reference program's by a relative error of at most 0.012.
Values may be sent and summed in bfloat16 or wider, within the bound.
No kernel may reach another device: no remote copies, remote signals or barrier semaphores. Data moves between devices by JAX's collectives and lax.ppermute only.
A program may use at most 256 MiB of HBM per device.

```python
import math
import jax
import jax.numpy as jnp
import numpy as np
from jax import lax

D = 1280
H = 640
KERNEL_TAPS = 5
DILATION_RATE = 128
LEN = 1024
PROTEINS = 6
NS_STEPS = 5
STEP = 10
TOKENS = 24576
ROWS = 24
NVEC = 7680


def draw_vectors(key, part):
    key = jax.random.fold_in(key, 11)
    gain_key, bias_key = jax.random.split(key)
    places = jnp.arange(NVEC)
    gains = 1.0 + jax.random.uniform(gain_key, (NVEC,), jnp.float32, -0.4, 0.4)
    biases = 0.3 * jax.random.truncated_normal(bias_key, -4.0, 4.0, (NVEC,), jnp.float32)
    is_gain = (places < D) | (places >= 3 * D + H) & (places < 3 * D + 2 * H) | (places >= 3 * D + 4 * H) & (places < 3 * D + 5 * H)
    return jnp.where(is_gain, gains, biases)


def level_of(own_key, shape, cuts, low, largest):
    level, own = 1.0, jax.random.fold_in(own_key, 6)
    for dim, shards_of in cuts:
        steps = jnp.exp(jax.random.uniform(jax.random.fold_in(own, dim), (shards_of,), jnp.float32, low / len(cuts), largest / len(cuts)))
        level = level * jnp.repeat(steps, shape[dim] // shards_of).reshape([-1 if axis == dim else 1 for axis in range(len(shape))])
    return level


def split_up(number_of, total, reach, lean):
    portions = [(1 << 20) // math.isqrt(standing ** lean) + 1 for standing in range(2, number_of + 1)]
    surplus, counts = total - reach - (number_of - 1), [1] * (number_of - 1)
    while surplus > 0:
        movable = [i for i in range(number_of - 1) if counts[i] < reach]
        pool, remaining = sum([portions[i] for i in movable]), surplus
        for i in movable:
            extra = min(reach - counts[i], max(1, remaining * portions[i] // pool), surplus)
            counts[i] = counts[i] + extra
            surplus = surplus - extra
    return np.array([reach] + counts)


def uneven(rng, count, total, reach, slope):
    if count == 2:
        one = jax.random.randint(rng, (), max(1, total - reach), min(reach, total - 1) + 1)
        return jnp.stack([one, total - one])
    sizes = jnp.asarray(split_up(count, total, reach, slope), jnp.int32)
    couples = (count - 1) // 2
    source_of, receiver = sizes[1:1 + 2 * couples:2], sizes[2:2 + 2 * couples:2]
    slack = jnp.minimum(source_of - 1, reach - receiver)
    moved = jax.random.randint(jax.random.fold_in(rng, 1), (couples,), 0, 1 << 20) % (slack + 1)
    sizes = sizes.at[1:1 + 2 * couples:2].set(source_of - moved).at[2:2 + 2 * couples:2].set(receiver + moved)
    return sizes[jax.random.permutation(jax.random.fold_in(rng, 2), count)]


def scatter_about(rng, extent, scale, limit, shards=(), held_as=jnp.bfloat16):
    drawn = scale * jax.random.normal(rng, extent, jnp.float32)
    if shards:
        drawn = drawn * level_of(rng, extent, shards, -0.22, 0.18)
    return jnp.clip(drawn, -limit, limit).astype(held_as)


def setup_inputs(seed: int = 0) -> dict:
    key_list = jax.random.split(jax.random.key(seed), 13)
    tokens = scatter_about(key_list[0], (TOKENS, D), 1.0, 6.0, ((0, 32),))
    cotangent = scatter_about(key_list[1], (TOKENS, D), 1.0, 6.0, ((0, 32),))
    protein_lengths = jax.vmap(lambda own: uneven(own, PROTEINS, LEN, LEN // 2, 2))(jax.random.split(key_list[2], ROWS)).reshape((ROWS, PROTEINS)).astype(jnp.int32)
    w_in = scatter_about(key_list[3], (D, H), D ** -0.5, 0.15625, ((0, 32),), jnp.float32)
    w_conv = scatter_about(key_list[4], (KERNEL_TAPS, H, H), (KERNEL_TAPS * H) ** -0.5, 0.109375, ((1, 32),), jnp.float32)
    w_out = scatter_about(key_list[5], (H, D), H ** -0.5, 0.25, ((0, 32),), jnp.float32)
    vectors = draw_vectors(jax.random.fold_in(key_list[12], 71), 0)
    mom_in = scatter_about(key_list[7], (D, H), (0.8 * TOKENS ** 0.5), 768.0, ((0, 32),), jnp.float32)
    mom_conv = scatter_about(key_list[8], (KERNEL_TAPS, H, H), (0.8 * TOKENS ** 0.5), 768.0, ((1, 32),), jnp.float32)
    mom_out = scatter_about(key_list[9], (H, D), (0.8 * TOKENS ** 0.5), 768.0, ((0, 32),), jnp.float32)
    vec_mean = scatter_about(key_list[10], (NVEC,), (0.11 * TOKENS ** 0.5), 112.0, ((0, 32),), jnp.float32)
    vec_square = jnp.clip(jnp.exp(math.log(7372.8) - 2.014903 * jax.random.uniform(key_list[11], (NVEC,), jnp.float32) ** level_of(key_list[11], (NVEC,), ((0, 32),), -0.2, 0.2)), 983.04, 7372.8)
    return dict(tokens=tokens, cotangent=cotangent, protein_lengths=protein_lengths, w_in=w_in, w_conv=w_conv, w_out=w_out, vectors=vectors, mom_in=mom_in, mom_conv=mom_conv, mom_out=mom_out, vec_mean=vec_mean, vec_square=vec_square)


@jax.custom_vjp
def low(v):
    return lax.optimization_barrier(v.astype(jnp.bfloat16)).astype(jnp.float32)

@jax.custom_vjp
def low_back(v):
    return v

def low_keep(v):
    return (low(v), None)

def low_pass(kept, grad):
    return (grad,)

def back_keep(v):
    return (v, None)

def back_low(kept, grad):
    return (low(grad),)
low.defvjp(low_keep, low_pass)
low_back.defvjp(back_keep, back_low)
eps_norm = 1e-05
coef_a = 3.4445
coef_b = -4.775
coef_c = 2.0315
momentum_decay = 0.95
muon_rate = 0.5
beta_one = 0.9
beta_two = 0.95
adam_rate = 0.2
adam_eps = 1e-08

def normalize(values):
    average = lax.optimization_barrier(jnp.mean(values, axis=-1, keepdims=True))
    centered = values - average
    variance = lax.optimization_barrier(jnp.mean(centered * centered, axis=-1, keepdims=True))
    return centered * lax.rsqrt(variance + eps_norm)

def front_piece(values, gain, shift):
    return jax.nn.gelu(normalize(values) * gain + shift, approximate=False)

def split_vectors(vectors):
    widths = [D, D, D, H, H, H, H, H, H]
    pieces = []
    start = 0
    for width in widths:
        pieces.append(vectors[start:start + width])
        start = start + width
    return pieces

def move_rows(values, start_offset, fill, axis):
    if start_offset == 0:
        return values
    length_here = values.shape[axis]
    filler_shape = list(values.shape)
    filler_shape[axis] = abs(start_offset)
    filler = jnp.full(filler_shape, fill, values.dtype)
    if start_offset > 0:
        kept = lax.slice_in_dim(values, start_offset, length_here, axis=axis)
        return jnp.concatenate([kept, filler], axis=axis)
    kept = lax.slice_in_dim(values, 0, length_here + start_offset, axis=axis)
    return jnp.concatenate([filler, kept], axis=axis)

def protein_ids(protein_lengths):
    row_ends = jnp.cumsum(protein_lengths, axis=1).astype(jnp.int32)
    places = jnp.arange(LEN, dtype=jnp.int32)
    local = lax.optimization_barrier(jnp.sum((places[None, :, None] >= row_ends[:, None, :]).astype(jnp.int32), axis=2))
    row_index = jnp.arange(protein_lengths.shape[0], dtype=jnp.int32)
    return (row_index[:, None] * protein_lengths.shape[1] + local).astype(jnp.int32)

def block_forward(inputs, params, ids):
    w_in, w_conv, w_out, vectors = params
    gain_one, shift_one, bias_out, bias_in, gain_two, shift_two, bias_conv, gain_three, shift_three = split_vectors(low(vectors))
    in_low = low(w_in)
    conv_low = low(w_conv)
    out_low = low(w_out)
    highest = lax.Precision.HIGHEST
    hidden_one = low(front_piece(inputs, gain_one, shift_one))
    first_out = low_back(jnp.einsum('bld,dh->blh', hidden_one, in_low, precision=highest) + bias_in)
    hidden_two = low_back(low(front_piece(first_out, gain_two, shift_two)))
    conv_sum = jnp.zeros(hidden_two.shape, jnp.float32) + bias_conv
    for kernel_tap_index in range(KERNEL_TAPS):
        start_offset = (kernel_tap_index - KERNEL_TAPS // 2) * DILATION_RATE
        shifted = move_rows(hidden_two, start_offset, 0.0, 1)
        moved_ids = move_rows(ids, start_offset, -1, 1)
        tap_mask = (moved_ids == ids).astype(jnp.float32)
        conv_sum = conv_sum + jnp.einsum('blh,hk->blk', shifted * tap_mask[:, :, None], conv_low[kernel_tap_index], precision=highest)
    second_out = low_back(low(conv_sum))
    hidden_three = low(front_piece(second_out, gain_three, shift_three))
    return inputs + jnp.einsum('blh,hd->bld', hidden_three, out_low, precision=highest) + bias_out

def add_trees(left, right):
    return jax.tree.map(jnp.add, left, right)

def orthogonalize(matrix):
    highest = lax.Precision.HIGHEST
    scaled = matrix / (jnp.sqrt(jnp.sum(matrix * matrix)) + 1e-07)
    flipped = scaled.shape[0] > scaled.shape[1]
    if flipped:
        scaled = scaled.T
    for iteration in range(NS_STEPS):
        gram = jnp.dot(scaled, scaled.T, precision=highest)
        poly = coef_b * gram + coef_c * jnp.dot(gram, gram, precision=highest)
        scaled = coef_a * scaled + jnp.dot(poly, scaled, precision=highest)
    if flipped:
        scaled = scaled.T
    return scaled

def reference(tokens, cotangent, protein_lengths, w_in, w_conv, w_out, vectors, mom_in, mom_conv, mom_out, vec_mean, vec_square):
    blocks = ROWS // 4
    ids = protein_ids(protein_lengths).reshape(blocks, 4, LEN)
    token_blocks = tokens.astype(jnp.float32).reshape(blocks, 4, LEN, D)
    back_blocks = cotangent.astype(jnp.float32).reshape(blocks, 4, LEN, D)
    params = (w_in, w_conv, w_out, vectors)

    def one_block(totals, items):
        inputs, backs, block_ids = items

        def forward(values, weights):
            return block_forward(values, weights, block_ids)
        result, pullback = jax.vjp(forward, inputs, params)
        grad_inputs, grad_params = pullback(backs)
        return (add_trees(totals, grad_params), (result.astype(jnp.bfloat16), grad_inputs.astype(jnp.bfloat16)))
    zeros = jax.tree.map(jnp.zeros_like, params)
    grads, (outputs, input_grads) = lax.scan(one_block, zeros, (token_blocks, back_blocks, ids))
    grad_in, grad_conv, grad_out, vec_grad = grads
    output = outputs.reshape(TOKENS, D)
    input_grad = input_grads.reshape(TOKENS, D)
    moment_in = momentum_decay * mom_in + grad_in
    moment_conv = momentum_decay * mom_conv + grad_conv
    moment_out = momentum_decay * mom_out + grad_out
    new_in = w_in - muon_rate * orthogonalize(moment_in)
    new_conv = w_conv - muon_rate * jnp.stack([orthogonalize(moment_conv[kernel_tap_index]) for kernel_tap_index in range(KERNEL_TAPS)])
    new_out = w_out - muon_rate * orthogonalize(moment_out)
    vec_mean_new = beta_one * vec_mean + (1.0 - beta_one) * vec_grad
    vec_square_new = beta_two * vec_square + (1.0 - beta_two) * vec_grad * vec_grad
    corrected_mean = vec_mean_new / (1.0 - beta_one ** STEP)
    corrected_square = vec_square_new / (1.0 - beta_two ** STEP)
    vec_new = vectors - adam_rate * corrected_mean / (jnp.sqrt(corrected_square) + adam_eps)
    return (output, input_grad, grad_in, grad_conv, grad_out, moment_in, moment_conv, moment_out, new_in, new_conv, new_out, vec_grad, vec_mean_new, vec_square_new, vec_new)
```

```python
import functools

import jax
import jax.numpy as jnp
import numpy as np
from jax import lax
from jax.experimental import pallas as pl
from jax.experimental.pallas import tpu as pltpu
from jax.sharding import PartitionSpec as P

D = 1280
H = 640
TAPS = 5
DILATION = 128
LEN = 1024
NS_STEPS = 5
STEP = 10
HALO = (TAPS // 2) * DILATION
CORES = 2
PLANE = 4
PIECES = CORES * PLANE
GROUPS = 8

EPS = 1e-05
COEF_A = 3.4445
COEF_B = -4.775
COEF_C = 2.0315
MOMENTUM = 0.95
MUON_RATE = 0.5
BETA_ONE = 0.9
BETA_TWO = 0.95
ADAM_RATE = 0.2
ADAM_EPS = 1e-08

F32 = jnp.float32
BF16 = jnp.bfloat16
NN = (((1,), (0,)), ((), ()))
NT = (((1,), (1,)), ((), ()))
TN = (((0,), (0,)), ((), ()))
INV_SQRT2 = 0.7071067811865476
INV_SQRT2PI = 0.3989422804014327
VMEM_LIMIT = 56 << 20

ANY = pl.BlockSpec(memory_space=pl.ANY)
VMEM = pl.BlockSpec(memory_space=pltpu.VMEM)
SMEM = pl.BlockSpec(memory_space=pltpu.SMEM)


def dot(left, right, dims=NN):
    return lax.dot_general(left, right, dims, preferred_element_type=F32)


def call(kernel, **kwargs):
    return pl.pallas_call(
        kernel,
        compiler_params=pltpu.CompilerParams(vmem_limit_bytes=VMEM_LIMIT),
        **kwargs,
    )


def shape(dims, dtype):
    return jax.ShapeDtypeStruct(dims, dtype)


def rows_spec(rows, width):
    return pl.BlockSpec((rows, width), lambda i: (i, 0))


def whole_spec(*dims):
    return pl.BlockSpec(dims, lambda i: (0,) * len(dims))


def front(values, gain, shift):
    average = jnp.mean(values, axis=-1, keepdims=True)
    centered = values - average
    scale = lax.rsqrt(jnp.mean(centered * centered, axis=-1, keepdims=True) + EPS)
    normal = centered * scale
    arg = normal * gain + shift
    below = 0.5 + 0.5 * lax.erf(arg * INV_SQRT2)
    slope = below + arg * (jnp.exp(-0.5 * arg * arg) * INV_SQRT2PI)
    return arg * below, normal, slope, scale


def front_back(incoming, gain, normal, slope, scale):
    d_arg = incoming * slope
    d_normal = d_arg * gain
    mean_one = jnp.mean(d_normal, axis=-1, keepdims=True)
    mean_two = jnp.mean(d_normal * normal, axis=-1, keepdims=True)
    grad = (d_normal - mean_one - normal * mean_two) * scale
    gain_grad = jnp.sum(d_arg * normal, axis=0, keepdims=True)
    shift_grad = jnp.sum(d_arg, axis=0, keepdims=True)
    return grad, gain_grad, shift_grad


def load_pieces(me_ref, pieces, held, sems):
    copies = []
    for core in range(CORES):
        for place in range(PLANE):
            number = core * PLANE + place
            copies.append(
                pltpu.make_async_copy(
                    pieces[number],
                    held.at[me_ref[0] ^ core, me_ref[1] ^ place],
                    sems.at[number],
                )
            )
    for copy in copies:
        copy.start()
    return copies


def front_one_kernel(tokens_ref, vec_ref, hidden_ref, normal_ref, slope_ref, scale_ref):
    hidden, normal, slope, scale = front(tokens_ref[...].astype(F32), vec_ref[0:1, :], vec_ref[1:2, :])
    hidden_ref[...] = hidden.astype(BF16)
    normal_ref[...] = normal.astype(BF16)
    slope_ref[...] = slope.astype(BF16)
    scale_ref[...] = scale


def first_kernel(nz, me_ref, hidden_ref, vec_ref, *refs):
    pieces, outs, (held, sems) = refs[:PIECES], refs[PIECES:-2], refs[-2:]
    weight_ref, two_ref, normal_ref, slope_ref, scale_ref = outs
    part = D // PIECES // nz

    @pl.when(pl.program_id(0) == 0)
    def _():
        for copy in load_pieces(me_ref, pieces, held, sems):
            copy.wait()
        blocks = [
            [held[core, place].astype(F32) for core in range(CORES)] for place in range(PLANE)
        ]
        for line in range(nz):
            rows = []
            for place in range(PLANE):
                for core in range(CORES):
                    rows.append(blocks[place][core][line * part : (line + 1) * part])
            length = part * PIECES
            weight_ref[line * length : (line + 1) * length, :] = jnp.concatenate(rows, axis=0).astype(BF16)

    first = dot(hidden_ref[...], weight_ref[...]) + vec_ref[0:1, :]
    hidden, normal, slope, scale = front(first, vec_ref[1:2, :], vec_ref[2:3, :])
    two_ref[...] = hidden.astype(BF16)
    normal_ref[...] = normal.astype(BF16)
    slope_ref[...] = slope.astype(BF16)
    scale_ref[...] = scale


def masked_tap(mask_ref, ext, start, rows, tap):
    values = ext[pl.ds(pl.multiple_of(start, DILATION), rows), :]
    if tap == TAPS // 2:
        return values
    return values * mask_ref[:, tap : tap + 1].astype(BF16)


def fill_ext(ext, local_ref, left_ref, right_ref, sems):
    rows = local_ref.shape[0]
    copies = [
        pltpu.make_async_copy(left_ref, ext.at[pl.ds(0, HALO)], sems.at[0]),
        pltpu.make_async_copy(local_ref, ext.at[pl.ds(HALO, rows)], sems.at[1]),
        pltpu.make_async_copy(right_ref, ext.at[pl.ds(HALO + rows, HALO)], sems.at[2]),
    ]
    for copy in copies:
        copy.start()
    return copies


def start_conv(me_ref, pieces, held, sems, ext, local_ref, left_ref, right_ref, ext_sems):
    @pl.when(pl.program_id(0) == 0)
    def _():
        copies = load_pieces(me_ref, pieces, held, sems)
        copies += fill_ext(ext, local_ref, left_ref, right_ref, ext_sems)
        for copy in copies:
            copy.wait()


def tap_weight(held, tap):
    return held[:, :, tap].reshape(H, H)


def second_kernel(me_ref, mask_ref, vec_ref, local_ref, left_ref, right_ref, *refs):
    pieces, outs, (held, sems, ext, ext_sems) = refs[:PIECES], refs[PIECES:-4], refs[-4:]
    three_ref, normal_ref, slope_ref, scale_ref = outs
    start_conv(me_ref, pieces, held, sems, ext, local_ref, left_ref, right_ref, ext_sems)
    rows = mask_ref.shape[0]
    total = vec_ref[3:4, :]
    for tap in range(TAPS):
        start = pl.program_id(0) * rows + tap * DILATION
        total = total + dot(masked_tap(mask_ref, ext, start, rows, tap), tap_weight(held, tap))
    second = total.astype(BF16).astype(F32)
    hidden, normal, slope, scale = front(second, vec_ref[4:5, :], vec_ref[5:6, :])
    three_ref[...] = hidden.astype(BF16)
    normal_ref[...] = normal.astype(BF16)
    slope_ref[...] = slope.astype(BF16)
    scale_ref[...] = scale


def back_second_kernel(me_ref, cot_ref, vec_ref, normal_ref, slope_ref, scale_ref, *refs):
    pieces, outs, (held, sems) = refs[:PIECES], refs[PIECES:-2], refs[-2:]
    weight_ref, back_ref, sums_ref = outs

    @pl.when(pl.program_id(0) == 0)
    def _():
        for copy in load_pieces(me_ref, pieces, held, sems):
            copy.wait()
        weight_ref[...] = held[...].reshape(H, D)
        sums_ref[...] = jnp.zeros_like(sums_ref)

    back_three = dot(cot_ref[...], weight_ref[...], NT)
    grad, gain_grad, shift_grad = front_back(
        back_three, vec_ref[4:5, :], normal_ref[...].astype(F32), slope_ref[...].astype(F32), scale_ref[...]
    )
    back = grad.astype(BF16)
    back_ref[...] = back
    sums_ref[0:1, :] += gain_grad
    sums_ref[1:2, :] += shift_grad
    sums_ref[2:3, :] += jnp.sum(back.astype(F32), axis=0, keepdims=True)


def output_kernel(tokens_ref, three_ref, weight_ref, vec_ref, output_ref):
    product = dot(three_ref[...], weight_ref[...])
    output_ref[...] = (tokens_ref[...].astype(F32) + product + vec_ref[2:3, :]).astype(BF16)


def place_rows(me_ref, held, tiles):
    for core in range(CORES):
        for place in range(PLANE):
            held[me_ref[0] ^ core, me_ref[1] ^ place] = tiles[core][place]


def grad_out_kernel(me_ref, three_ref, cot_ref, keep_ref, send_ref, sum_ref, held):
    cot = cot_ref[...]
    grad = dot(three_ref[...], cot, TN).astype(BF16)
    quarter = H // PIECES
    tiles = [
        [grad[(core * PLANE + place) * quarter : (core * PLANE + place + 1) * quarter] for place in range(PLANE)]
        for core in range(CORES)
    ]
    place_rows(me_ref, held, tiles)
    keep_ref[...] = held[0]
    send_ref[...] = held[1]
    sum_ref[...] = jnp.broadcast_to(jnp.sum(cot.astype(F32), axis=0, keepdims=True), sum_ref.shape)


def back_first_kernel(
    me_ref, mask_ref, vec_ref, normal_ref, slope_ref, scale_ref, local_ref, left_ref, right_ref, *refs
):
    pieces, outs, (held, sems, ext, ext_sems) = refs[:PIECES], refs[PIECES:-4], refs[-4:]
    back_ref, sums_ref = outs
    start_conv(me_ref, pieces, held, sems, ext, local_ref, left_ref, right_ref, ext_sems)

    @pl.when(pl.program_id(0) == 0)
    def _():
        sums_ref[...] = jnp.zeros_like(sums_ref)

    rows = mask_ref.shape[0]
    total = None
    for tap in range(TAPS):
        start = pl.program_id(0) * rows + tap * DILATION
        term = dot(masked_tap(mask_ref, ext, start, rows, tap), tap_weight(held, TAPS - 1 - tap), NT)
        total = term if total is None else total + term
    back_two = total.astype(BF16).astype(F32)
    grad, gain_grad, shift_grad = front_back(
        back_two, vec_ref[1:2, :], normal_ref[...].astype(F32), slope_ref[...].astype(F32), scale_ref[...]
    )
    back = grad.astype(BF16)
    back_ref[...] = back
    sums_ref[0:1, :] += gain_grad
    sums_ref[1:2, :] += shift_grad
    sums_ref[2:3, :] += jnp.sum(back.astype(F32), axis=0, keepdims=True)


def grad_in_kernel(nz, me_ref, one_ref, back_ref, keep_ref, send_ref, grad_ref, held):
    for start in range(0, H, 256):
        width = min(256, H - start)
        grad_ref[:, start : start + width] = dot(one_ref[...], back_ref[:, start : start + width], TN)
    part = D // PIECES // nz
    tiles = []
    for core in range(CORES):
        tiles.append([])
        for place in range(PLANE):
            rows = []
            for line in range(nz):
                first = ((line * PLANE + place) * CORES + core) * part
                rows.append(grad_ref[first : first + part, :])
            tiles[core].append(jnp.concatenate(rows, axis=0).astype(BF16))
    place_rows(me_ref, held, tiles)
    keep_ref[...] = held[0]
    send_ref[...] = held[1]


def grad_conv_kernel(me_ref, mask_ref, back_ref, local_ref, left_ref, right_ref, keep_ref, send_ref, held, ext, ext_sems):
    tap = pl.program_id(0)

    @pl.when(tap == 0)
    def _():
        for copy in fill_ext(ext, local_ref, left_ref, right_ref, ext_sems):
            copy.wait()

    rows = back_ref.shape[0]
    values = ext[pl.ds(pl.multiple_of(tap * DILATION, DILATION), rows), :]
    values = values * mask_ref[0].astype(BF16)
    grad = dot(values, back_ref[...], TN).astype(BF16)
    quarter = H // PIECES
    tiles = [
        [grad[(core * PLANE + place) * quarter : (core * PLANE + place + 1) * quarter] for place in range(PLANE)]
        for core in range(CORES)
    ]
    place_rows(me_ref, held, tiles)
    keep_ref[:, 0] = held[0]
    send_ref[:, 0] = held[1]


def input_grad_kernel(back_ref, weight_ref, vec_ref, normal_ref, slope_ref, scale_ref, cot_ref, grad_ref, sums_ref):
    @pl.when(pl.program_id(0) == 0)
    def _():
        sums_ref[...] = jnp.zeros_like(sums_ref)

    back_one = dot(back_ref[...], weight_ref[...], NT)
    grad, gain_grad, shift_grad = front_back(
        back_one, vec_ref[0:1, :], normal_ref[...].astype(F32), slope_ref[...].astype(F32), scale_ref[...]
    )
    grad_ref[...] = (cot_ref[...].astype(F32) + grad).astype(BF16)
    sums_ref[0:1, :] += gain_grad
    sums_ref[1:2, :] += shift_grad


def line_kernel(nz, widths, me_ref, *refs):
    shards, out_refs, held = refs[:nz], refs[nz:-1], refs[-1]
    for number in range(nz):
        held[number] = shards[number][...]
    blocks = [held[me_ref[2] ^ line].astype(F32) for line in range(nz)]
    start = 0
    for out_ref, (groups, rows) in zip(out_refs, widths):
        for group in range(groups):
            stop = start + rows
            joined = jnp.concatenate([block[start:stop] for block in blocks], axis=0).astype(BF16)
            if groups == 1:
                out_ref[...] = joined
            else:
                out_ref[group] = joined
            start = stop


def newton_schulz(x_ref, low_ref, gram_ref, poly_ref, own):
    size, width = x_ref.shape
    square = jnp.sum(x_ref[...] * x_ref[...])
    factor = 1.0 / (jnp.sqrt(square) + 1e-07)
    x_ref[...] = x_ref[...] * factor
    low_ref[...] = x_ref[...].astype(BF16)
    square = square * factor * factor
    for step in range(NS_STEPS):
        shift = square * (1.0 / size)
        for start in range(0, size, 256):
            span = min(256, size - start)
            gram = dot(low_ref[...], low_ref[start : start + span, :], NT)
            row = lax.broadcasted_iota(jnp.int32, (size, span), 0)
            column = lax.broadcasted_iota(jnp.int32, (size, span), 1) + start
            gram_ref[:, start : start + span] = gram - jnp.where(row == column, shift, 0.0)
        gram_low = gram_ref[...].astype(BF16)
        linear = COEF_B + 2.0 * COEF_C * shift
        for start in range(0, size, 256):
            span = min(256, size - start)
            squared = dot(gram_low, gram_low[:, start : start + span])
            poly_ref[:, start : start + span] = (
                linear * gram_ref[:, start : start + span] + COEF_C * squared
            ).astype(BF16)
        coefficient = COEF_A + COEF_B * shift + COEF_C * shift * shift
        if step == NS_STEPS - 1:
            own(coefficient)
            return
        square = jnp.zeros((), F32)
        for start in range(0, width, 256):
            span = min(256, width - start)
            fresh = coefficient * x_ref[:, start : start + span] + dot(
                poly_ref[...], low_ref[:, start : start + span]
            )
            square = square + jnp.sum(fresh * fresh)
            x_ref[:, start : start + span] = fresh
        low_ref[...] = x_ref[...].astype(BF16)


def orth_in_kernel(*refs):
    pieces, out_ref, (held, x_ref, low_ref, gram_ref, poly_ref) = refs[:PIECES], refs[PIECES], refs[-5:]
    rows = D // PIECES
    for number in range(PIECES):
        held[number * rows : (number + 1) * rows, :] = pieces[number][...].astype(F32)
    for start in range(0, D, 256):
        x_ref[:, start : start + 256] = held[start : start + 256, :].T

    def own(coefficient):
        fresh = coefficient * x_ref[:, 0:256] + dot(poly_ref[...], low_ref[:, 0:256])
        out_ref[...] = fresh.T[0:rows]

    newton_schulz(x_ref, low_ref, gram_ref, poly_ref, own)


def orth_out_kernel(*refs):
    pieces, out_ref, (x_ref, low_ref, gram_ref, poly_ref) = refs[:PIECES], refs[PIECES], refs[-4:]
    rows = H // PIECES
    for number in range(PIECES):
        x_ref[number * rows : (number + 1) * rows, :] = pieces[number][...].astype(F32)

    def own(coefficient):
        out_ref[...] = coefficient * x_ref[0:rows, :] + dot(poly_ref[0:rows, :], low_ref[...])

    newton_schulz(x_ref, low_ref, gram_ref, poly_ref, own)


def orth_conv_kernel(members, me_ref, blocks_ref, out_ref, x_ref, low_ref, gram_ref, poly_ref):
    part = blocks_ref.shape[1]
    rows = GROUPS * part
    for number in range(members):
        member = me_ref[3] ^ number
        joined = jnp.concatenate(
            [blocks_ref[group * members + member].astype(F32) for group in range(GROUPS)], axis=0
        )
        x_ref[number * rows : (number + 1) * rows, :] = joined

    def own(coefficient):
        fresh = coefficient * x_ref[0:rows, :] + dot(poly_ref[0:rows, :], low_ref[...])
        for group in range(GROUPS):
            out_ref[group] = fresh[group * part : (group + 1) * part].astype(BF16)

    newton_schulz(x_ref, low_ref, gram_ref, poly_ref, own)


class Layout:
    def __init__(self, count):
        self.count = count
        self.lines = count // PIECES
        self.part = H // count
        self.members = count // GROUPS
        places = np.arange(H)
        row = places % self.part
        line = places // self.part % self.lines
        plane = places // (self.part * self.lines) % PLANE
        core = places // (self.part * self.lines * PLANE)
        self.natural = ((line * PLANE + plane) * CORES + core) * self.part + row

    def swap(self, values, mask):
        return lax.ppermute(values, "seq", [(one, one ^ mask) for one in range(self.count)])

    def swap_line(self, values, step):
        return self.swap(values, step * PIECES)

    def swap_plane(self, values, step):
        return self.swap(values, step * CORES)

    def along_line(self, values):
        return [values] + [self.swap_line(values, step) for step in range(1, self.lines)]

    def to_all(self, values):
        plane = [values] + [self.swap_plane(values, step) for step in range(1, PLANE)]
        return plane + [self.swap(piece, 1) for piece in plane]

    def shard_sum(self, keep, send, line_of):
        other = self.swap(send, 1)
        total = keep[0].astype(F32) + other[0].astype(F32)
        for step in range(1, PLANE):
            partial = (keep[step].astype(F32) + other[step].astype(F32)).astype(BF16)
            total = total + self.swap_plane(partial, step).astype(F32)
        result = line_of(total, 0)
        for step in range(1, self.lines):
            result = result + self.swap_line(line_of(total, step).astype(BF16), step).astype(F32)
        return result


def front_outs(rows, width):
    return [shape((rows, width), BF16)] * 3 + [shape((rows, 1), F32)]


def front_out_specs(rows, width):
    return [rows_spec(rows, width)] * 3 + [rows_spec(rows, 1)]


def body(
    count,
    tokens,
    cotangent,
    protein_lengths,
    w_in,
    w_conv,
    w_out,
    vectors,
    mom_in,
    mom_conv,
    mom_out,
    vec_mean,
    vec_square,
):
    lay = Layout(count)
    index = lax.axis_index("seq")
    core, plane, line, member = index & 1, (index >> 1) & (PLANE - 1), index // PIECES, index % lay.members
    me = jnp.stack([core, plane, line, member]).astype(jnp.int32)
    rows = tokens.shape[0]
    block = 256
    grid = (rows // block,)
    quarter = H // PIECES
    piece_in = D // PIECES
    natural = jnp.asarray(lay.natural, jnp.int32)
    to_order = (jnp.arange(H, dtype=jnp.int32)[:, None] == natural[None, :]).astype(BF16)

    def order_low(values):
        return jnp.dot(values, to_order, preferred_element_type=F32).astype(BF16)

    def unorder(values):
        return lax.dot_general(
            values, to_order.astype(F32), NT, precision=lax.Precision.HIGHEST, preferred_element_type=F32
        )

    vec_low = vectors.astype(BF16)
    vec_all = lax.all_to_all(
        jnp.broadcast_to(vec_low[None, :], (count, vec_low.shape[0])), "seq", split_axis=0, concat_axis=0, tiled=True
    ).reshape(-1)
    vec_d = vec_all[: 3 * D].reshape(3, D).astype(F32)
    vec_h = order_low(vec_all[3 * D :].reshape(6, H)).astype(F32)

    in_line = lay.along_line(order_low(w_in.astype(BF16)))
    part = lay.part
    in_own = call(
        functools.partial(line_kernel, lay.lines, [(1, D // count)]),
        out_shape=[shape((piece_in, H), BF16)],
        in_specs=[SMEM] + [VMEM] * lay.lines,
        out_specs=[VMEM],
        scratch_shapes=[pltpu.VMEM((lay.lines, D // count, H), BF16)],
    )(me, *in_line)[0]
    in_pieces = lay.to_all(in_own)
    conv_line = lay.along_line(order_low(w_conv.reshape(TAPS * part, H).astype(BF16)))
    conv_own = call(
        functools.partial(line_kernel, lay.lines, [(TAPS, part)]),
        out_shape=[shape((TAPS, quarter, H), BF16)],
        in_specs=[SMEM] + [VMEM] * lay.lines,
        out_specs=[VMEM],
        scratch_shapes=[pltpu.VMEM((lay.lines, TAPS * part, H), BF16)],
    )(me, *conv_line)[0]
    conv_pieces = lay.to_all(conv_own)
    out_line = lay.along_line(w_out.astype(BF16))
    out_own = call(
        functools.partial(line_kernel, lay.lines, [(1, part)]),
        out_shape=[shape((quarter, D), BF16)],
        in_specs=[SMEM] + [VMEM] * lay.lines,
        out_specs=[VMEM],
        scratch_shapes=[pltpu.VMEM((lay.lines, part, D), BF16)],
    )(me, *out_line)[0]
    out_pieces = lay.to_all(out_own)

    row_ends = jnp.cumsum(protein_lengths, axis=1) + jnp.arange(protein_lengths.shape[0], dtype=jnp.int32)[:, None] * LEN
    places = index * rows - HALO + jnp.arange(rows + 2 * HALO, dtype=jnp.int32)
    ids = jnp.sum((places[:, None] >= row_ends.reshape(1, -1)).astype(jnp.int32), axis=1)
    ids = jnp.where(places < 0, -1, ids)
    own_ids = ids[HALO : HALO + rows]
    masks = jnp.stack(
        [(ids[tap * DILATION : tap * DILATION + rows] == own_ids).astype(F32) for tap in range(TAPS)]
    )
    mask_rows = masks.T
    mask_taps = masks[:, :, None]

    edges = [one for one in range(count - 1) if (one + 1) * rows % LEN != 0]

    def halos(values):
        left = lax.ppermute(values[rows - HALO :], "seq", [(one, one + 1) for one in edges])
        right = lax.ppermute(values[:HALO], "seq", [(one + 1, one) for one in edges])
        return left, right

    one_low, normal_one, slope_one, scale_one = call(
        front_one_kernel,
        grid=grid,
        out_shape=front_outs(rows, D),
        in_specs=[rows_spec(block, D), whole_spec(3, D)],
        out_specs=front_out_specs(block, D),
    )(tokens, vec_d)
    in_low, two_low, normal_two, slope_two, scale_two = call(
        functools.partial(first_kernel, lay.lines),
        grid=grid,
        out_shape=[shape((D, H), BF16)] + front_outs(rows, H),
        in_specs=[SMEM, rows_spec(block, D), whole_spec(6, H)] + [ANY] * PIECES,
        out_specs=[whole_spec(D, H)] + front_out_specs(block, H),
        scratch_shapes=[pltpu.VMEM((CORES, PLANE, piece_in, H), BF16), pltpu.SemaphoreType.DMA((PIECES,))],
    )(me, one_low, vec_h, *in_pieces)
    two_left, two_right = halos(two_low)
    conv_scratch = [
        pltpu.VMEM((CORES, PLANE, TAPS, quarter, H), BF16),
        pltpu.SemaphoreType.DMA((PIECES,)),
        pltpu.VMEM((rows + 2 * HALO, H), BF16),
        pltpu.SemaphoreType.DMA((3,)),
    ]
    three_low, normal_three, slope_three, scale_three = call(
        second_kernel,
        grid=grid,
        out_shape=front_outs(rows, H),
        in_specs=[SMEM, rows_spec(block, TAPS), whole_spec(6, H)] + [ANY] * (3 + PIECES),
        out_specs=front_out_specs(block, H),
        scratch_shapes=conv_scratch,
    )(me, mask_rows, vec_h, two_low, two_left, two_right, *conv_pieces)

    out_low, back_second, sums_three = call(
        back_second_kernel,
        grid=grid,
        out_shape=[shape((H, D), BF16), shape((rows, H), BF16), shape((8, H), F32)],
        in_specs=[SMEM, rows_spec(block, D), whole_spec(6, H), rows_spec(block, H), rows_spec(block, H), rows_spec(block, 1)]
        + [ANY] * PIECES,
        out_specs=[whole_spec(H, D), rows_spec(block, H), whole_spec(8, H)],
        scratch_shapes=[pltpu.VMEM((CORES, PLANE, quarter, D), BF16), pltpu.SemaphoreType.DMA((PIECES,))],
    )(me, cotangent, vec_h, normal_three, slope_three, scale_three, *out_pieces)
    back_left, back_right = halos(back_second)
    keep_out, send_out, sum_cot = call(
        grad_out_kernel,
        grid=(D // 256,),
        out_shape=[shape((PLANE, quarter, D), BF16)] * 2 + [shape((8, D), F32)],
        in_specs=[SMEM, whole_spec(rows, H), pl.BlockSpec((rows, 256), lambda i: (0, i))],
        out_specs=[pl.BlockSpec((PLANE, quarter, 256), lambda i: (0, 0, i))] * 2 + [pl.BlockSpec((8, 256), lambda i: (0, i))],
        scratch_shapes=[pltpu.VMEM((CORES, PLANE, quarter, 256), BF16)],
    )(me, three_low, cotangent)
    output = call(
        output_kernel,
        grid=grid,
        out_shape=shape((rows, D), BF16),
        in_specs=[rows_spec(block, D), rows_spec(block, H), whole_spec(H, D), whole_spec(3, D)],
        out_specs=rows_spec(block, D),
    )(tokens, three_low, out_low, vec_d)
    keep_conv, send_conv = call(
        grad_conv_kernel,
        grid=(TAPS,),
        out_shape=[shape((PLANE, TAPS, quarter, H), BF16)] * 2,
        in_specs=[SMEM, pl.BlockSpec((1, rows, 1), lambda i: (i, 0, 0)), whole_spec(rows, H)] + [ANY] * 3,
        out_specs=[pl.BlockSpec((PLANE, 1, quarter, H), lambda i: (0, i, 0, 0))] * 2,
        scratch_shapes=[
            pltpu.VMEM((CORES, PLANE, quarter, H), BF16),
            pltpu.VMEM((rows + 2 * HALO, H), BF16),
            pltpu.SemaphoreType.DMA((3,)),
        ],
    )(me, mask_taps, back_second, two_low, two_left, two_right)
    back_first, sums_two = call(
        back_first_kernel,
        grid=grid,
        out_shape=[shape((rows, H), BF16), shape((8, H), F32)],
        in_specs=[SMEM, rows_spec(block, TAPS), whole_spec(6, H), rows_spec(block, H), rows_spec(block, H), rows_spec(block, 1)]
        + [ANY] * (3 + PIECES),
        out_specs=[rows_spec(block, H), whole_spec(8, H)],
        scratch_shapes=conv_scratch,
    )(me, mask_rows, vec_h, normal_two, slope_two, scale_two, back_second, back_left, back_right, *conv_pieces)
    keep_in, send_in = call(
        functools.partial(grad_in_kernel, lay.lines),
        out_shape=[shape((PLANE, piece_in, H), BF16)] * 2,
        in_specs=[SMEM, VMEM, VMEM],
        out_specs=[VMEM] * 2,
        scratch_shapes=[pltpu.VMEM((D, H), F32), pltpu.VMEM((CORES, PLANE, piece_in, H), BF16)],
    )(me, one_low, back_first)
    input_grad, sums_one = call(
        input_grad_kernel,
        grid=grid,
        out_shape=[shape((rows, D), BF16), shape((8, D), F32)],
        in_specs=[
            rows_spec(block, H),
            whole_spec(D, H),
            whole_spec(3, D),
            rows_spec(block, D),
            rows_spec(block, D),
            rows_spec(block, 1),
            rows_spec(block, D),
        ],
        out_specs=[rows_spec(block, D), whole_spec(8, D)],
    )(back_first, in_low, vec_d, normal_one, slope_one, scale_one, cotangent)

    def line_rows(values, step):
        width = values.shape[-1]
        split = values.reshape(-1, lay.lines, values.shape[-2] // lay.lines, width)
        return lax.dynamic_index_in_dim(split, line ^ step, axis=1, keepdims=False)

    sum_out = lay.shard_sum(keep_out, send_out, line_rows)[0]
    sum_conv = lay.shard_sum(keep_conv, send_conv, line_rows)
    sum_in = lay.shard_sum(keep_in, send_in, line_rows)[0]
    sum_conv = unorder(sum_conv.reshape(TAPS * part, H)).reshape(TAPS, part, H)
    sum_in = unorder(sum_in)
    hidden_sums = unorder(
        jnp.stack([sums_two[2], sums_two[0], sums_two[1], sums_three[2], sums_three[0], sums_three[1]])
    )
    vec_terms = jnp.concatenate([sums_one[0], sums_one[1], sum_cot[0], hidden_sums.reshape(-1)])
    sum_vec = jnp.sum(
        lax.all_to_all(vec_terms.reshape(count, -1), "seq", split_axis=0, concat_axis=0, tiled=True), axis=0
    )

    moment_in = MOMENTUM * mom_in + sum_in
    moment_conv = MOMENTUM * mom_conv + sum_conv
    moment_out = MOMENTUM * mom_out + sum_out

    def orth_scratch(width):
        return [
            pltpu.VMEM((H, width), F32),
            pltpu.VMEM((H, width), BF16),
            pltpu.VMEM((H, H), F32),
            pltpu.VMEM((H, H), BF16),
        ]

    out_pieces_m = lay.to_all(jnp.concatenate(lay.along_line(moment_out.astype(BF16)), axis=0))
    orth_out = call(
        orth_out_kernel,
        out_shape=shape((quarter, D), F32),
        in_specs=[VMEM] * PIECES,
        out_specs=VMEM,
        scratch_shapes=orth_scratch(D),
    )(*out_pieces_m)[:part]
    moment_low = jnp.concatenate(
        [moment_conv.astype(BF16), jnp.zeros((GROUPS - TAPS, part, H), BF16)], axis=0
    )
    moment_blocks = lax.all_to_all(
        jnp.broadcast_to(moment_low[:, None], (GROUPS, lay.members, part, H)).reshape(count, part, H),
        "seq",
        split_axis=0,
        concat_axis=0,
        tiled=True,
    )
    conv_blocks = call(
        functools.partial(orth_conv_kernel, lay.members),
        out_shape=shape((GROUPS, part, H), BF16),
        in_specs=[SMEM, VMEM],
        out_specs=VMEM,
        scratch_shapes=orth_scratch(H),
    )(me, moment_blocks)
    orth_conv = lax.all_to_all(
        conv_blocks,
        "seq",
        split_axis=0,
        concat_axis=0,
        tiled=True,
        axis_index_groups=[[group * lay.members + one for group in range(GROUPS)] for one in range(lay.members)],
    )[:TAPS].astype(F32)
    in_pieces_m = lay.to_all(jnp.concatenate(lay.along_line(moment_in.astype(BF16)), axis=0))
    orth_in = call(
        orth_in_kernel,
        out_shape=shape((piece_in, H), F32),
        in_specs=[VMEM] * PIECES,
        out_specs=VMEM,
        scratch_shapes=[pltpu.VMEM((D, H), F32)] + orth_scratch(D),
    )(*in_pieces_m)[: D // count]
    new_in = w_in - MUON_RATE * orth_in
    new_conv = w_conv - MUON_RATE * orth_conv
    new_out = w_out - MUON_RATE * orth_out

    vec_mean_new = BETA_ONE * vec_mean + (1.0 - BETA_ONE) * sum_vec
    vec_square_new = BETA_TWO * vec_square + (1.0 - BETA_TWO) * sum_vec * sum_vec
    corrected_mean = vec_mean_new / (1.0 - BETA_ONE**STEP)
    corrected_square = vec_square_new / (1.0 - BETA_TWO**STEP)
    vec_new = vectors - ADAM_RATE * corrected_mean / (jnp.sqrt(corrected_square) + ADAM_EPS)
    return (
        output,
        input_grad,
        sum_in,
        sum_conv,
        sum_out,
        moment_in,
        moment_conv,
        moment_out,
        new_in,
        new_conv,
        new_out,
        sum_vec,
        vec_mean_new,
        vec_square_new,
        vec_new,
    )


def solution(mesh):
    matrix, taps, vector = P("seq", None), P(None, "seq", None), P("seq")
    return jax.shard_map(
        functools.partial(body, mesh.shape["seq"]),
        mesh=mesh,
        in_specs=(matrix, matrix, P(), matrix, taps, matrix, vector, matrix, taps, matrix, vector, vector),
        out_specs=(
            matrix,
            matrix,
            matrix,
            taps,
            matrix,
            matrix,
            taps,
            matrix,
            matrix,
            taps,
            matrix,
            vector,
            vector,
            vector,
            vector,
        ),
        check_vma=False,
    )
```

```python
import functools

import jax
import jax.numpy as jnp
import numpy as np
from jax import lax
from jax.experimental import pallas as pl
from jax.experimental.pallas import tpu as pltpu
from jax.sharding import PartitionSpec as P

D = 1280
H = 640
TAPS = 5
DILATION = 128
LEN = 1024
NS_STEPS = 5
STEP = 10
HALO = (TAPS // 2) * DILATION
CORES = 2
PLANE = 4
PIECES = CORES * PLANE
PAIRS = PIECES // 2
UNITS = 2
SLOTS = 4
SLOT_IN = 1
SLOT_OUT = 2
TAP_UNITS = ((0, 0), (0, 1), (1, 1), (3, 0), (3, 1))

EPS = 1e-05
COEF_A = 3.4445
COEF_B = -4.775
COEF_C = 2.0315
MOMENTUM = 0.95
MUON_RATE = 0.5
BETA_ONE = 0.9
BETA_TWO = 0.95
ADAM_RATE = 0.2
ADAM_EPS = 1e-08

F32 = jnp.float32
BF16 = jnp.bfloat16
NN = (((1,), (0,)), ((), ()))
NT = (((1,), (1,)), ((), ()))
TN = (((0,), (0,)), ((), ()))
INV_SQRT2 = 0.7071067811865476
INV_SQRT2PI = 0.3989422804014327
VMEM_LIMIT = 56 << 20
RELATIVE = 0.05

ANY = pl.BlockSpec(memory_space=pl.ANY)
VMEM = pl.BlockSpec(memory_space=pltpu.VMEM)
SMEM = pl.BlockSpec(memory_space=pltpu.SMEM)


def dot(left, right, dims=NN):
    return lax.dot_general(left, right, dims, preferred_element_type=F32)


def call(kernel, micros, **kwargs):
    return pl.pallas_call(
        kernel,
        name=getattr(kernel, "func", kernel).__name__,
        cost_estimate=pl.CostEstimate(flops=int(micros * RELATIVE * 1e9), bytes_accessed=int(micros * RELATIVE * 1e6), transcendentals=0),
        compiler_params=pltpu.CompilerParams(vmem_limit_bytes=VMEM_LIMIT),
        **kwargs,
    )


def tie(*values):
    return lax.optimization_barrier(values)


def shape(dims, dtype):
    return jax.ShapeDtypeStruct(dims, dtype)


def rows_spec(rows, width):
    return pl.BlockSpec((rows, width), lambda i: (i, 0))


def whole_spec(*dims):
    return pl.BlockSpec(dims, lambda i: (0,) * len(dims))


def front(values, gain, shift):
    average = jnp.mean(values, axis=-1, keepdims=True)
    centered = values - average
    scale = lax.rsqrt(jnp.mean(centered * centered, axis=-1, keepdims=True) + EPS)
    normal = centered * scale
    arg = normal * gain + shift
    below = 0.5 + 0.5 * lax.erf(arg * INV_SQRT2)
    slope = below + arg * (jnp.exp(-0.5 * arg * arg) * INV_SQRT2PI)
    return arg * below, normal, slope, scale


def front_back(incoming, gain, normal, slope, scale):
    d_arg = incoming * slope
    d_normal = d_arg * gain
    mean_one = jnp.mean(d_normal, axis=-1, keepdims=True)
    mean_two = jnp.mean(d_normal * normal, axis=-1, keepdims=True)
    grad = (d_normal - mean_one - normal * mean_two) * scale
    gain_grad = jnp.sum(d_arg * normal, axis=0, keepdims=True)
    shift_grad = jnp.sum(d_arg, axis=0, keepdims=True)
    return grad, gain_grad, shift_grad


def load_pieces(me_ref, pieces, held, sems):
    copies = []
    for other in range(CORES):
        core = me_ref[0] ^ other
        for number in range(PLANE):
            place = (0, 1 + core, 2 - core, 3)[number]
            copies.append(
                pltpu.make_async_copy(
                    pieces[2 * other + number // 2].at[number % 2], held.at[core, me_ref[1] ^ place], sems.at[other * PLANE + number]
                )
            )
    for copy in copies:
        copy.start()
    return copies


def front_one_kernel(
    tokens_ref, left_ref, right_ref, vec_ref, hidden_ref, normal_ref, slope_ref, scale_ref, halo_ref
):
    step = pl.program_id(0)
    values = jnp.where(step == 0, left_ref[...], jnp.where(step == 1, right_ref[...], tokens_ref[...]))
    hidden, normal, slope, scale = front(values.astype(F32), vec_ref[0:1, :], vec_ref[1:2, :])
    hidden_ref[...] = hidden.astype(BF16)
    normal_ref[...] = normal.astype(BF16)
    slope_ref[...] = slope.astype(BF16)
    scale_ref[...] = scale

    @pl.when(step < 2)
    def _():
        halo_ref[...] = hidden.astype(BF16)


def first_kernel(nz, me_ref, hidden_ref, halo_ref, vec_ref, *refs):
    pieces, outs, (held, sems) = refs[:PAIRS], refs[PAIRS:-2], refs[-2:]
    weight_ref, two_ref, normal_ref, slope_ref, scale_ref, left_ref, right_ref = outs
    part = D // PIECES // nz
    step = pl.program_id(0)

    @pl.when(step == 0)
    def _():
        for copy in load_pieces(me_ref, pieces, held, sems):
            copy.wait()
        blocks = [
            [held[core, place].astype(F32) for core in range(CORES)] for place in range(PLANE)
        ]
        for line in range(nz):
            rows = []
            for place in range(PLANE):
                for core in range(CORES):
                    rows.append(blocks[place][core][line * part : (line + 1) * part])
            length = part * PIECES
            weight_ref[line * length : (line + 1) * length, :] = jnp.concatenate(rows, axis=0).astype(BF16)

    values = jnp.where(step < 2, halo_ref[...], hidden_ref[...])
    first = dot(values, weight_ref[...]) + vec_ref[0:1, :]
    hidden, normal, slope, scale = front(first, vec_ref[1:2, :], vec_ref[2:3, :])
    two_ref[...] = hidden.astype(BF16)
    normal_ref[...] = normal.astype(BF16)
    slope_ref[...] = slope.astype(BF16)
    scale_ref[...] = scale

    @pl.when(step == 0)
    def _():
        left_ref[...] = hidden.astype(BF16)

    @pl.when(step == 1)
    def _():
        right_ref[...] = hidden.astype(BF16)


def mask_kernel(me_ref, ends_ref, mask_ref):
    rows = mask_ref.shape[0]
    first = me_ref[4] - HALO
    place = lax.broadcasted_iota(jnp.int32, (rows + 2 * HALO, 1), 0) + first
    ids = jnp.sum((place >= ends_ref[...]).astype(F32), axis=1, keepdims=True)
    ids = jnp.where(place < 0, -1.0, ids)
    column = lax.broadcasted_iota(jnp.int32, mask_ref.shape, 1)
    mask = jnp.zeros(mask_ref.shape, F32)
    for tap in range(TAPS):
        same = ids[tap * DILATION : tap * DILATION + rows] == ids[HALO : HALO + rows]
        mask = mask + jnp.where((column == tap) & same, 1.0, 0.0)
    mask_ref[...] = mask


def masked_tap(mask_ref, ext, start, rows, tap):
    values = ext[pl.ds(pl.multiple_of(start, DILATION), rows), :]
    if tap == TAPS // 2:
        return values
    return values * mask_ref[:, tap : tap + 1].astype(BF16)


def fill_ext(ext, local_ref, left_ref, right_ref, sems):
    rows = local_ref.shape[0]
    copies = [
        pltpu.make_async_copy(left_ref, ext.at[pl.ds(0, HALO)], sems.at[0]),
        pltpu.make_async_copy(local_ref, ext.at[pl.ds(HALO, rows)], sems.at[1]),
        pltpu.make_async_copy(right_ref, ext.at[pl.ds(HALO + rows, HALO)], sems.at[2]),
    ]
    for copy in copies:
        copy.start()
    return copies


def start_conv(me_ref, pieces, held, sems, ext, local_ref, left_ref, right_ref, ext_sems):
    @pl.when(pl.program_id(0) == 0)
    def _():
        copies = load_pieces(me_ref, pieces, held, sems)
        copies += fill_ext(ext, local_ref, left_ref, right_ref, ext_sems)
        for copy in copies:
            copy.wait()


def tap_weight(held, tap):
    return held[:, :, tap].reshape(H, H)


def second_kernel(me_ref, mask_ref, vec_ref, local_ref, left_ref, right_ref, *refs):
    pieces, outs, (held, sems, ext, ext_sems) = refs[:PAIRS], refs[PAIRS:-4], refs[-4:]
    three_ref, normal_ref, slope_ref, scale_ref = outs
    start_conv(me_ref, pieces, held, sems, ext, local_ref, left_ref, right_ref, ext_sems)
    rows = mask_ref.shape[0]
    total = vec_ref[3:4, :]
    for tap in range(TAPS):
        start = pl.program_id(0) * rows + tap * DILATION
        total = total + dot(masked_tap(mask_ref, ext, start, rows, tap), tap_weight(held, tap))
    second = total.astype(BF16).astype(F32)
    hidden, normal, slope, scale = front(second, vec_ref[4:5, :], vec_ref[5:6, :])
    three_ref[...] = hidden.astype(BF16)
    normal_ref[...] = normal.astype(BF16)
    slope_ref[...] = slope.astype(BF16)
    scale_ref[...] = scale


def back_second_kernel(me_ref, cot_ref, vec_ref, normal_ref, slope_ref, scale_ref, *refs):
    pieces, outs, (held, sems) = refs[:PAIRS], refs[PAIRS:-2], refs[-2:]
    weight_ref, back_ref, sums_ref = outs

    @pl.when(pl.program_id(0) == 0)
    def _():
        for copy in load_pieces(me_ref, pieces, held, sems):
            copy.wait()
        for unit in range(UNITS):
            weight_ref[:, unit * H : (unit + 1) * H] = held[:, :, unit].reshape(H, H)
        sums_ref[...] = jnp.zeros_like(sums_ref)

    back_three = dot(cot_ref[...], weight_ref[...], NT)
    grad, gain_grad, shift_grad = front_back(
        back_three, vec_ref[4:5, :], normal_ref[...].astype(F32), slope_ref[...].astype(F32), scale_ref[...]
    )
    back = grad.astype(BF16)
    back_ref[...] = back
    sums_ref[0:1, :] += gain_grad
    sums_ref[1:2, :] += shift_grad
    sums_ref[2:3, :] += jnp.sum(back.astype(F32), axis=0, keepdims=True)


def output_kernel(tokens_ref, three_ref, weight_ref, vec_ref, output_ref):
    product = dot(three_ref[...], weight_ref[...])
    output_ref[...] = (tokens_ref[...].astype(F32) + product + vec_ref[2:3, :]).astype(BF16)


def place_rows(me_ref, held, tiles):
    for core in range(CORES):
        for place in range(PLANE):
            step = me_ref[1] ^ place
            number = step if core else 2 * (step & 1) + (step >> 1)
            held[me_ref[0] ^ core, number] = tiles[core][place]


def grad_out_kernel(me_ref, three_ref, cot_ref, keep_ref, send_ref, sum_ref, held):
    cot = cot_ref[...]
    grad = dot(three_ref[...], cot, TN).astype(BF16)
    quarter = H // PIECES
    tiles = [
        [grad[(core * PLANE + place) * quarter : (core * PLANE + place + 1) * quarter] for place in range(PLANE)]
        for core in range(CORES)
    ]
    place_rows(me_ref, held, tiles)
    keep_ref[...] = held[0]
    send_ref[...] = held[1]
    sum_ref[...] = jnp.broadcast_to(jnp.sum(cot.astype(F32), axis=0, keepdims=True), sum_ref.shape)


def back_first_kernel(
    me_ref, mask_ref, vec_ref, normal_ref, slope_ref, scale_ref, local_ref, left_ref, right_ref, *refs
):
    pieces, outs, (held, sems, ext, ext_sems) = refs[:PAIRS], refs[PAIRS:-4], refs[-4:]
    back_ref, sums_ref = outs
    start_conv(me_ref, pieces, held, sems, ext, local_ref, left_ref, right_ref, ext_sems)

    @pl.when(pl.program_id(0) == 0)
    def _():
        sums_ref[...] = jnp.zeros_like(sums_ref)

    rows = mask_ref.shape[0]
    total = None
    for tap in range(TAPS):
        start = pl.program_id(0) * rows + tap * DILATION
        term = dot(masked_tap(mask_ref, ext, start, rows, tap), tap_weight(held, TAPS - 1 - tap), NT)
        total = term if total is None else total + term
    back_two = total.astype(BF16).astype(F32)
    grad, gain_grad, shift_grad = front_back(
        back_two, vec_ref[1:2, :], normal_ref[...].astype(F32), slope_ref[...].astype(F32), scale_ref[...]
    )
    back = grad.astype(BF16)
    back_ref[...] = back
    sums_ref[0:1, :] += gain_grad
    sums_ref[1:2, :] += shift_grad
    sums_ref[2:3, :] += jnp.sum(back.astype(F32), axis=0, keepdims=True)


def grad_in_kernel(nz, me_ref, one_ref, back_ref, keep_ref, send_ref, grad_ref, held):
    for start in range(0, H, 256):
        width = min(256, H - start)
        grad_ref[:, start : start + width] = dot(one_ref[...], back_ref[:, start : start + width], TN)
    part = D // PIECES // nz
    tiles = []
    for core in range(CORES):
        tiles.append([])
        for place in range(PLANE):
            rows = []
            for line in range(nz):
                first = ((line * PLANE + place) * CORES + core) * part
                rows.append(grad_ref[first : first + part, :])
            tiles[core].append(jnp.concatenate(rows, axis=0).astype(BF16))
    place_rows(me_ref, held, tiles)
    keep_ref[...] = held[0]
    send_ref[...] = held[1]


def grad_conv_kernel(me_ref, mask_ref, back_ref, local_ref, left_ref, right_ref, keep_ref, send_ref, held, ext, ext_sems):
    tap = pl.program_id(0)

    @pl.when(tap == 0)
    def _():
        for copy in fill_ext(ext, local_ref, left_ref, right_ref, ext_sems):
            copy.wait()

    rows = back_ref.shape[0]
    values = ext[pl.ds(pl.multiple_of(tap * DILATION, DILATION), rows), :]
    column = lax.broadcasted_iota(jnp.int32, mask_ref.shape, 1)
    mask = jnp.sum(jnp.where(column == tap, mask_ref[...], 0.0), axis=1, keepdims=True)
    values = values * mask.astype(BF16)
    grad = dot(values, back_ref[...], TN).astype(BF16)
    quarter = H // PIECES
    tiles = [
        [grad[(core * PLANE + place) * quarter : (core * PLANE + place + 1) * quarter] for place in range(PLANE)]
        for core in range(CORES)
    ]
    place_rows(me_ref, held, tiles)
    keep_ref[:, 0] = held[0]
    send_ref[:, 0] = held[1]


def vec_kernel(order_ref, one_ref, cot_ref, two_ref, three_ref, out_ref):
    for number, row in enumerate([one_ref[0:1, :], one_ref[1:2, :], cot_ref[0:1, :]]):
        out_ref[2 * number : 2 * number + 1, :] = row[:, :H]
        out_ref[2 * number + 1 : 2 * number + 2, :] = row[:, H:]
    hidden = jnp.concatenate([two_ref[...], three_ref[...]], axis=0)
    natural = exact_dot(hidden, order_ref[...], NT)
    for number, row in enumerate([2, 0, 1, 10, 8, 9]):
        out_ref[6 + number : 7 + number, :] = natural[row : row + 1, :]


def input_grad_kernel(back_ref, weight_ref, vec_ref, normal_ref, slope_ref, scale_ref, cot_ref, grad_ref, sums_ref):
    @pl.when(pl.program_id(0) == 0)
    def _():
        sums_ref[...] = jnp.zeros_like(sums_ref)

    back_one = dot(back_ref[...], weight_ref[...], NT)
    grad, gain_grad, shift_grad = front_back(
        back_one, vec_ref[0:1, :], normal_ref[...].astype(F32), slope_ref[...].astype(F32), scale_ref[...]
    )
    grad_ref[...] = (cot_ref[...].astype(F32) + grad).astype(BF16)
    sums_ref[0:1, :] += gain_grad
    sums_ref[1:2, :] += shift_grad


def exact_dot(values, order, dims):
    result = 0.0
    for _ in range(3):
        low = values.astype(BF16)
        result = result + dot(low, order, dims)
        values = values - low.astype(F32)
    return result


def pack_kernel(w_in_ref, w_conv_ref, w_out_ref, order_ref, packed_ref):
    ordered = jnp.concatenate([w_in_ref[...]] + [w_conv_ref[tap] for tap in range(TAPS)], axis=0)
    ordered = dot(ordered.astype(BF16), order_ref[...])
    products = [w_out_ref[:, unit * H : (unit + 1) * H] for unit in range(UNITS)]
    packed_ref[...] = jnp.concatenate([ordered] + products, axis=0).astype(BF16)


def momenta_kernel(me_ref, mom_in_ref, mom_conv_ref, mom_out_ref, order_ref, *refs):
    out_refs, held = refs[:-1], refs[-1]
    ordered = jnp.concatenate([mom_in_ref[...]] + [mom_conv_ref[tap] for tap in range(TAPS)], axis=0)
    ordered = exact_dot(ordered, order_ref[...], NN)
    rows, part = mom_in_ref.shape[0], mom_conv_ref.shape[1]
    taps = [ordered[rows + tap * part : rows + (tap + 1) * part] for tap in range(TAPS)]
    products = [mom_out_ref[:, unit * H : (unit + 1) * H] for unit in range(UNITS)]
    units = [taps[0:2], [taps[2]] * 2, products, taps[3:5]]
    for slot in range(SLOTS):
        held[slot ^ me_ref[3]] = jnp.concatenate(units[slot] + [ordered[:rows]], axis=0)
    for step, out_ref in enumerate(out_refs):
        out_ref[...] = held[step]


def line_kernel(nz, widths, me_ref, *refs):
    shards, out_refs, held = refs[:nz], refs[nz:-1], refs[-1]
    for number in range(nz):
        held[number] = shards[number][...]
    blocks = [held[me_ref[2] ^ line].astype(F32) for line in range(nz)]
    start = 0
    for out_ref, (groups, rows) in zip(out_refs, widths):
        for group in range(groups):
            stop = start + rows
            joined = jnp.concatenate([block[start:stop] for block in blocks], axis=0).astype(out_ref.dtype)
            if groups == 1:
                out_ref[...] = joined
            else:
                out_ref[group] = joined
            start = stop


def units_kernel(me_ref, *refs):
    conv_refs, product_refs, (keep_ref, send_ref, held) = refs[:4], refs[4:8], refs[8:]

    def total(parts):
        return functools.reduce(jnp.add, [part.astype(F32) for part in parts]).astype(BF16)

    def tap(number):
        return total([ref[0, number] for ref in conv_refs[:3]] + [conv_refs[3][number]])

    product = total([ref[0] for ref in product_refs[:3]] + [product_refs[3][...]])
    units = [[tap(0), tap(1)], [tap(2)] * 2, [product[:, :H], product[:, H:]], [tap(3), tap(4)]]
    for slot in range(SLOTS):
        for unit in range(UNITS):
            held[slot ^ me_ref[3], unit] = units[slot][unit]
    for number in range(SLOTS // 2):
        keep_ref[number] = held[2 * number]
        send_ref[number] = held[2 * number + 1]


def spread(nz, me_ref, order_ref, values, out_refs, held):
    natural = jnp.where(me_ref[3] == SLOT_OUT, values[...].astype(F32), dot(values[...], order_ref[...], NT))
    sizes = [H // PIECES] * UNITS + [D // PIECES]
    for line in range(nz):
        start, parts = 0, []
        for size in sizes:
            part = size // nz
            parts.append(natural[start + line * part : start + (line + 1) * part])
            start += size
        held[line] = jnp.concatenate(parts, axis=0).astype(BF16)
    for step, out_ref in enumerate(out_refs):
        out_ref[...] = held[me_ref[2] ^ step]


def spread_sums_kernel(nz, me_ref, order_ref, units_ref, in_ref, *refs):
    out_refs, (held, values) = refs[:-2], refs[-2:]
    rows = units_ref.shape[1]
    for unit in range(UNITS):
        values[unit * rows : (unit + 1) * rows, :] = units_ref[unit].astype(BF16)
    values[UNITS * rows :, :] = in_ref[...].astype(BF16)
    spread(nz, me_ref, order_ref, values, out_refs, held)


def spread_results_kernel(nz, me_ref, order_ref, mine_ref, other_ref, *refs):
    out_refs, (held, values) = refs[:-2], refs[-2:]
    rows = H // PIECES
    for unit in range(UNITS):
        place = slice(unit * rows, (unit + 1) * rows)
        mine = (me_ref[3] == SLOT_OUT) | (me_ref[0] == unit)
        values[place, :] = jnp.where(mine, mine_ref[place, :], other_ref[0:rows, :])
    values[UNITS * rows :, :] = jnp.where(me_ref[0] == 0, mine_ref[UNITS * rows :, :], other_ref[rows:, :])
    spread(nz, me_ref, order_ref, values, out_refs, held)


def rows_of(me_ref, shards, held, part):
    for number in range(SLOTS):
        held[number] = shards[number][...]
    slots = [held[slot ^ me_ref[3]].astype(F32) for slot in range(SLOTS)]
    taps = [slots[slot][unit * part : (unit + 1) * part] for slot, unit in TAP_UNITS]
    products = [slots[SLOT_OUT][unit * part : (unit + 1) * part] for unit in range(UNITS)]
    return slots[SLOT_IN][UNITS * part :], taps, products


def finish_sums_kernel(me_ref, *refs):
    shards, (mom_in, mom_conv, mom_out), rest = refs[:SLOTS], refs[SLOTS : SLOTS + 3], refs[SLOTS + 3 :]
    sum_in, sum_conv, sum_out, new_in, new_conv, new_out, held = rest
    rows, taps, products = rows_of(me_ref, shards, held, mom_out.shape[0])
    sum_in[...] = rows
    new_in[...] = MOMENTUM * mom_in[...] + rows
    for tap in range(TAPS):
        sum_conv[tap] = taps[tap]
        new_conv[tap] = MOMENTUM * mom_conv[tap] + taps[tap]
    for unit in range(UNITS):
        columns = slice(unit * H, (unit + 1) * H)
        sum_out[:, columns] = products[unit]
        new_out[:, columns] = MOMENTUM * mom_out[:, columns] + products[unit]


def finish_results_kernel(me_ref, *refs):
    shards, (w_in, w_conv, w_out), rest = refs[:SLOTS], refs[SLOTS : SLOTS + 3], refs[SLOTS + 3 :]
    new_in, new_conv, new_out, held = rest
    rows, taps, products = rows_of(me_ref, shards, held, w_out.shape[0])
    new_in[...] = w_in[...] - MUON_RATE * rows
    for tap in range(TAPS):
        new_conv[tap] = w_conv[tap] - MUON_RATE * taps[tap]
    for unit in range(UNITS):
        columns = slice(unit * H, (unit + 1) * H)
        new_out[:, columns] = w_out[:, columns] - MUON_RATE * products[unit]


def newton_schulz(x_ref, low_ref, gram_ref, poly_ref, own):
    size, width = x_ref.shape
    square = jnp.sum(x_ref[...] * x_ref[...])
    factor = 1.0 / (jnp.sqrt(square) + 1e-07)
    x_ref[...] = x_ref[...] * factor
    low_ref[...] = x_ref[...].astype(BF16)
    square = square * factor * factor
    for step in range(NS_STEPS):
        shift = square * (1.0 / size)
        for start in range(0, size, 256):
            span = min(256, size - start)
            gram = dot(low_ref[...], low_ref[start : start + span, :], NT)
            row = lax.broadcasted_iota(jnp.int32, (size, span), 0)
            column = lax.broadcasted_iota(jnp.int32, (size, span), 1) + start
            gram_ref[:, start : start + span] = gram - jnp.where(row == column, shift, 0.0)
        gram_low = gram_ref[...].astype(BF16)
        linear = COEF_B + 2.0 * COEF_C * shift
        for start in range(0, size, 256):
            span = min(256, size - start)
            squared = dot(gram_low, gram_low[:, start : start + span])
            poly_ref[:, start : start + span] = (
                linear * gram_ref[:, start : start + span] + COEF_C * squared
            ).astype(BF16)
        coefficient = COEF_A + COEF_B * shift + COEF_C * shift * shift
        if step == NS_STEPS - 1:
            own(coefficient)
            return
        square = jnp.zeros((), F32)
        for start in range(0, width, 256):
            span = min(256, width - start)
            fresh = coefficient * x_ref[:, start : start + span] + dot(
                poly_ref[...], low_ref[:, start : start + span]
            )
            square = square + jnp.sum(fresh * fresh)
            x_ref[:, start : start + span] = fresh
        low_ref[...] = x_ref[...].astype(BF16)


def orth_kernel(me_ref, *refs):
    in_pieces, unit_pieces = refs[:PAIRS], refs[PAIRS : 2 * PAIRS]
    mine_ref, other_ref = refs[2 * PAIRS : 2 * PAIRS + 2]
    held, x_ref, low_ref, wide_ref, wide_low_ref, gram_ref, poly_ref = refs[2 * PAIRS + 2 :]
    slot, core = me_ref[3], me_ref[0]
    is_in = (slot == SLOT_IN) & (core == 0)
    is_out = slot == SLOT_OUT
    places = [(pair, one) for pair in range(PAIRS) for one in range(2)]

    @pl.when(jnp.logical_not(is_in | is_out))
    def _():
        rows = H // PIECES
        for number, (pair, one) in enumerate(places):
            x_ref[number * rows : (number + 1) * rows, :] = unit_pieces[pair][one, core].astype(F32)

        def own(coefficient):
            for start in (0, PLANE * rows):
                part = slice(start, start + rows)
                fresh = (coefficient * x_ref[part, :] + dot(poly_ref[part, :], low_ref[...])).astype(BF16)
                if start == 0:
                    mine_ref[pl.ds(pl.multiple_of(core * rows, 16), rows), :] = fresh
                else:
                    other_ref[0:rows, :] = fresh

        newton_schulz(x_ref, low_ref, gram_ref, poly_ref, own)

    @pl.when(is_out)
    def _():
        rows = H // PIECES
        for number, (pair, one) in enumerate(places):
            for unit in range(UNITS):
                wide_ref[number * rows : (number + 1) * rows, unit * H : (unit + 1) * H] = unit_pieces[pair][
                    one, unit
                ].astype(F32)

    @pl.when(is_in)
    def _():
        rows = D // PIECES
        for number, (pair, one) in enumerate(places):
            held[number * rows : (number + 1) * rows, :] = in_pieces[pair][one].astype(F32)
        for start in range(0, D, 256):
            wide_ref[:, start : start + 256] = held[start : start + 256, :].T

    @pl.when(is_in | is_out)
    def _():
        def own(coefficient):
            @pl.when(is_out)
            def _():
                rows = H // PIECES
                fresh = coefficient * wide_ref[0:rows, :] + dot(poly_ref[0:rows, :], wide_low_ref[...])
                for unit in range(UNITS):
                    mine_ref[unit * rows : (unit + 1) * rows, :] = fresh[:, unit * H : (unit + 1) * H].astype(BF16)

            @pl.when(is_in)
            def _():
                rows = D // PIECES
                for out_ref, start in ((mine_ref, 0), (other_ref, PLANE * rows)):
                    columns = slice(start, start + 256)
                    fresh = coefficient * wide_ref[:, columns] + dot(poly_ref[...], wide_low_ref[:, columns])
                    out_ref[out_ref.shape[0] - rows :, :] = fresh.T[0:rows].astype(BF16)

        newton_schulz(wide_ref, wide_low_ref, gram_ref, poly_ref, own)


class Layout:
    def __init__(self, count):
        self.count = count
        self.lines = count // PIECES
        self.part = H // count
        places = np.arange(H)
        row = places % self.part
        line = places // self.part % self.lines
        plane = places // (self.part * self.lines) % PLANE
        core = places // (self.part * self.lines * PLANE)
        self.natural = ((line * PLANE + plane) * CORES + core) * self.part + row

    def swap(self, values, mask, keep=lambda source, target: True):
        pairs = [(one, one ^ mask) for one in range(self.count)]
        pairs = [pair for pair in pairs if keep(pair[0] // PIECES % SLOTS, pair[1] // PIECES % SLOTS)]
        return lax.ppermute(values, "seq", pairs)

    def swap_line(self, values, step, keep=lambda source, target: True):
        return self.swap(values, step * PIECES, keep)

    def swap_plane(self, values, step, keep=lambda source, target: True):
        pairs = [(one, one ^ (2 if one % CORES == step else 4)) for one in range(self.count)]
        pairs = [pair for pair in pairs if keep(pair[0] // PIECES % SLOTS, pair[1] // PIECES % SLOTS)]
        return lax.ppermute(values, "seq", pairs)

    def along_line(self, values):
        return [values] + [self.swap_line(values, step) for step in range(1, self.lines)]

    def to_all(self, values, keep=lambda source, target: True):
        pair = jnp.stack([values, self.swap_plane(values, 0, keep)])
        far = self.swap_plane(pair, 1, keep)
        return [pair, far, self.swap(pair, 1, keep), self.swap(far, 1, keep)]


def add(*terms):
    return functools.reduce(jnp.add, [term.astype(F32) for term in terms])


def front_outs(rows, width):
    return [shape((rows, width), BF16)] * 3 + [shape((rows, 1), F32)]


def late_spec(rows, width):
    return pl.BlockSpec((rows, width), lambda i: (jnp.maximum(i - 2, 0), 0))


def late_out_specs(rows, width):
    return [late_spec(rows, width)] * 3 + [late_spec(rows, 1)]


def front_out_specs(rows, width):
    return [rows_spec(rows, width)] * 3 + [rows_spec(rows, 1)]


def body(
    count,
    tokens,
    cotangent,
    protein_lengths,
    w_in,
    w_conv,
    w_out,
    vectors,
    mom_in,
    mom_conv,
    mom_out,
    vec_mean,
    vec_square,
):
    lay = Layout(count)
    index = lax.axis_index("seq")
    line_index = index // PIECES
    rows = tokens.shape[0]
    me = jnp.stack(
        [index & 1, (index >> 1) & (PLANE - 1), line_index, line_index % SLOTS, index * rows]
    ).astype(jnp.int32)
    block = 256
    grid = (rows // block,)
    quarter = H // PIECES
    piece_in = D // PIECES
    to_order = jnp.asarray(np.arange(H)[:, None] == lay.natural[None, :], BF16)

    def order_low(values):
        return jnp.dot(values, to_order, preferred_element_type=F32).astype(BF16)

    row_ends = jnp.cumsum(protein_lengths, axis=1) + jnp.arange(protein_lengths.shape[0], dtype=jnp.int32)[:, None] * LEN
    mask_rows = call(
        mask_kernel, 2.0, out_shape=shape((rows, 8), F32), in_specs=[SMEM, VMEM], out_specs=VMEM
    )(me, row_ends.reshape(1, -1))

    edges = [one for one in range(count - 1) if (one + 1) * rows % LEN != 0]

    def halos(to_right, to_left):
        left = lax.ppermute(to_right, "seq", [(one, one + 1) for one in edges])
        right = lax.ppermute(to_left, "seq", [(one + 1, one) for one in edges])
        return left, right

    part = lay.part
    line = line_index

    def join(shards, widths, outs):
        return call(
            functools.partial(line_kernel, lay.lines, widths),
            2.0,
            out_shape=outs,
            in_specs=[SMEM] + [VMEM] * lay.lines,
            out_specs=[VMEM] * len(outs),
            scratch_shapes=[pltpu.VMEM((lay.lines,) + shards[0].shape, shards[0].dtype)],
        )(me, *shards)

    in_rows = D // count
    shard_rows = UNITS * part + in_rows
    width = vectors.shape[0]
    packed = call(
        pack_kernel,
        2.0,
        out_shape=shape((in_rows + (TAPS + UNITS) * part, H), BF16),
        in_specs=[VMEM] * 4,
        out_specs=VMEM,
    )(w_in, w_conv, w_out, to_order)
    packed, to_right, to_left = tie(packed, tokens[rows - HALO :], tokens[:HALO])
    packed_line = lay.along_line(packed)
    token_left, token_right = halos(to_right, to_left)
    mom_blocks = list(call(
        momenta_kernel,
        2.0,
        out_shape=[shape((shard_rows, H), F32)] * SLOTS,
        in_specs=[SMEM] + [VMEM] * 4,
        out_specs=[VMEM] * SLOTS,
        scratch_shapes=[pltpu.VMEM((SLOTS, shard_rows, H), F32)],
    )(me, mom_in, mom_conv, mom_out, to_order))
    packed_line[0], mask_rows, mom_blocks[0], token_left, token_right = tie(
        packed_line[0], mask_rows, mom_blocks[0], token_left, token_right
    )
    in_own, conv_own, out_own = join(
        packed_line,
        [(1, in_rows), (TAPS, part), (UNITS, part)],
        [shape((piece_in, H), BF16), shape((TAPS, quarter, H), BF16), shape((UNITS, quarter, H), BF16)],
    )

    padded = -(-width // 128) * 128
    vec_own, token_left = tie(jnp.pad(vectors, (0, padded - width)).reshape(1, padded), token_left)
    vec_near = jnp.concatenate(lay.to_all(vec_own)).reshape(PIECES, padded)
    vec_near, in_own = tie(vec_near, in_own)
    vec_line = lay.along_line(vec_near)
    in_near, *vec_line = tie(lay.swap_plane(in_own, 0), *vec_line)
    vec_rows = jnp.concatenate(vec_line)
    number = jnp.arange(count, dtype=jnp.int32)
    from_core = me[0] ^ (number // PLANE % CORES)
    step = number % PLANE
    from_plane = me[1] ^ jnp.where(step == 1, 1 + from_core, jnp.where(step == 2, 2 - from_core, step))
    from_index = (me[2] ^ (number // PIECES)) * PIECES + from_plane * CORES + from_core
    pick = (number[:, None] == from_index[None, :]).astype(BF16)
    vec_all = jnp.dot(pick, vec_rows.astype(BF16), preferred_element_type=F32)[:, :width].reshape(-1)
    vec_d = vec_all[: 3 * D].reshape(3, D)
    vec_h = order_low(vec_all[3 * D :].reshape(6, H).astype(BF16)).astype(F32)

    one_low, normal_one, slope_one, scale_one, one_halo = call(
        front_one_kernel,
        10.0,
        grid=(2 + rows // block,),
        out_shape=front_outs(rows, D) + [shape((2 * HALO, D), BF16)],
        in_specs=[late_spec(block, D), whole_spec(HALO, D), whole_spec(HALO, D), whole_spec(3, D)],
        out_specs=late_out_specs(block, D) + [pl.BlockSpec((HALO, D), lambda i: (jnp.minimum(i, 1), 0))],
    )(tokens, token_left, token_right, vec_d)
    in_pair = jnp.stack([in_own, in_near])
    in_far = lay.swap_plane(in_pair, 1)
    late_in_pair, conv_own = tie(in_pair, conv_own)
    conv_near = lay.swap_plane(conv_own, 0)
    mom_lines = [mom_blocks[0]] + [lay.swap_line(mom_blocks[step % SLOTS], step) for step in range(1, lay.lines)]
    in_far, one_low, one_halo, *mom_lines[1:] = tie(in_far, one_low, one_halo, *mom_lines[1:])
    in_pieces = [late_in_pair, in_far, lay.swap(late_in_pair, 1), lay.swap(in_far, 1)]
    in_pieces[3], conv_near = tie(in_pieces[3], conv_near)
    conv_pair = jnp.stack([conv_own, conv_near])
    conv_far = lay.swap_plane(conv_pair, 1)
    late_conv_pair, out_own = tie(conv_pair, out_own)
    out_near = lay.swap_plane(out_own, 0)
    in_low, two_low, normal_two, slope_two, scale_two, two_left, two_right = call(
        functools.partial(first_kernel, lay.lines),
        11.0,
        grid=(2 + rows // block,),
        out_shape=[shape((D, H), BF16)] + front_outs(rows, H) + [shape((HALO, H), BF16)] * 2,
        in_specs=[
            SMEM,
            late_spec(block, D),
            pl.BlockSpec((HALO, D), lambda i: (jnp.minimum(i, 1), 0)),
            whole_spec(6, H),
        ]
        + [ANY] * PAIRS,
        out_specs=[whole_spec(D, H)] + late_out_specs(block, H) + [whole_spec(HALO, H)] * 2,
        scratch_shapes=[pltpu.VMEM((CORES, PLANE, piece_in, H), BF16), pltpu.SemaphoreType.DMA((PIECES,))],
    )(me, one_low, one_halo, vec_h, *in_pieces)
    conv_far, out_near, two_low = tie(conv_far, out_near, two_low)
    conv_pieces = [late_conv_pair, conv_far, lay.swap(late_conv_pair, 1), lay.swap(conv_far, 1)]
    out_pair = jnp.stack([out_own, out_near])
    out_far = lay.swap_plane(out_pair, 1)
    conv_pieces[3], late_out_pair = tie(conv_pieces[3], out_pair)
    conv_scratch = [
        pltpu.VMEM((CORES, PLANE, TAPS, quarter, H), BF16),
        pltpu.SemaphoreType.DMA((PIECES,)),
        pltpu.VMEM((rows + 2 * HALO, H), BF16),
        pltpu.SemaphoreType.DMA((3,)),
    ]
    three_low, normal_three, slope_three, scale_three = call(
        second_kernel,
        11.0,
        grid=grid,
        out_shape=front_outs(rows, H),
        in_specs=[SMEM, rows_spec(block, 8), whole_spec(6, H)] + [ANY] * (3 + PAIRS),
        out_specs=front_out_specs(block, H),
        scratch_shapes=conv_scratch,
    )(me, mask_rows, vec_h, two_low, two_left, two_right, *conv_pieces)

    three_low, out_far = tie(three_low, out_far)
    out_pieces = [late_out_pair, out_far, lay.swap(late_out_pair, 1), lay.swap(out_far, 1)]

    keep_out, send_out, sum_cot = call(
        grad_out_kernel,
        5.0,
        grid=(D // 256,),
        out_shape=[shape((PLANE, quarter, D), BF16)] * 2 + [shape((8, D), F32)],
        in_specs=[SMEM, whole_spec(rows, H), pl.BlockSpec((rows, 256), lambda i: (0, i))],
        out_specs=[pl.BlockSpec((PLANE, quarter, 256), lambda i: (0, 0, i))] * 2 + [pl.BlockSpec((8, 256), lambda i: (0, i))],
        scratch_shapes=[pltpu.VMEM((CORES, PLANE, quarter, 256), BF16)],
    )(me, three_low, cotangent)
    late_cotangent, send_out = tie(cotangent, send_out)
    out_low, back_second, sums_three = call(
        back_second_kernel,
        9.0,
        grid=grid,
        out_shape=[shape((H, D), BF16), shape((rows, H), BF16), shape((8, H), F32)],
        in_specs=[SMEM, rows_spec(block, D), whole_spec(6, H), rows_spec(block, H), rows_spec(block, H), rows_spec(block, 1)]
        + [ANY] * PAIRS,
        out_specs=[whole_spec(H, D), rows_spec(block, H), whole_spec(8, H)],
        scratch_shapes=[pltpu.VMEM((CORES, PLANE, UNITS, quarter, H), BF16), pltpu.SemaphoreType.DMA((PIECES,))],
    )(me, late_cotangent, vec_h, normal_three, slope_three, scale_three, *out_pieces)
    back_left, back_right = halos(back_second[rows - HALO :], back_second[:HALO])
    output = call(
        output_kernel,
        5.0,
        grid=grid,
        out_shape=shape((rows, D), BF16),
        in_specs=[rows_spec(block, D), rows_spec(block, H), whole_spec(H, D), whole_spec(3, D)],
        out_specs=rows_spec(block, D),
    )(tokens, three_low, out_low, vec_d)
    output, back_left, back_right, late_second = tie(output, back_left, back_right, back_second)
    keep_conv, send_conv = call(
        grad_conv_kernel,
        8.0,
        grid=(TAPS,),
        out_shape=[shape((PLANE, TAPS, quarter, H), BF16)] * 2,
        in_specs=[SMEM, whole_spec(rows, 8), whole_spec(rows, H)] + [ANY] * 3,
        out_specs=[pl.BlockSpec((PLANE, 1, quarter, H), lambda i: (0, i, 0, 0))] * 2,
        scratch_shapes=[
            pltpu.VMEM((CORES, PLANE, quarter, H), BF16),
            pltpu.VMEM((rows + 2 * HALO, H), BF16),
            pltpu.SemaphoreType.DMA((3,)),
        ],
    )(me, mask_rows, late_second, two_low, two_left, two_right)
    other_out, keep_conv = tie(lay.swap(send_out, 1), keep_conv)
    near_out = lay.swap_plane(add(keep_out[2:], other_out[2:]).astype(BF16), 0)
    other_conv = lay.swap(send_conv, 1)
    half_conv, late_second = tie(add(keep_conv[2:], other_conv[2:]).astype(BF16), late_second)
    near_conv = lay.swap_plane(half_conv, 0)
    back_first, sums_two = call(
        back_first_kernel,
        10.0,
        grid=grid,
        out_shape=[shape((rows, H), BF16), shape((8, H), F32)],
        in_specs=[SMEM, rows_spec(block, 8), whole_spec(6, H), rows_spec(block, H), rows_spec(block, H), rows_spec(block, 1)]
        + [ANY] * (3 + PAIRS),
        out_specs=[rows_spec(block, H), whole_spec(8, H)],
        scratch_shapes=conv_scratch,
    )(
        me,
        mask_rows,
        vec_h,
        normal_two,
        slope_two,
        scale_two,
        late_second,
        back_left,
        back_right,
        *conv_pieces,
    )
    near_conv, near_out, back_first = tie(near_conv, near_out, back_first)
    piece_conv, piece_out, back_first = tie(
        add(keep_conv[1], other_conv[1], near_conv[1]).astype(BF16),
        add(keep_out[1], other_out[1], near_out[1]).astype(BF16),
        back_first,
    )
    far_conv = lay.swap_plane(piece_conv, 1)
    far_out = lay.swap_plane(piece_out, 1)
    keep_in, send_in = call(
        functools.partial(grad_in_kernel, lay.lines),
        6.0,
        out_shape=[shape((PLANE, piece_in, H), BF16)] * 2,
        in_specs=[SMEM, VMEM, VMEM],
        out_specs=[VMEM] * 2,
        scratch_shapes=[pltpu.VMEM((D, H), F32), pltpu.VMEM((CORES, PLANE, piece_in, H), BF16)],
    )(me, one_low, back_first)
    other_in = lay.swap(send_in, 1)
    half_in, late_first = tie(add(keep_in[2:], other_in[2:]).astype(BF16), back_first)
    near_in = lay.swap_plane(half_in, 0)
    input_grad, sums_one = call(
        input_grad_kernel,
        8.0,
        grid=grid,
        out_shape=[shape((rows, D), BF16), shape((8, D), F32)],
        in_specs=[
            rows_spec(block, H),
            whole_spec(D, H),
            whole_spec(3, D),
            rows_spec(block, D),
            rows_spec(block, D),
            rows_spec(block, 1),
            rows_spec(block, D),
        ],
        out_specs=[rows_spec(block, D), whole_spec(8, D)],
    )(late_first, in_low, vec_d, normal_one, slope_one, scale_one, cotangent)
    near_in, input_grad = tie(near_in, input_grad)
    piece_in_sum, far_conv = tie(add(keep_in[1], other_in[1], near_in[1]).astype(BF16), far_conv)
    far_in = lay.swap_plane(piece_in_sum, 1)

    lines = lay.lines
    conv_block, out_block = whole_spec(1, TAPS, quarter, H), whole_spec(1, quarter, D)
    unit_keep, unit_send = call(
        units_kernel,
        3.0,
        grid=(1,),
        out_shape=[shape((SLOTS // 2, UNITS, quarter, H), BF16)] * 2,
        in_specs=[SMEM] + [conv_block] * 3 + [whole_spec(TAPS, quarter, H)] + [out_block] * 3 + [whole_spec(quarter, D)],
        out_specs=[whole_spec(SLOTS // 2, UNITS, quarter, H)] * 2,
        scratch_shapes=[pltpu.VMEM((SLOTS, UNITS, quarter, H), BF16)],
    )(me, keep_conv, other_conv, near_conv, far_conv, keep_out, other_out, near_out, far_out)
    unit_send, sums_one = tie(unit_send, sums_one)
    unit_near = lay.swap_line(unit_send, 1)
    vec_terms = call(
        vec_kernel,
        1.0,
        out_shape=shape((6 + 6, H), F32),
        in_specs=[VMEM] * 5,
        out_specs=VMEM,
    )(to_order, sums_one, sum_cot, sums_two, sums_three)
    mom_unit_pieces, mom_in_piece = join(
        mom_lines,
        [(UNITS, part), (1, in_rows)],
        [shape((UNITS, quarter, H), F32), shape((piece_in, H), F32)],
    )
    vec_sums = vec_terms + lay.swap(vec_terms, 1)
    unit_near, mom_in_piece, far_in, vec_sums = tie(unit_near, mom_in_piece, far_in, vec_sums)
    unit_half = add(unit_keep, unit_near)
    for step in range(SLOTS, lines):
        if step & (step - 1) == 0:
            unit_half = add(unit_half, lay.swap_line(unit_half.astype(BF16), step))
    unit_far = lay.swap_line(unit_half[1].astype(BF16), 2)
    vec_sums = vec_sums + lay.swap_plane(vec_sums, 0)
    unit_far, vec_sums = tie(unit_far, vec_sums)
    unit_sum = add(unit_half[0], unit_far)
    unit_moment = (MOMENTUM * mom_unit_pieces + unit_sum).astype(BF16)

    in_sum = add(keep_in[0], other_in[0], near_in[0], far_in)
    for step in range(SLOTS, lines):
        if step & (step - 1) == 0:
            in_sum = add(in_sum, lay.swap_line(in_sum.astype(BF16), step))
    to_near = lambda source, target: target in (SLOT_IN, SLOT_IN ^ 3)
    in_slot = lambda source, target: target == SLOT_IN
    in_sum = add(in_sum, lay.swap_line(in_sum.astype(BF16), 1, to_near))
    in_sum = add(in_sum, lay.swap_line(in_sum.astype(BF16), 3, in_slot))
    in_moment = (MOMENTUM * mom_in_piece + in_sum).astype(BF16)

    def orth_scratch(width):
        return [pltpu.VMEM((H, width), F32), pltpu.VMEM((H, width), BF16)]

    unit_pair = jnp.stack([unit_moment, lay.swap_plane(unit_moment, 0)])
    vec_sums = vec_sums + lay.swap_plane(vec_sums, 1)
    unit_pair, vec_sums = tie(unit_pair, vec_sums)
    unit_far = lay.swap_plane(unit_pair, 1)
    vec_step = 1
    while vec_step < lines:
        vec_sums = vec_sums + lay.swap_line(vec_sums, vec_step)
        vec_step *= 2
    in_pieces_m = lay.to_all(in_moment, in_slot)
    line_scratch = [
        pltpu.VMEM((lines, shard_rows, H), BF16),
        pltpu.VMEM((UNITS * quarter + piece_in, H), BF16),
    ]

    def spread_line(kernel, *values):
        blocks = call(
            functools.partial(kernel, lines),
            3.0,
            out_shape=[shape((shard_rows, H), BF16)] * SLOTS,
            in_specs=[SMEM] + [VMEM] * (1 + len(values)),
            out_specs=[VMEM] * SLOTS,
            scratch_shapes=line_scratch,
        )(me, to_order, *values)
        return blocks

    def to_line(blocks):
        return [blocks[0]] + [lay.swap_line(blocks[step], step) for step in range(1, SLOTS)]

    sum_blocks = spread_line(spread_sums_kernel, unit_sum, in_sum)
    unit_far, vec_sums, *sum_blocks = tie(unit_far, vec_sums, *sum_blocks)
    unit_pieces_m = [unit_pair, unit_far, lay.swap(unit_pair, 1), lay.swap(unit_far, 1)]
    sum_vec = lax.dynamic_slice_in_dim(vec_sums.reshape(-1), index * width, width)
    sum_shards = to_line(sum_blocks)
    mine, other = call(
        orth_kernel,
        21.0,
        out_shape=[shape((UNITS * quarter + piece_in, H), BF16), shape((quarter + piece_in, H), BF16)],
        in_specs=[SMEM] + [VMEM] * (2 * PAIRS),
        out_specs=[VMEM] * 2,
        scratch_shapes=[pltpu.VMEM((D, H), F32)]
        + orth_scratch(H)
        + orth_scratch(D)
        + [pltpu.VMEM((H, H), F32), pltpu.VMEM((H, H), BF16)],
    )(me, *in_pieces_m, *unit_pieces_m)
    orth_shards = to_line(spread_line(spread_results_kernel, mine, lay.swap(other, 1)))

    def finish(kernel, shards, *values, outs):
        return call(
            kernel,
            2.0,
            out_shape=[shape(one.shape, F32) for one in values] * outs,
            in_specs=[SMEM] + [VMEM] * (SLOTS + 3),
            out_specs=[VMEM] * (3 * outs),
            scratch_shapes=[pltpu.VMEM((SLOTS, shard_rows, H), BF16)],
        )(me, *shards, *values)

    sum_in, sum_conv, sum_out, moment_in, moment_conv, moment_out = finish(
        finish_sums_kernel, sum_shards, mom_in, mom_conv, mom_out, outs=2
    )
    new_in, new_conv, new_out = finish(finish_results_kernel, orth_shards, w_in, w_conv, w_out, outs=1)

    vec_mean_new = BETA_ONE * vec_mean + (1.0 - BETA_ONE) * sum_vec
    vec_square_new = BETA_TWO * vec_square + (1.0 - BETA_TWO) * sum_vec * sum_vec
    corrected_mean = vec_mean_new / (1.0 - BETA_ONE**STEP)
    corrected_square = vec_square_new / (1.0 - BETA_TWO**STEP)
    vec_new = vectors - ADAM_RATE * corrected_mean / (jnp.sqrt(corrected_square) + ADAM_EPS)
    return (
        output,
        input_grad,
        sum_in,
        sum_conv,
        sum_out,
        moment_in,
        moment_conv,
        moment_out,
        new_in,
        new_conv,
        new_out,
        sum_vec,
        vec_mean_new,
        vec_square_new,
        vec_new,
    )


def solution(mesh):
    matrix, taps, vector = P("seq", None), P(None, "seq", None), P("seq")
    return jax.shard_map(
        functools.partial(body, mesh.shape["seq"]),
        mesh=mesh,
        in_specs=(matrix, matrix, P(), matrix, taps, matrix, vector, matrix, taps, matrix, vector, vector),
        out_specs=(
            matrix,
            matrix,
            matrix,
            taps,
            matrix,
            matrix,
            taps,
            matrix,
            matrix,
            taps,
            matrix,
            vector,
            vector,
            vector,
            vector,
        ),
        check_vma=False,
    )
```

```python
import functools

import jax
import jax.numpy as jnp
import numpy as np
from jax import lax
from jax.experimental import pallas as pl
from jax.experimental.pallas import tpu as pltpu
from jax.sharding import PartitionSpec as P

D = 1280
H = 640
TAPS = 5
DILATION = 128
LEN = 1024
NS_STEPS = 5
STEP = 10
HALO = (TAPS // 2) * DILATION
CORES = 2
PLANE = 4
PIECES = CORES * PLANE
PAIRS = PIECES // 2
UNITS = 2
SLOTS = 4
SLOT_IN = 1
SLOT_OUT = 2
TAP_UNITS = ((0, 0), (0, 1), (1, 1), (3, 0), (3, 1))

EPS = 1e-05
COEF_A = 3.4445
COEF_B = -4.775
COEF_C = 2.0315
MOMENTUM = 0.95
MUON_RATE = 0.5
BETA_ONE = 0.9
BETA_TWO = 0.95
ADAM_RATE = 0.2
ADAM_EPS = 1e-08

F32 = jnp.float32
BF16 = jnp.bfloat16
NN = (((1,), (0,)), ((), ()))
NT = (((1,), (1,)), ((), ()))
TN = (((0,), (0,)), ((), ()))
INV_SQRT2 = 0.7071067811865476
INV_SQRT2PI = 0.3989422804014327
VMEM_LIMIT = 20 << 20
RELATIVE = 0.05

ANY = pl.BlockSpec(memory_space=pl.ANY)
VMEM = pl.BlockSpec(memory_space=pltpu.VMEM)
SMEM = pl.BlockSpec(memory_space=pltpu.SMEM)


def dot(left, right, dims=NN):
    return lax.dot_general(left, right, dims, preferred_element_type=F32)


def call(kernel, micros, **kwargs):
    return pl.pallas_call(
        kernel,
        name=getattr(kernel, "func", kernel).__name__,
        cost_estimate=pl.CostEstimate(flops=int(micros * RELATIVE * 1e9), bytes_accessed=int(micros * RELATIVE * 1e6), transcendentals=0),
        compiler_params=pltpu.CompilerParams(vmem_limit_bytes=VMEM_LIMIT),
        **kwargs,
    )


def tie(*values):
    return lax.optimization_barrier(values)


def shape(dims, dtype):
    return jax.ShapeDtypeStruct(dims, dtype)


def rows_spec(rows, width):
    return pl.BlockSpec((rows, width), lambda i: (i, 0))


def whole_spec(*dims):
    return pl.BlockSpec(dims, lambda i: (0,) * len(dims))


def front(values, gain, shift):
    average = jnp.mean(values, axis=-1, keepdims=True)
    centered = values - average
    scale = lax.rsqrt(jnp.mean(centered * centered, axis=-1, keepdims=True) + EPS)
    normal = centered * scale
    arg = normal * gain + shift
    below = 0.5 + 0.5 * lax.erf(arg * INV_SQRT2)
    slope = below + arg * (jnp.exp(-0.5 * arg * arg) * INV_SQRT2PI)
    return arg * below, normal, slope, scale


def front_back(incoming, gain, normal, slope, scale):
    d_arg = incoming * slope
    d_normal = d_arg * gain
    mean_one = jnp.mean(d_normal, axis=-1, keepdims=True)
    mean_two = jnp.mean(d_normal * normal, axis=-1, keepdims=True)
    grad = (d_normal - mean_one - normal * mean_two) * scale
    gain_grad = jnp.sum(d_arg * normal, axis=0, keepdims=True)
    shift_grad = jnp.sum(d_arg, axis=0, keepdims=True)
    return grad, gain_grad, shift_grad


def load_pieces(me_ref, pieces, held, sems):
    copies = []
    for other in range(CORES):
        core = me_ref[0] ^ other
        for number in range(PLANE):
            place = (0, 1 + core, 2 - core, 3)[number]
            copies.append(
                pltpu.make_async_copy(
                    pieces[2 * other + number // 2].at[number % 2, pl.ds(0, held.shape[2])],
                    held.at[core, me_ref[1] ^ place],
                    sems.at[other * PLANE + number],
                )
            )
    for copy in copies:
        copy.start()
    return copies


def front_one_kernel(tokens_ref, vec_ref, hidden_ref, normal_ref, slope_ref, scale_ref):
    hidden, normal, slope, scale = front(tokens_ref[...].astype(F32), vec_ref[0:1, :], vec_ref[1:2, :])
    hidden_ref[...] = hidden.astype(BF16)
    normal_ref[...] = normal.astype(BF16)
    slope_ref[...] = slope.astype(BF16)
    scale_ref[...] = scale


def front_halo_kernel(left_ref, right_ref, vec_ref, hidden_ref):
    values = jnp.where(pl.program_id(0) == 0, left_ref[...], right_ref[...])
    hidden_ref[...] = front(values.astype(F32), vec_ref[0:1, :], vec_ref[1:2, :])[0].astype(BF16)


def first_kernel(nz, me_ref, hidden_ref, halo_ref, vec_ref, *refs):
    pieces, outs, (held, sems) = refs[:PAIRS], refs[PAIRS:-2], refs[-2:]
    weight_ref, two_ref, normal_ref, slope_ref, scale_ref, left_ref, right_ref = outs
    part = D // PIECES // nz
    step = pl.program_id(0)

    @pl.when(step == 0)
    def _():
        for copy in load_pieces(me_ref, pieces, held, sems):
            copy.wait()
        blocks = [
            [held[core, place].astype(F32) for core in range(CORES)] for place in range(PLANE)
        ]
        for line in range(nz):
            rows = []
            for place in range(PLANE):
                for core in range(CORES):
                    rows.append(blocks[place][core][line * part : (line + 1) * part])
            length = part * PIECES
            weight_ref[line * length : (line + 1) * length, :] = jnp.concatenate(rows, axis=0).astype(BF16)

    values = jnp.where(step < 2, halo_ref[...], hidden_ref[...])
    first = dot(values, weight_ref[...]) + vec_ref[0:1, :]
    hidden, normal, slope, scale = front(first, vec_ref[1:2, :], vec_ref[2:3, :])
    two_ref[...] = hidden.astype(BF16)
    normal_ref[...] = normal.astype(BF16)
    slope_ref[...] = slope.astype(BF16)
    scale_ref[...] = scale

    @pl.when(step == 0)
    def _():
        left_ref[...] = hidden.astype(BF16)

    @pl.when(step == 1)
    def _():
        right_ref[...] = hidden.astype(BF16)


def mask_kernel(me_ref, ends_ref, mask_ref):
    rows = mask_ref.shape[0]
    first = me_ref[4] - HALO
    place = lax.broadcasted_iota(jnp.int32, (rows + 2 * HALO, 1), 0) + first
    ids = jnp.sum((place >= ends_ref[...]).astype(F32), axis=1, keepdims=True)
    ids = jnp.where(place < 0, -1.0, ids)
    column = lax.broadcasted_iota(jnp.int32, mask_ref.shape, 1)
    mask = jnp.zeros(mask_ref.shape, F32)
    for tap in range(TAPS):
        same = ids[tap * DILATION : tap * DILATION + rows] == ids[HALO : HALO + rows]
        mask = mask + jnp.where((column == tap) & same, 1.0, 0.0)
    mask_ref[...] = mask


def masked_tap(mask_ref, ext, start, rows, tap):
    values = ext[pl.ds(pl.multiple_of(start, DILATION), rows), :]
    if tap == TAPS // 2:
        return values
    return values * mask_ref[:, tap : tap + 1].astype(BF16)


def fill_ext(ext, local_ref, left_ref, right_ref, sems):
    rows = local_ref.shape[0]
    copies = [
        pltpu.make_async_copy(left_ref, ext.at[pl.ds(0, HALO)], sems.at[0]),
        pltpu.make_async_copy(local_ref, ext.at[pl.ds(HALO, rows)], sems.at[1]),
        pltpu.make_async_copy(right_ref, ext.at[pl.ds(HALO + rows, HALO)], sems.at[2]),
    ]
    for copy in copies:
        copy.start()
    return copies


def start_conv(me_ref, pieces, held, sems, ext, local_ref, left_ref, right_ref, ext_sems):
    @pl.when(pl.program_id(0) == 0)
    def _():
        copies = load_pieces(me_ref, pieces, held, sems)
        copies += fill_ext(ext, local_ref, left_ref, right_ref, ext_sems)
        for copy in copies:
            copy.wait()


def tap_weight(held, tap):
    return held[:, :, tap].reshape(H, H)


def second_kernel(me_ref, mask_ref, vec_ref, local_ref, left_ref, right_ref, *refs):
    pieces, outs, (held, sems, ext, ext_sems) = refs[:PAIRS], refs[PAIRS:-4], refs[-4:]
    three_ref, normal_ref, slope_ref, scale_ref = outs
    start_conv(me_ref, pieces, held, sems, ext, local_ref, left_ref, right_ref, ext_sems)
    rows = mask_ref.shape[0]
    total = vec_ref[3:4, :]
    for tap in range(TAPS):
        start = pl.program_id(0) * rows + tap * DILATION
        total = total + dot(masked_tap(mask_ref, ext, start, rows, tap), tap_weight(held, tap))
    second = total.astype(BF16).astype(F32)
    hidden, normal, slope, scale = front(second, vec_ref[4:5, :], vec_ref[5:6, :])
    three_ref[...] = hidden.astype(BF16)
    normal_ref[...] = normal.astype(BF16)
    slope_ref[...] = slope.astype(BF16)
    scale_ref[...] = scale


def back_second_kernel(me_ref, cot_ref, vec_ref, normal_ref, slope_ref, scale_ref, *refs):
    pieces, outs, (held, sems) = refs[:PAIRS], refs[PAIRS:-2], refs[-2:]
    weight_ref, back_ref, sums_ref = outs

    @pl.when(pl.program_id(0) == 0)
    def _():
        for copy in load_pieces(me_ref, pieces, held, sems):
            copy.wait()
        for unit in range(UNITS):
            weight_ref[:, unit * H : (unit + 1) * H] = held[:, :, unit].reshape(H, H)
        sums_ref[...] = jnp.zeros_like(sums_ref)

    back_three = dot(cot_ref[...], weight_ref[...], NT)
    grad, gain_grad, shift_grad = front_back(
        back_three, vec_ref[4:5, :], normal_ref[...].astype(F32), slope_ref[...].astype(F32), scale_ref[...]
    )
    back = grad.astype(BF16)
    back_ref[...] = back
    sums_ref[0:1, :] += gain_grad
    sums_ref[1:2, :] += shift_grad
    sums_ref[2:3, :] += jnp.sum(back.astype(F32), axis=0, keepdims=True)


def output_kernel(tokens_ref, three_ref, weight_ref, vec_ref, output_ref):
    product = dot(three_ref[...], weight_ref[...])
    output_ref[...] = (tokens_ref[...].astype(F32) + product + vec_ref[2:3, :]).astype(BF16)


def place_rows(me_ref, held, tiles):
    for core in range(CORES):
        for place in range(PLANE):
            step = me_ref[1] ^ place
            number = step if core else 2 * (step & 1) + (step >> 1)
            held[me_ref[0] ^ core, number] = tiles[core][place]


def grad_out_kernel(me_ref, three_ref, cot_ref, keep_ref, send_ref, sum_ref, held):
    cot = cot_ref[...]
    grad = dot(three_ref[...], cot, TN).astype(BF16)
    quarter = H // PIECES
    tiles = [
        [grad[(core * PLANE + place) * quarter : (core * PLANE + place + 1) * quarter] for place in range(PLANE)]
        for core in range(CORES)
    ]
    place_rows(me_ref, held, tiles)
    keep_ref[...] = held[0]
    send_ref[...] = held[1]
    sum_ref[...] = jnp.broadcast_to(jnp.sum(cot.astype(F32), axis=0, keepdims=True), sum_ref.shape)


def back_first_kernel(
    me_ref, mask_ref, vec_ref, normal_ref, slope_ref, scale_ref, local_ref, left_ref, right_ref, *refs
):
    pieces, outs, (held, sems, ext, ext_sems) = refs[:PAIRS], refs[PAIRS:-4], refs[-4:]
    back_ref, sums_ref = outs
    start_conv(me_ref, pieces, held, sems, ext, local_ref, left_ref, right_ref, ext_sems)

    @pl.when(pl.program_id(0) == 0)
    def _():
        sums_ref[...] = jnp.zeros_like(sums_ref)

    rows = mask_ref.shape[0]
    total = None
    for tap in range(TAPS):
        start = pl.program_id(0) * rows + tap * DILATION
        term = dot(masked_tap(mask_ref, ext, start, rows, tap), tap_weight(held, TAPS - 1 - tap), NT)
        total = term if total is None else total + term
    back_two = total.astype(BF16).astype(F32)
    grad, gain_grad, shift_grad = front_back(
        back_two, vec_ref[1:2, :], normal_ref[...].astype(F32), slope_ref[...].astype(F32), scale_ref[...]
    )
    back = grad.astype(BF16)
    back_ref[...] = back
    sums_ref[0:1, :] += gain_grad
    sums_ref[1:2, :] += shift_grad
    sums_ref[2:3, :] += jnp.sum(back.astype(F32), axis=0, keepdims=True)


def grad_in_kernel(nz, me_ref, one_ref, back_ref, keep_ref, send_ref, grad_ref, held):
    for start in range(0, H, 256):
        width = min(256, H - start)
        grad_ref[:, start : start + width] = dot(one_ref[...], back_ref[:, start : start + width], TN)
    part = D // PIECES // nz
    tiles = []
    for core in range(CORES):
        tiles.append([])
        for place in range(PLANE):
            rows = []
            for line in range(nz):
                first = ((line * PLANE + place) * CORES + core) * part
                rows.append(grad_ref[first : first + part, :])
            tiles[core].append(jnp.concatenate(rows, axis=0).astype(BF16))
    place_rows(me_ref, held, tiles)
    keep_ref[...] = held[0]
    send_ref[...] = held[1]


def grad_conv_kernel(me_ref, mask_ref, back_ref, local_ref, left_ref, right_ref, keep_ref, send_ref, held, ext, ext_sems):
    tap = pl.program_id(0)

    @pl.when(tap == 0)
    def _():
        for copy in fill_ext(ext, local_ref, left_ref, right_ref, ext_sems):
            copy.wait()

    rows = back_ref.shape[0]
    values = ext[pl.ds(pl.multiple_of(tap * DILATION, DILATION), rows), :]
    column = lax.broadcasted_iota(jnp.int32, mask_ref.shape, 1)
    mask = jnp.sum(jnp.where(column == tap, mask_ref[...], 0.0), axis=1, keepdims=True)
    values = values * mask.astype(BF16)
    grad = dot(values, back_ref[...], TN).astype(BF16)
    quarter = H // PIECES
    tiles = [
        [grad[(core * PLANE + place) * quarter : (core * PLANE + place + 1) * quarter] for place in range(PLANE)]
        for core in range(CORES)
    ]
    place_rows(me_ref, held, tiles)
    keep_ref[:, 0] = held[0]
    send_ref[:, 0] = held[1]


def vec_kernel(order_ref, one_ref, cot_ref, two_ref, three_ref, out_ref):
    for number, row in enumerate([one_ref[0:1, :], one_ref[1:2, :], cot_ref[0:1, :]]):
        out_ref[2 * number : 2 * number + 1, :] = row[:, :H]
        out_ref[2 * number + 1 : 2 * number + 2, :] = row[:, H:]
    hidden = jnp.concatenate([two_ref[...], three_ref[...]], axis=0)
    natural = exact_dot(hidden, order_ref[...], NT)
    for number, row in enumerate([2, 0, 1, 10, 8, 9]):
        out_ref[6 + number : 7 + number, :] = natural[row : row + 1, :]


def input_grad_kernel(back_ref, weight_ref, vec_ref, normal_ref, slope_ref, scale_ref, cot_ref, grad_ref, sums_ref):
    @pl.when(pl.program_id(0) == 0)
    def _():
        sums_ref[...] = jnp.zeros_like(sums_ref)

    back_one = dot(back_ref[...], weight_ref[...], NT)
    grad, gain_grad, shift_grad = front_back(
        back_one, vec_ref[0:1, :], normal_ref[...].astype(F32), slope_ref[...].astype(F32), scale_ref[...]
    )
    grad_ref[...] = (cot_ref[...].astype(F32) + grad).astype(BF16)
    sums_ref[0:1, :] += gain_grad
    sums_ref[1:2, :] += shift_grad


def exact_dot(values, order, dims):
    result = 0.0
    for _ in range(3):
        low = values.astype(BF16)
        result = result + dot(low, order, dims)
        values = values - low.astype(F32)
    return result


def pack_in_kernel(w_in_ref, vec_ref, order_ref, packed_ref):
    rows = [dot(w_in_ref[...].astype(BF16), order_ref[...]), vec_ref[...]]
    left = packed_ref.shape[0] - sum(one.shape[0] for one in rows)
    packed_ref[...] = jnp.concatenate(rows + [jnp.zeros((left, H), F32)], axis=0).astype(BF16)


def pack_rest_kernel(w_conv_ref, w_out_ref, order_ref, packed_ref):
    taps = jnp.concatenate([w_conv_ref[tap] for tap in range(TAPS)], axis=0)
    products = [w_out_ref[:, unit * H : (unit + 1) * H] for unit in range(UNITS)]
    packed_ref[...] = jnp.concatenate([dot(taps.astype(BF16), order_ref[...])] + products, axis=0).astype(BF16)


def momenta_kernel(me_ref, mom_in_ref, mom_conv_ref, mom_out_ref, order_ref, *refs):
    out_refs, held = refs[:-1], refs[-1]
    ordered = jnp.concatenate([mom_in_ref[...]] + [mom_conv_ref[tap] for tap in range(TAPS)], axis=0)
    ordered = exact_dot(ordered, order_ref[...], NN)
    rows, part = mom_in_ref.shape[0], mom_conv_ref.shape[1]
    taps = [ordered[rows + tap * part : rows + (tap + 1) * part] for tap in range(TAPS)]
    products = [mom_out_ref[:, unit * H : (unit + 1) * H] for unit in range(UNITS)]
    units = [taps[0:2], [taps[2]] * 2, products, taps[3:5]]
    for slot in range(SLOTS):
        held[slot ^ me_ref[3]] = jnp.concatenate(units[slot] + [ordered[:rows]], axis=0)
    for step, out_ref in enumerate(out_refs):
        out_ref[...] = held[step]


def line_kernel(nz, widths, me_ref, *refs):
    shards, out_refs, held = refs[:nz], refs[nz:-1], refs[-1]
    for number in range(nz):
        held[number] = shards[number][...]
    blocks = [held[me_ref[2] ^ line].astype(F32) for line in range(nz)]
    start = 0
    for out_ref, (groups, rows) in zip(out_refs, widths):
        for group in range(groups):
            stop = start + rows
            joined = jnp.concatenate([block[start:stop] for block in blocks], axis=0).astype(out_ref.dtype)
            if groups == 1:
                out_ref[...] = joined
            else:
                out_ref[group] = joined
            start = stop


def line_in_kernel(nz, rows, me_ref, *refs):
    shards, out_ref, held = refs[:nz], refs[nz], refs[nz + 1]
    for number in range(nz):
        held[number] = shards[number][...]
    blocks = [held[me_ref[2] ^ line].astype(F32) for line in range(nz)]
    joined = [block[:rows] for block in blocks] + [block[rows : rows + 1] for block in blocks]
    left = out_ref.shape[0] - nz * (rows + 1)
    if left:
        joined.append(jnp.zeros((left, H), F32))
    out_ref[...] = jnp.concatenate(joined, axis=0).astype(BF16)


def units_kernel(me_ref, *refs):
    conv_refs, product_refs, (keep_ref, send_ref, held) = refs[:4], refs[4:8], refs[8:]

    def total(parts):
        return functools.reduce(jnp.add, [part.astype(F32) for part in parts]).astype(BF16)

    def tap(number):
        return total([ref[0, number] for ref in conv_refs[:3]] + [conv_refs[3][number]])

    product = total([ref[0] for ref in product_refs[:3]] + [product_refs[3][...]])
    units = [[tap(0), tap(1)], [tap(2)] * 2, [product[:, :H], product[:, H:]], [tap(3), tap(4)]]
    for slot in range(SLOTS):
        for unit in range(UNITS):
            held[slot ^ me_ref[3], unit] = units[slot][unit]
    for number in range(SLOTS // 2):
        keep_ref[number] = held[2 * number]
        send_ref[number] = held[2 * number + 1]


def spread(nz, me_ref, values, out_refs, held):
    natural = values[...].astype(F32)
    sizes = [H // PIECES] * UNITS + [D // PIECES]
    for line in range(nz):
        start, parts = 0, []
        for size in sizes:
            part = size // nz
            parts.append(natural[start + line * part : start + (line + 1) * part])
            start += size
        held[line] = jnp.concatenate(parts, axis=0).astype(BF16)
    for step, out_ref in enumerate(out_refs):
        out_ref[...] = held[me_ref[2] ^ step]


def spread_sums_kernel(nz, me_ref, units_ref, in_ref, *refs):
    out_refs, (held, values) = refs[:-2], refs[-2:]
    rows = units_ref.shape[1]
    for unit in range(UNITS):
        values[unit * rows : (unit + 1) * rows, :] = units_ref[unit].astype(BF16)
    values[UNITS * rows :, :] = in_ref[...].astype(BF16)
    spread(nz, me_ref, values, out_refs, held)


def spread_results_kernel(nz, me_ref, mine_ref, other_ref, *refs):
    out_refs, (held, values) = refs[:-2], refs[-2:]
    rows = H // PIECES
    for unit in range(UNITS):
        place = slice(unit * rows, (unit + 1) * rows)
        mine = (me_ref[3] == SLOT_OUT) | (me_ref[0] == unit)
        values[place, :] = jnp.where(mine, mine_ref[place, :], other_ref[0:rows, :])
    values[UNITS * rows :, :] = jnp.where(me_ref[0] == 0, mine_ref[UNITS * rows :, :], other_ref[rows:, :])
    spread(nz, me_ref, values, out_refs, held)


def rows_of(me_ref, order_ref, shards, held, part):
    for number in range(SLOTS):
        held[number] = shards[number][...]
    slots = [held[slot ^ me_ref[3]] for slot in range(SLOTS)]
    natural = [None if slot == SLOT_OUT else dot(slots[slot], order_ref[...], NT) for slot in range(SLOTS)]
    taps = [natural[slot][unit * part : (unit + 1) * part] for slot, unit in TAP_UNITS]
    products = [slots[SLOT_OUT].astype(F32)[unit * part : (unit + 1) * part] for unit in range(UNITS)]
    return natural[SLOT_IN][UNITS * part :], taps, products


def finish_sums_kernel(me_ref, order_ref, *refs):
    shards, (mom_in, mom_conv, mom_out), rest = refs[:SLOTS], refs[SLOTS : SLOTS + 3], refs[SLOTS + 3 :]
    sum_in, sum_conv, sum_out, new_in, new_conv, new_out, held = rest
    rows, taps, products = rows_of(me_ref, order_ref, shards, held, mom_out.shape[0])
    sum_in[...] = rows
    new_in[...] = MOMENTUM * mom_in[...] + rows
    for tap in range(TAPS):
        sum_conv[tap] = taps[tap]
        new_conv[tap] = MOMENTUM * mom_conv[tap] + taps[tap]
    for unit in range(UNITS):
        columns = slice(unit * H, (unit + 1) * H)
        sum_out[:, columns] = products[unit]
        new_out[:, columns] = MOMENTUM * mom_out[:, columns] + products[unit]


def finish_results_kernel(me_ref, order_ref, *refs):
    shards, (w_in, w_conv, w_out), rest = refs[:SLOTS], refs[SLOTS : SLOTS + 3], refs[SLOTS + 3 :]
    new_in, new_conv, new_out, held = rest
    rows, taps, products = rows_of(me_ref, order_ref, shards, held, w_out.shape[0])
    new_in[...] = w_in[...] - MUON_RATE * rows
    for tap in range(TAPS):
        new_conv[tap] = w_conv[tap] - MUON_RATE * taps[tap]
    for unit in range(UNITS):
        columns = slice(unit * H, (unit + 1) * H)
        new_out[:, columns] = w_out[:, columns] - MUON_RATE * products[unit]


def newton_schulz(x_ref, low_ref, gram_ref, poly_ref, own):
    size, width = x_ref.shape
    square = jnp.sum(x_ref[...] * x_ref[...])
    factor = 1.0 / (jnp.sqrt(square) + 1e-07)
    x_ref[...] = x_ref[...] * factor
    low_ref[...] = x_ref[...].astype(BF16)
    square = square * factor * factor
    for step in range(NS_STEPS):
        shift = square * (1.0 / size)
        for start in range(0, size, 256):
            span = min(256, size - start)
            gram = dot(low_ref[...], low_ref[start : start + span, :], NT)
            row = lax.broadcasted_iota(jnp.int32, (size, span), 0)
            column = lax.broadcasted_iota(jnp.int32, (size, span), 1) + start
            gram_ref[:, start : start + span] = gram - jnp.where(row == column, shift, 0.0)
        gram_low = gram_ref[...].astype(BF16)
        linear = COEF_B + 2.0 * COEF_C * shift
        for start in range(0, size, 256):
            span = min(256, size - start)
            squared = dot(gram_low, gram_low[:, start : start + span])
            poly_ref[:, start : start + span] = (
                linear * gram_ref[:, start : start + span] + COEF_C * squared
            ).astype(BF16)
        coefficient = COEF_A + COEF_B * shift + COEF_C * shift * shift
        if step == NS_STEPS - 1:
            own(coefficient)
            return
        square = jnp.zeros((), F32)
        for start in range(0, width, 256):
            span = min(256, width - start)
            fresh = coefficient * x_ref[:, start : start + span] + dot(
                poly_ref[...], low_ref[:, start : start + span]
            )
            square = square + jnp.sum(fresh * fresh)
            x_ref[:, start : start + span] = fresh
        low_ref[...] = x_ref[...].astype(BF16)


def orth_kernel(me_ref, *refs):
    in_pieces, unit_pieces = refs[:PAIRS], refs[PAIRS : 2 * PAIRS]
    mine_ref, other_ref = refs[2 * PAIRS : 2 * PAIRS + 2]
    held, x_ref, low_ref, wide_ref, wide_low_ref, gram_ref, poly_ref = refs[2 * PAIRS + 2 :]
    slot, core = me_ref[3], me_ref[0]
    is_in = (slot == SLOT_IN) & (core == 0)
    is_out = slot == SLOT_OUT
    places = [(pair, one) for pair in range(PAIRS) for one in range(2)]

    @pl.when(jnp.logical_not(is_in | is_out))
    def _():
        rows = H // PIECES
        for number, (pair, one) in enumerate(places):
            x_ref[number * rows : (number + 1) * rows, :] = unit_pieces[pair][one, core].astype(F32)

        def own(coefficient):
            for start in (0, PLANE * rows):
                part = slice(start, start + rows)
                fresh = (coefficient * x_ref[part, :] + dot(poly_ref[part, :], low_ref[...])).astype(BF16)
                if start == 0:
                    mine_ref[pl.ds(pl.multiple_of(core * rows, 16), rows), :] = fresh
                else:
                    other_ref[0:rows, :] = fresh

        newton_schulz(x_ref, low_ref, gram_ref, poly_ref, own)

    @pl.when(is_out)
    def _():
        rows = H // PIECES
        for number, (pair, one) in enumerate(places):
            for unit in range(UNITS):
                wide_ref[number * rows : (number + 1) * rows, unit * H : (unit + 1) * H] = unit_pieces[pair][
                    one, unit
                ].astype(F32)

    @pl.when(is_in)
    def _():
        rows = D // PIECES
        for number, (pair, one) in enumerate(places):
            held[number * rows : (number + 1) * rows, :] = in_pieces[pair][one].astype(F32)
        for start in range(0, D, 256):
            wide_ref[:, start : start + 256] = held[start : start + 256, :].T

    @pl.when(is_in | is_out)
    def _():
        def own(coefficient):
            @pl.when(is_out)
            def _():
                rows = H // PIECES
                fresh = coefficient * wide_ref[0:rows, :] + dot(poly_ref[0:rows, :], wide_low_ref[...])
                for unit in range(UNITS):
                    mine_ref[unit * rows : (unit + 1) * rows, :] = fresh[:, unit * H : (unit + 1) * H].astype(BF16)

            @pl.when(is_in)
            def _():
                rows = D // PIECES
                for out_ref, start in ((mine_ref, 0), (other_ref, PLANE * rows)):
                    columns = slice(start, start + 256)
                    fresh = coefficient * wide_ref[:, columns] + dot(poly_ref[...], wide_low_ref[:, columns])
                    out_ref[out_ref.shape[0] - rows :, :] = fresh.T[0:rows].astype(BF16)

        newton_schulz(wide_ref, wide_low_ref, gram_ref, poly_ref, own)


class Layout:
    def __init__(self, count):
        self.count = count
        self.lines = count // PIECES
        self.part = H // count
        places = np.arange(H)
        row = places % self.part
        line = places // self.part % self.lines
        plane = places // (self.part * self.lines) % PLANE
        core = places // (self.part * self.lines * PLANE)
        self.natural = ((line * PLANE + plane) * CORES + core) * self.part + row

    def swap(self, values, mask, keep=lambda source, target: True):
        pairs = [(one, one ^ mask) for one in range(self.count)]
        pairs = [pair for pair in pairs if keep(pair[0] // PIECES % SLOTS, pair[1] // PIECES % SLOTS)]
        return lax.ppermute(values, "seq", pairs)

    def swap_line(self, values, step, keep=lambda source, target: True):
        return self.swap(values, step * PIECES, keep)

    def swap_plane(self, values, step, keep=lambda source, target: True):
        pairs = [(one, one ^ (2 if one % CORES == step else 4)) for one in range(self.count)]
        pairs = [pair for pair in pairs if keep(pair[0] // PIECES % SLOTS, pair[1] // PIECES % SLOTS)]
        return lax.ppermute(values, "seq", pairs)

    def along_line(self, values):
        return [values] + [self.swap_line(values, step) for step in range(1, self.lines)]

    def to_all(self, values, keep=lambda source, target: True):
        pair = jnp.stack([values, self.swap_plane(values, 0, keep)])
        far = self.swap_plane(pair, 1, keep)
        return [pair, far, self.swap(pair, 1, keep), self.swap(far, 1, keep)]


def add(*terms):
    return functools.reduce(jnp.add, [term.astype(F32) for term in terms])


def front_outs(rows, width):
    return [shape((rows, width), BF16)] * 3 + [shape((rows, 1), F32)]


def late_spec(rows, width):
    return pl.BlockSpec((rows, width), lambda i: (jnp.maximum(i - 2, 0), 0))


def late_out_specs(rows, width):
    return [late_spec(rows, width)] * 3 + [late_spec(rows, 1)]


def front_out_specs(rows, width):
    return [rows_spec(rows, width)] * 3 + [rows_spec(rows, 1)]


def body(
    count,
    tokens,
    cotangent,
    protein_lengths,
    w_in,
    w_conv,
    w_out,
    vectors,
    mom_in,
    mom_conv,
    mom_out,
    vec_mean,
    vec_square,
):
    lay = Layout(count)
    index = lax.axis_index("seq")
    line_index = index // PIECES
    rows = tokens.shape[0]
    me = jnp.stack(
        [index & 1, (index >> 1) & (PLANE - 1), line_index, line_index % SLOTS, index * rows]
    ).astype(jnp.int32)
    block = 256
    grid = (rows // block,)
    quarter = H // PIECES
    piece_in = D // PIECES
    to_order = jnp.asarray(np.arange(H)[:, None] == lay.natural[None, :], BF16)

    def order_low(values):
        return jnp.dot(values, to_order, preferred_element_type=F32).astype(BF16)

    row_ends = jnp.cumsum(protein_lengths, axis=1) + jnp.arange(protein_lengths.shape[0], dtype=jnp.int32)[:, None] * LEN
    mask_rows = call(
        mask_kernel, 2.0, out_shape=shape((rows, 8), F32), in_specs=[SMEM, VMEM], out_specs=VMEM
    )(me, row_ends.reshape(1, -1))

    edges = [one for one in range(count - 1) if (one + 1) * rows % LEN != 0]
    to_next = [(one, one + 1) for one in edges]
    to_previous = [(one + 1, one) for one in edges]

    part = lay.part
    line = line_index

    def join(shards, widths, outs):
        return call(
            functools.partial(line_kernel, lay.lines, widths),
            2.0,
            out_shape=outs,
            in_specs=[SMEM] + [VMEM] * lay.lines,
            out_specs=[VMEM] * len(outs),
            scratch_shapes=[pltpu.VMEM((lay.lines,) + shards[0].shape, shards[0].dtype)],
        )(me, *shards)

    in_rows = D // count
    shard_rows = UNITS * part + in_rows
    width = vectors.shape[0]
    packed_in = call(
        pack_in_kernel,
        1.0,
        out_shape=shape((-(-(in_rows + 1) // 16) * 16, H), BF16),
        in_specs=[VMEM] * 3,
        out_specs=VMEM,
    )(w_in, jnp.pad(vectors, (0, H - width)).reshape(1, H), to_order)
    line_in = lay.along_line(packed_in)
    packed = call(
        pack_rest_kernel,
        2.0,
        out_shape=shape(((TAPS + UNITS) * part, H), BF16),
        in_specs=[VMEM] * 3,
        out_specs=VMEM,
    )(w_conv, w_out, to_order)
    packed_line = lay.along_line(packed)
    mom_blocks = list(call(
        momenta_kernel,
        2.0,
        out_shape=[shape((shard_rows, H), F32)] * SLOTS,
        in_specs=[SMEM] + [VMEM] * 4,
        out_specs=[VMEM] * SLOTS,
        scratch_shapes=[pltpu.VMEM((SLOTS, shard_rows, H), F32)],
    )(me, mom_in, mom_conv, mom_out, to_order))
    in_own = call(
        functools.partial(line_in_kernel, lay.lines, in_rows),
        2.0,
        out_shape=shape((piece_in + 16, H), BF16),
        in_specs=[SMEM] + [VMEM] * lay.lines,
        out_specs=VMEM,
        scratch_shapes=[pltpu.VMEM((lay.lines,) + packed_in.shape, BF16)],
    )(me, *line_in)
    in_near = lay.swap_plane(in_own, 0)
    token_left, to_left = tie(lax.ppermute(tokens[rows - HALO :], "seq", to_next), tokens[:HALO])
    token_right = lax.ppermute(to_left, "seq", to_previous)
    in_near, mask_rows, mom_blocks[0], *packed_line[1:] = tie(in_near, mask_rows, mom_blocks[0], *packed_line[1:])
    in_pair = jnp.stack([in_own, in_near])
    in_far = lay.swap_plane(in_pair, 1)
    late_in_pair, packed_line[0] = tie(in_pair, packed_line[0])
    conv_own, out_own = join(
        packed_line,
        [(TAPS, part), (UNITS, part)],
        [shape((TAPS, quarter, H), BF16), shape((UNITS, quarter, H), BF16)],
    )
    conv_near = lay.swap_plane(conv_own, 0)
    in_far, conv_own, token_left, token_right = tie(in_far, conv_own, token_left, token_right)
    in_pieces = [late_in_pair, in_far, lay.swap(late_in_pair, 1), lay.swap(in_far, 1)]

    vec_rows = jnp.concatenate([piece[:, piece_in:] for piece in in_pieces]).reshape(-1, H)
    number = jnp.arange(vec_rows.shape[0], dtype=jnp.int32)
    from_core = me[0] ^ (number // (PLANE * 16))
    step = number // 16 % PLANE
    from_plane = me[1] ^ jnp.where(step == 1, 1 + from_core, jnp.where(step == 2, 2 - from_core, step))
    from_index = number % 16 * PIECES + from_plane * CORES + from_core
    pick = (jnp.arange(count, dtype=jnp.int32)[:, None] == from_index[None, :]).astype(BF16)
    vec_all = jnp.dot(pick, vec_rows, preferred_element_type=F32)[:, :width].reshape(-1)
    vec_d = vec_all[: 3 * D].reshape(3, D)
    vec_h = order_low(vec_all[3 * D :].reshape(6, H).astype(BF16)).astype(F32)

    one_halo = call(
        front_halo_kernel,
        5.0,
        grid=(2,),
        out_shape=shape((2 * HALO, D), BF16),
        in_specs=[whole_spec(HALO, D), whole_spec(HALO, D), whole_spec(3, D)],
        out_specs=rows_spec(HALO, D),
    )(token_left, token_right, vec_d)
    conv_near, one_halo = tie(conv_near, one_halo)
    conv_pair = jnp.stack([conv_own, conv_near])
    conv_far = lay.swap_plane(conv_pair, 1)
    late_conv_pair, late_tokens, mom_blocks[1] = tie(conv_pair, tokens, mom_blocks[1])
    mom_lines = [mom_blocks[0]] + [lay.swap_line(mom_blocks[step % SLOTS], step) for step in range(1, lay.lines)]
    one_low, normal_one, slope_one, scale_one = call(
        front_one_kernel,
        6.0,
        grid=grid,
        out_shape=front_outs(rows, D),
        in_specs=[rows_spec(block, D), whole_spec(3, D)],
        out_specs=front_out_specs(block, D),
    )(late_tokens, vec_d)
    one_low, out_own = tie(one_low, out_own)
    out_near = lay.swap_plane(out_own, 0)
    in_low, two_low, normal_two, slope_two, scale_two, two_left, two_right = call(
        functools.partial(first_kernel, lay.lines),
        11.0,
        grid=(2 + rows // block,),
        out_shape=[shape((D, H), BF16)] + front_outs(rows, H) + [shape((HALO, H), BF16)] * 2,
        in_specs=[
            SMEM,
            late_spec(block, D),
            pl.BlockSpec((HALO, D), lambda i: (jnp.minimum(i, 1), 0)),
            whole_spec(6, H),
        ]
        + [ANY] * PAIRS,
        out_specs=[whole_spec(D, H)] + late_out_specs(block, H) + [whole_spec(HALO, H)] * 2,
        scratch_shapes=[pltpu.VMEM((CORES, PLANE, piece_in, H), BF16), pltpu.SemaphoreType.DMA((PIECES,))],
    )(me, one_low, one_halo, vec_h, *in_pieces)
    conv_far, out_near, two_low, *mom_lines[1:] = tie(conv_far, out_near, two_low, *mom_lines[1:])
    conv_pieces = [late_conv_pair, conv_far, lay.swap(late_conv_pair, 1), lay.swap(conv_far, 1)]
    out_pair = jnp.stack([out_own, out_near])
    out_far = lay.swap_plane(out_pair, 1)
    conv_pieces[3], late_out_pair = tie(conv_pieces[3], out_pair)
    conv_scratch = [
        pltpu.VMEM((CORES, PLANE, TAPS, quarter, H), BF16),
        pltpu.SemaphoreType.DMA((PIECES,)),
        pltpu.VMEM((rows + 2 * HALO, H), BF16),
        pltpu.SemaphoreType.DMA((3,)),
    ]
    three_low, normal_three, slope_three, scale_three = call(
        second_kernel,
        11.0,
        grid=grid,
        out_shape=front_outs(rows, H),
        in_specs=[SMEM, rows_spec(block, 8), whole_spec(6, H)] + [ANY] * (3 + PAIRS),
        out_specs=front_out_specs(block, H),
        scratch_shapes=conv_scratch,
    )(me, mask_rows, vec_h, two_low, two_left, two_right, *conv_pieces)

    three_low, out_far = tie(three_low, out_far)
    out_pieces = [late_out_pair, out_far, lay.swap(late_out_pair, 1), lay.swap(out_far, 1)]

    out_low, back_second, sums_three = call(
        back_second_kernel,
        9.0,
        grid=grid,
        out_shape=[shape((H, D), BF16), shape((rows, H), BF16), shape((8, H), F32)],
        in_specs=[SMEM, rows_spec(block, D), whole_spec(6, H), rows_spec(block, H), rows_spec(block, H), rows_spec(block, 1)]
        + [ANY] * PAIRS,
        out_specs=[whole_spec(H, D), rows_spec(block, H), whole_spec(8, H)],
        scratch_shapes=[pltpu.VMEM((CORES, PLANE, UNITS, quarter, H), BF16), pltpu.SemaphoreType.DMA((PIECES,))],
    )(me, cotangent, vec_h, normal_three, slope_three, scale_three, *out_pieces)
    back_left = lax.ppermute(back_second[rows - HALO :], "seq", to_next)
    back_right = lax.ppermute(back_second[:HALO], "seq", to_previous)
    back_second, late_cotangent = tie(back_second, cotangent)
    keep_out, send_out, sum_cot = call(
        grad_out_kernel,
        5.0,
        grid=(D // 256,),
        out_shape=[shape((PLANE, quarter, D), BF16)] * 2 + [shape((8, D), F32)],
        in_specs=[SMEM, whole_spec(rows, H), pl.BlockSpec((rows, 256), lambda i: (0, i))],
        out_specs=[pl.BlockSpec((PLANE, quarter, 256), lambda i: (0, 0, i))] * 2 + [pl.BlockSpec((8, 256), lambda i: (0, i))],
        scratch_shapes=[pltpu.VMEM((CORES, PLANE, quarter, 256), BF16)],
    )(me, three_low, late_cotangent)
    keep_out, send_out, back_left, back_right, late_second = tie(keep_out, send_out, back_left, back_right, back_second)
    keep_conv, send_conv = call(
        grad_conv_kernel,
        8.0,
        grid=(TAPS,),
        out_shape=[shape((PLANE, TAPS, quarter, H), BF16)] * 2,
        in_specs=[SMEM, whole_spec(rows, 8), whole_spec(rows, H)] + [ANY] * 3,
        out_specs=[pl.BlockSpec((PLANE, 1, quarter, H), lambda i: (0, i, 0, 0))] * 2,
        scratch_shapes=[
            pltpu.VMEM((CORES, PLANE, quarter, H), BF16),
            pltpu.VMEM((rows + 2 * HALO, H), BF16),
            pltpu.SemaphoreType.DMA((3,)),
        ],
    )(me, mask_rows, late_second, two_low, two_left, two_right)
    other_out, keep_conv, send_conv, late_tokens = tie(lay.swap(send_out, 1), keep_conv, send_conv, tokens)
    output = call(
        output_kernel,
        5.0,
        grid=grid,
        out_shape=shape((rows, D), BF16),
        in_specs=[rows_spec(block, D), rows_spec(block, H), whole_spec(H, D), whole_spec(3, D)],
        out_specs=rows_spec(block, D),
    )(late_tokens, three_low, out_low, vec_d)
    near_out = lay.swap_plane(add(keep_out[2:], other_out[2:]).astype(BF16), 0)
    other_conv, output = tie(lay.swap(send_conv, 1), output)
    half_conv, late_second = tie(add(keep_conv[2:], other_conv[2:]).astype(BF16), late_second)
    near_conv = lay.swap_plane(half_conv, 0)
    back_first, sums_two = call(
        back_first_kernel,
        10.0,
        grid=grid,
        out_shape=[shape((rows, H), BF16), shape((8, H), F32)],
        in_specs=[SMEM, rows_spec(block, 8), whole_spec(6, H), rows_spec(block, H), rows_spec(block, H), rows_spec(block, 1)]
        + [ANY] * (3 + PAIRS),
        out_specs=[rows_spec(block, H), whole_spec(8, H)],
        scratch_shapes=conv_scratch,
    )(
        me,
        mask_rows,
        vec_h,
        normal_two,
        slope_two,
        scale_two,
        late_second,
        back_left,
        back_right,
        *conv_pieces,
    )
    back_first, mom_lines[0] = tie(back_first, mom_lines[0])
    mom_unit_pieces, mom_in_piece = join(
        mom_lines,
        [(UNITS, part), (1, in_rows)],
        [shape((UNITS, quarter, H), F32), shape((piece_in, H), F32)],
    )
    near_conv, near_out, back_first, mom_unit_pieces = tie(near_conv, near_out, back_first, mom_unit_pieces)
    piece_conv, piece_out, back_first = tie(
        add(keep_conv[1], other_conv[1], near_conv[1]).astype(BF16),
        add(keep_out[1], other_out[1], near_out[1]).astype(BF16),
        back_first,
    )
    far_conv = lay.swap_plane(piece_conv, 1)
    far_out = lay.swap_plane(piece_out, 1)
    keep_in, send_in = call(
        functools.partial(grad_in_kernel, lay.lines),
        6.0,
        out_shape=[shape((PLANE, piece_in, H), BF16)] * 2,
        in_specs=[SMEM, VMEM, VMEM],
        out_specs=[VMEM] * 2,
        scratch_shapes=[pltpu.VMEM((D, H), F32), pltpu.VMEM((CORES, PLANE, piece_in, H), BF16)],
    )(me, one_low, back_first)
    far_conv, far_out, keep_in, send_in = tie(far_conv, far_out, keep_in, send_in)
    other_in = lay.swap(send_in, 1)
    lines = lay.lines
    conv_block, out_block = whole_spec(1, TAPS, quarter, H), whole_spec(1, quarter, D)
    unit_keep, unit_send = call(
        units_kernel,
        3.0,
        grid=(1,),
        out_shape=[shape((SLOTS // 2, UNITS, quarter, H), BF16)] * 2,
        in_specs=[SMEM] + [conv_block] * 3 + [whole_spec(TAPS, quarter, H)] + [out_block] * 3 + [whole_spec(quarter, D)],
        out_specs=[whole_spec(SLOTS // 2, UNITS, quarter, H)] * 2,
        scratch_shapes=[pltpu.VMEM((SLOTS, UNITS, quarter, H), BF16)],
    )(me, keep_conv, other_conv, near_conv, far_conv, keep_out, other_out, near_out, far_out)
    unit_near = lay.swap_line(unit_send, 1)
    other_in, unit_keep = tie(other_in, unit_keep)
    half_in, late_first = tie(add(keep_in[2:], other_in[2:]).astype(BF16), back_first)
    near_in = lay.swap_plane(half_in, 0)
    input_grad, sums_one = call(
        input_grad_kernel,
        8.0,
        grid=grid,
        out_shape=[shape((rows, D), BF16), shape((8, D), F32)],
        in_specs=[
            rows_spec(block, H),
            whole_spec(D, H),
            whole_spec(3, D),
            rows_spec(block, D),
            rows_spec(block, D),
            rows_spec(block, 1),
            rows_spec(block, D),
        ],
        out_specs=[rows_spec(block, D), whole_spec(8, D)],
    )(late_first, in_low, vec_d, normal_one, slope_one, scale_one, cotangent)
    near_in, input_grad = tie(near_in, input_grad)
    piece_in_sum, sums_one = tie(add(keep_in[1], other_in[1], near_in[1]).astype(BF16), sums_one)
    far_in = lay.swap_plane(piece_in_sum, 1)
    vec_terms = call(
        vec_kernel,
        1.0,
        out_shape=shape((6 + 6, H), F32),
        in_specs=[VMEM] * 5,
        out_specs=VMEM,
    )(to_order, sums_one, sum_cot, sums_two, sums_three)
    far_in, vec_terms = tie(far_in, vec_terms)
    in_sum = add(keep_in[0], other_in[0], near_in[0], far_in)
    for step in range(SLOTS, lines):
        if step & (step - 1) == 0:
            in_sum = add(in_sum, lay.swap_line(in_sum.astype(BF16), step))
    in_slot = lambda source, target: target == SLOT_IN
    in_parts = [lay.swap_line(in_sum.astype(BF16), step, in_slot) for step in range(1, SLOTS)]
    unit_half = add(unit_keep, unit_near)
    for step in range(SLOTS, lines):
        if step & (step - 1) == 0:
            unit_half = add(unit_half, lay.swap_line(unit_half.astype(BF16), step))
    unit_far = lay.swap_line(unit_half[1].astype(BF16), 2)
    in_sum = add(in_sum, *in_parts)
    in_moment = (MOMENTUM * mom_in_piece + in_sum).astype(BF16)
    vec_sums = vec_terms + lay.swap(vec_terms, 1)
    unit_far, vec_sums = tie(unit_far, vec_sums)
    unit_sum = add(unit_half[0], unit_far)
    unit_moment = (MOMENTUM * mom_unit_pieces + unit_sum).astype(BF16)

    def orth_scratch(width):
        return [pltpu.VMEM((H, width), F32), pltpu.VMEM((H, width), BF16)]

    vec_sums = vec_sums + lay.swap_plane(vec_sums, 0)
    near, vec_sums = tie(lay.swap_plane(unit_moment, 0), vec_sums)
    unit_pair = jnp.stack([unit_moment, near])
    in_pieces_m = lay.to_all(in_moment, in_slot)
    line_scratch = [
        pltpu.VMEM((lines, shard_rows, H), BF16),
        pltpu.VMEM((UNITS * quarter + piece_in, H), BF16),
    ]

    def spread_line(kernel, *values):
        blocks = call(
            functools.partial(kernel, lines),
            3.0,
            out_shape=[shape((shard_rows, H), BF16)] * SLOTS,
            in_specs=[SMEM] + [VMEM] * len(values),
            out_specs=[VMEM] * SLOTS,
            scratch_shapes=line_scratch,
        )(me, *values)
        return blocks

    def to_line(blocks):
        return [blocks[0]] + [lay.swap_line(blocks[step], step) for step in range(1, SLOTS)]

    sum_shards = to_line(spread_line(spread_sums_kernel, unit_sum, in_sum))
    vec_sums = vec_sums + lay.swap_plane(vec_sums, 1)
    unit_far, vec_sums, *sum_shards[1:] = tie(lay.swap_plane(unit_pair, 1), vec_sums, *sum_shards[1:])
    unit_pieces_m = [unit_pair, unit_far, lay.swap(unit_pair, 1), lay.swap(unit_far, 1)]
    mine, other = call(
        orth_kernel,
        21.0,
        out_shape=[shape((UNITS * quarter + piece_in, H), BF16), shape((quarter + piece_in, H), BF16)],
        in_specs=[SMEM] + [VMEM] * (2 * PAIRS),
        out_specs=[VMEM] * 2,
        scratch_shapes=[pltpu.VMEM((D, H), F32)]
        + orth_scratch(H)
        + orth_scratch(D)
        + [pltpu.VMEM((H, H), F32), pltpu.VMEM((H, H), BF16)],
    )(me, *in_pieces_m, *unit_pieces_m)
    orth_blocks = spread_line(spread_results_kernel, mine, lay.swap(other, 1))
    orth_shards = to_line(orth_blocks)
    orth_shards[0], sum_shards[0] = tie(orth_shards[0], sum_shards[0])
    step = 1
    while step < lines:
        vec_sums = vec_sums + lay.swap_line(vec_sums, step)
        step *= 2
    sum_vec = lax.dynamic_slice_in_dim(vec_sums.reshape(-1), index * width, width)

    def finish(kernel, shards, *values, outs):
        return call(
            kernel,
            2.0,
            out_shape=[shape(one.shape, F32) for one in values] * outs,
            in_specs=[SMEM] + [VMEM] * (SLOTS + 4),
            out_specs=[VMEM] * (3 * outs),
            scratch_shapes=[pltpu.VMEM((SLOTS, shard_rows, H), BF16)],
        )(me, to_order, *shards, *values)

    sum_in, sum_conv, sum_out, moment_in, moment_conv, moment_out = finish(
        finish_sums_kernel, sum_shards, mom_in, mom_conv, mom_out, outs=2
    )
    new_in, new_conv, new_out = finish(finish_results_kernel, orth_shards, w_in, w_conv, w_out, outs=1)

    vec_mean_new = BETA_ONE * vec_mean + (1.0 - BETA_ONE) * sum_vec
    vec_square_new = BETA_TWO * vec_square + (1.0 - BETA_TWO) * sum_vec * sum_vec
    corrected_mean = vec_mean_new / (1.0 - BETA_ONE**STEP)
    corrected_square = vec_square_new / (1.0 - BETA_TWO**STEP)
    vec_new = vectors - ADAM_RATE * corrected_mean / (jnp.sqrt(corrected_square) + ADAM_EPS)
    return (
        output,
        input_grad,
        sum_in,
        sum_conv,
        sum_out,
        moment_in,
        moment_conv,
        moment_out,
        new_in,
        new_conv,
        new_out,
        sum_vec,
        vec_mean_new,
        vec_square_new,
        vec_new,
    )


def solution(mesh):
    matrix, taps, vector = P("seq", None), P(None, "seq", None), P("seq")
    return jax.shard_map(
        functools.partial(body, mesh.shape["seq"]),
        mesh=mesh,
        in_specs=(matrix, matrix, P(), matrix, taps, matrix, vector, matrix, taps, matrix, vector, vector),
        out_specs=(
            matrix,
            matrix,
            matrix,
            taps,
            matrix,
            matrix,
            taps,
            matrix,
            matrix,
            taps,
            matrix,
            vector,
            vector,
            vector,
            vector,
        ),
        check_vma=False,
    )
```

```python
import functools

import jax
import jax.numpy as jnp
import numpy as np
from jax import lax
from jax.experimental import pallas as pl
from jax.experimental.pallas import tpu as pltpu
from jax.sharding import PartitionSpec as P

D = 1280
H = 640
TAPS = 5
DILATION = 128
LEN = 1024
NS_STEPS = 5
STEP = 10
HALO = (TAPS // 2) * DILATION
CORES = 2
PLANE = 4
PIECES = CORES * PLANE
PAIRS = PIECES // 2
UNITS = 2
SLOTS = 4
SLOT_IN = 1
SLOT_OUT = 2
TAP_UNITS = ((0, 0), (0, 1), (1, 1), (3, 0), (3, 1))

EPS = 1e-05
COEF_A = 3.4445
COEF_B = -4.775
COEF_C = 2.0315
MOMENTUM = 0.95
MUON_RATE = 0.5
BETA_ONE = 0.9
BETA_TWO = 0.95
ADAM_RATE = 0.2
ADAM_EPS = 1e-08

F32 = jnp.float32
BF16 = jnp.bfloat16
NN = (((1,), (0,)), ((), ()))
NT = (((1,), (1,)), ((), ()))
TN = (((0,), (0,)), ((), ()))
INV_SQRT2 = 0.7071067811865476
INV_SQRT2PI = 0.3989422804014327
VMEM_LIMIT = 20 << 20
RELATIVE = 0.05

ANY = pl.BlockSpec(memory_space=pl.ANY)
VMEM = pl.BlockSpec(memory_space=pltpu.VMEM)
SMEM = pl.BlockSpec(memory_space=pltpu.SMEM)


def dot(left, right, dims=NN):
    return lax.dot_general(left, right, dims, preferred_element_type=F32)


def call(kernel, micros, **kwargs):
    return pl.pallas_call(
        kernel,
        name=getattr(kernel, "func", kernel).__name__,
        cost_estimate=pl.CostEstimate(flops=int(micros * RELATIVE * 1e9), bytes_accessed=int(micros * RELATIVE * 1e6), transcendentals=0),
        compiler_params=pltpu.CompilerParams(vmem_limit_bytes=VMEM_LIMIT),
        **kwargs,
    )


def tie(*values):
    return lax.optimization_barrier(values)


def shape(dims, dtype):
    return jax.ShapeDtypeStruct(dims, dtype)


def rows_spec(rows, width):
    return pl.BlockSpec((rows, width), lambda i: (i, 0))


def whole_spec(*dims):
    return pl.BlockSpec(dims, lambda i: (0,) * len(dims))


def front(values, gain, shift):
    average = jnp.mean(values, axis=-1, keepdims=True)
    centered = values - average
    scale = lax.rsqrt(jnp.mean(centered * centered, axis=-1, keepdims=True) + EPS)
    normal = centered * scale
    arg = normal * gain + shift
    below = 0.5 + 0.5 * lax.erf(arg * INV_SQRT2)
    slope = below + arg * (jnp.exp(-0.5 * arg * arg) * INV_SQRT2PI)
    return arg * below, normal, slope, scale


def front_back(incoming, gain, normal, slope, scale):
    d_arg = incoming * slope
    d_normal = d_arg * gain
    mean_one = jnp.mean(d_normal, axis=-1, keepdims=True)
    mean_two = jnp.mean(d_normal * normal, axis=-1, keepdims=True)
    grad = (d_normal - mean_one - normal * mean_two) * scale
    gain_grad = jnp.sum(d_arg * normal, axis=0, keepdims=True)
    shift_grad = jnp.sum(d_arg, axis=0, keepdims=True)
    return grad, gain_grad, shift_grad


def load_pieces(me_ref, pieces, held, sems):
    copies = []
    for other in range(CORES):
        core = me_ref[0] ^ other
        for number in range(PLANE):
            place = (0, 1 + core, 2 - core, 3)[number]
            copies.append(
                pltpu.make_async_copy(
                    pieces[2 * other + number // 2].at[number % 2, pl.ds(0, held.shape[2])],
                    held.at[core, me_ref[1] ^ place],
                    sems.at[other * PLANE + number],
                )
            )
    for copy in copies:
        copy.start()
    return copies


def front_one_kernel(tokens_ref, vec_ref, hidden_ref, normal_ref, slope_ref, scale_ref):
    hidden, normal, slope, scale = front(tokens_ref[...].astype(F32), vec_ref[0:1, :], vec_ref[1:2, :])
    hidden_ref[...] = hidden.astype(BF16)
    normal_ref[...] = normal.astype(BF16)
    slope_ref[...] = slope.astype(BF16)
    scale_ref[...] = scale


def front_halo_kernel(left_ref, right_ref, vec_ref, hidden_ref):
    values = jnp.where(pl.program_id(0) == 0, left_ref[...], right_ref[...])
    hidden_ref[...] = front(values.astype(F32), vec_ref[0:1, :], vec_ref[1:2, :])[0].astype(BF16)


def first_kernel(nz, me_ref, hidden_ref, halo_ref, vec_ref, *refs):
    pieces, outs, (held, sems) = refs[:PAIRS], refs[PAIRS:-2], refs[-2:]
    weight_ref, two_ref, normal_ref, slope_ref, scale_ref, left_ref, right_ref = outs
    part = D // PIECES // nz
    step = pl.program_id(0)

    @pl.when(step == 0)
    def _():
        for copy in load_pieces(me_ref, pieces, held, sems):
            copy.wait()
        blocks = [
            [held[core, place].astype(F32) for core in range(CORES)] for place in range(PLANE)
        ]
        for line in range(nz):
            rows = []
            for place in range(PLANE):
                for core in range(CORES):
                    rows.append(blocks[place][core][line * part : (line + 1) * part])
            length = part * PIECES
            weight_ref[line * length : (line + 1) * length, :] = jnp.concatenate(rows, axis=0).astype(BF16)

    values = jnp.where(step < 2, halo_ref[...], hidden_ref[...])
    first = dot(values, weight_ref[...]) + vec_ref[0:1, :]
    hidden, normal, slope, scale = front(first, vec_ref[1:2, :], vec_ref[2:3, :])
    two_ref[...] = hidden.astype(BF16)
    normal_ref[...] = normal.astype(BF16)
    slope_ref[...] = slope.astype(BF16)
    scale_ref[...] = scale

    @pl.when(step == 0)
    def _():
        left_ref[...] = hidden.astype(BF16)

    @pl.when(step == 1)
    def _():
        right_ref[...] = hidden.astype(BF16)


def mask_kernel(me_ref, ends_ref, mask_ref):
    rows = mask_ref.shape[0]
    first = me_ref[4] - HALO
    place = lax.broadcasted_iota(jnp.int32, (rows + 2 * HALO, 1), 0) + first
    ids = jnp.sum((place >= ends_ref[...]).astype(F32), axis=1, keepdims=True)
    ids = jnp.where(place < 0, -1.0, ids)
    column = lax.broadcasted_iota(jnp.int32, mask_ref.shape, 1)
    mask = jnp.zeros(mask_ref.shape, F32)
    for tap in range(TAPS):
        same = ids[tap * DILATION : tap * DILATION + rows] == ids[HALO : HALO + rows]
        mask = mask + jnp.where((column == tap) & same, 1.0, 0.0)
    mask_ref[...] = mask


def masked_tap(mask_ref, ext, start, rows, tap):
    values = ext[pl.ds(pl.multiple_of(start, DILATION), rows), :]
    if tap == TAPS // 2:
        return values
    return values * mask_ref[:, tap : tap + 1].astype(BF16)


def fill_ext(ext, local_ref, left_ref, right_ref, sems):
    rows = local_ref.shape[0]
    copies = [
        pltpu.make_async_copy(left_ref, ext.at[pl.ds(0, HALO)], sems.at[0]),
        pltpu.make_async_copy(local_ref, ext.at[pl.ds(HALO, rows)], sems.at[1]),
        pltpu.make_async_copy(right_ref, ext.at[pl.ds(HALO + rows, HALO)], sems.at[2]),
    ]
    for copy in copies:
        copy.start()
    return copies


def start_conv(me_ref, pieces, held, sems, ext, local_ref, left_ref, right_ref, ext_sems):
    @pl.when(pl.program_id(0) == 0)
    def _():
        copies = load_pieces(me_ref, pieces, held, sems)
        copies += fill_ext(ext, local_ref, left_ref, right_ref, ext_sems)
        for copy in copies:
            copy.wait()


def tap_weight(held, tap):
    return held[:, :, tap].reshape(H, H)


def second_kernel(me_ref, mask_ref, vec_ref, local_ref, left_ref, right_ref, *refs):
    pieces, outs, (held, sems, ext, ext_sems) = refs[:PAIRS], refs[PAIRS:-4], refs[-4:]
    three_ref, normal_ref, slope_ref, scale_ref = outs
    start_conv(me_ref, pieces, held, sems, ext, local_ref, left_ref, right_ref, ext_sems)
    rows = mask_ref.shape[0]
    total = vec_ref[3:4, :]
    for tap in range(TAPS):
        start = pl.program_id(0) * rows + tap * DILATION
        total = total + dot(masked_tap(mask_ref, ext, start, rows, tap), tap_weight(held, tap))
    second = total.astype(BF16).astype(F32)
    hidden, normal, slope, scale = front(second, vec_ref[4:5, :], vec_ref[5:6, :])
    three_ref[...] = hidden.astype(BF16)
    normal_ref[...] = normal.astype(BF16)
    slope_ref[...] = slope.astype(BF16)
    scale_ref[...] = scale


def back_second_kernel(me_ref, cot_ref, vec_ref, normal_ref, slope_ref, scale_ref, *refs):
    pieces, outs, (held, sems) = refs[:PAIRS], refs[PAIRS:-2], refs[-2:]
    weight_ref, back_ref, sums_ref = outs

    @pl.when(pl.program_id(0) == 0)
    def _():
        for copy in load_pieces(me_ref, pieces, held, sems):
            copy.wait()
        for unit in range(UNITS):
            weight_ref[:, unit * H : (unit + 1) * H] = held[:, :, unit].reshape(H, H)
        sums_ref[...] = jnp.zeros_like(sums_ref)

    back_three = dot(cot_ref[...], weight_ref[...], NT)
    grad, gain_grad, shift_grad = front_back(
        back_three, vec_ref[4:5, :], normal_ref[...].astype(F32), slope_ref[...].astype(F32), scale_ref[...]
    )
    back = grad.astype(BF16)
    back_ref[...] = back
    sums_ref[0:1, :] += gain_grad
    sums_ref[1:2, :] += shift_grad
    sums_ref[2:3, :] += jnp.sum(back.astype(F32), axis=0, keepdims=True)


def output_kernel(tokens_ref, three_ref, weight_ref, vec_ref, output_ref):
    product = dot(three_ref[...], weight_ref[...])
    output_ref[...] = (tokens_ref[...].astype(F32) + product + vec_ref[2:3, :]).astype(BF16)


def place_rows(me_ref, held, tiles):
    for core in range(CORES):
        for place in range(PLANE):
            step = me_ref[1] ^ place
            number = step if core else 2 * (step & 1) + (step >> 1)
            held[me_ref[0] ^ core, number] = tiles[core][place]


def grad_out_kernel(me_ref, three_ref, cot_ref, keep_ref, send_ref, sum_ref, held):
    cot = cot_ref[...]
    grad = dot(three_ref[...], cot, TN).astype(BF16)
    quarter = H // PIECES
    tiles = [
        [grad[(core * PLANE + place) * quarter : (core * PLANE + place + 1) * quarter] for place in range(PLANE)]
        for core in range(CORES)
    ]
    place_rows(me_ref, held, tiles)
    keep_ref[...] = held[0]
    send_ref[...] = held[1]
    sum_ref[...] = jnp.broadcast_to(jnp.sum(cot.astype(F32), axis=0, keepdims=True), sum_ref.shape)


def back_first_kernel(
    me_ref, mask_ref, vec_ref, normal_ref, slope_ref, scale_ref, local_ref, left_ref, right_ref, *refs
):
    pieces, outs, (held, sems, ext, ext_sems) = refs[:PAIRS], refs[PAIRS:-4], refs[-4:]
    back_ref, sums_ref = outs
    start_conv(me_ref, pieces, held, sems, ext, local_ref, left_ref, right_ref, ext_sems)

    @pl.when(pl.program_id(0) == 0)
    def _():
        sums_ref[...] = jnp.zeros_like(sums_ref)

    rows = mask_ref.shape[0]
    total = None
    for tap in range(TAPS):
        start = pl.program_id(0) * rows + tap * DILATION
        term = dot(masked_tap(mask_ref, ext, start, rows, tap), tap_weight(held, TAPS - 1 - tap), NT)
        total = term if total is None else total + term
    back_two = total.astype(BF16).astype(F32)
    grad, gain_grad, shift_grad = front_back(
        back_two, vec_ref[1:2, :], normal_ref[...].astype(F32), slope_ref[...].astype(F32), scale_ref[...]
    )
    back = grad.astype(BF16)
    back_ref[...] = back
    sums_ref[0:1, :] += gain_grad
    sums_ref[1:2, :] += shift_grad
    sums_ref[2:3, :] += jnp.sum(back.astype(F32), axis=0, keepdims=True)


def grad_in_kernel(nz, me_ref, one_ref, back_ref, keep_ref, send_ref, grad_ref, held):
    for start in range(0, H, 256):
        width = min(256, H - start)
        grad_ref[:, start : start + width] = dot(one_ref[...], back_ref[:, start : start + width], TN)
    part = D // PIECES // nz
    tiles = []
    for core in range(CORES):
        tiles.append([])
        for place in range(PLANE):
            rows = []
            for line in range(nz):
                first = ((line * PLANE + place) * CORES + core) * part
                rows.append(grad_ref[first : first + part, :])
            tiles[core].append(jnp.concatenate(rows, axis=0).astype(BF16))
    place_rows(me_ref, held, tiles)
    keep_ref[...] = held[0]
    send_ref[...] = held[1]


def grad_conv_kernel(me_ref, mask_ref, back_ref, local_ref, left_ref, right_ref, keep_ref, send_ref, held, ext, ext_sems):
    tap = pl.program_id(0)

    @pl.when(tap == 0)
    def _():
        for copy in fill_ext(ext, local_ref, left_ref, right_ref, ext_sems):
            copy.wait()

    rows = back_ref.shape[0]
    values = ext[pl.ds(pl.multiple_of(tap * DILATION, DILATION), rows), :]
    column = lax.broadcasted_iota(jnp.int32, mask_ref.shape, 1)
    mask = jnp.sum(jnp.where(column == tap, mask_ref[...], 0.0), axis=1, keepdims=True)
    values = values * mask.astype(BF16)
    grad = dot(values, back_ref[...], TN).astype(BF16)
    quarter = H // PIECES
    tiles = [
        [grad[(core * PLANE + place) * quarter : (core * PLANE + place + 1) * quarter] for place in range(PLANE)]
        for core in range(CORES)
    ]
    place_rows(me_ref, held, tiles)
    keep_ref[:, 0] = held[0]
    send_ref[:, 0] = held[1]


def vec_kernel(order_ref, one_ref, cot_ref, two_ref, three_ref, out_ref):
    for number, row in enumerate([one_ref[0:1, :], one_ref[1:2, :], cot_ref[0:1, :]]):
        out_ref[2 * number : 2 * number + 1, :] = row[:, :H]
        out_ref[2 * number + 1 : 2 * number + 2, :] = row[:, H:]
    hidden = jnp.concatenate([two_ref[...], three_ref[...]], axis=0)
    natural = exact_dot(hidden, order_ref[...], NT)
    for number, row in enumerate([2, 0, 1, 10, 8, 9]):
        out_ref[6 + number : 7 + number, :] = natural[row : row + 1, :]


def input_grad_kernel(back_ref, weight_ref, vec_ref, normal_ref, slope_ref, scale_ref, cot_ref, grad_ref, sums_ref):
    @pl.when(pl.program_id(0) == 0)
    def _():
        sums_ref[...] = jnp.zeros_like(sums_ref)

    back_one = dot(back_ref[...], weight_ref[...], NT)
    grad, gain_grad, shift_grad = front_back(
        back_one, vec_ref[0:1, :], normal_ref[...].astype(F32), slope_ref[...].astype(F32), scale_ref[...]
    )
    grad_ref[...] = (cot_ref[...].astype(F32) + grad).astype(BF16)
    sums_ref[0:1, :] += gain_grad
    sums_ref[1:2, :] += shift_grad


def exact_dot(values, order, dims):
    result = 0.0
    for _ in range(3):
        low = values.astype(BF16)
        result = result + dot(low, order, dims)
        values = values - low.astype(F32)
    return result


def pack_in_kernel(w_in_ref, vec_ref, order_ref, packed_ref):
    rows = [dot(w_in_ref[...].astype(BF16), order_ref[...]), vec_ref[...]]
    left = packed_ref.shape[0] - sum(one.shape[0] for one in rows)
    packed_ref[...] = jnp.concatenate(rows + [jnp.zeros((left, H), F32)], axis=0).astype(BF16)


def pack_rest_kernel(w_conv_ref, w_out_ref, order_ref, packed_ref):
    taps = jnp.concatenate([w_conv_ref[tap] for tap in range(TAPS)], axis=0)
    products = [w_out_ref[:, unit * H : (unit + 1) * H] for unit in range(UNITS)]
    packed_ref[...] = jnp.concatenate([dot(taps.astype(BF16), order_ref[...])] + products, axis=0).astype(BF16)


def momenta_kernel(me_ref, mom_in_ref, mom_conv_ref, mom_out_ref, order_ref, *refs):
    out_refs, held = refs[:-1], refs[-1]
    ordered = jnp.concatenate([mom_in_ref[...]] + [mom_conv_ref[tap] for tap in range(TAPS)], axis=0)
    ordered = exact_dot(ordered, order_ref[...], NN)
    rows, part = mom_in_ref.shape[0], mom_conv_ref.shape[1]
    taps = [ordered[rows + tap * part : rows + (tap + 1) * part] for tap in range(TAPS)]
    products = [mom_out_ref[:, unit * H : (unit + 1) * H] for unit in range(UNITS)]
    units = [taps[0:2], [taps[2]] * 2, products, taps[3:5]]
    for slot in range(SLOTS):
        held[slot ^ me_ref[3]] = jnp.concatenate(units[slot] + [ordered[:rows]], axis=0)
    for step, out_ref in enumerate(out_refs):
        out_ref[...] = held[step]


def line_kernel(nz, widths, me_ref, *refs):
    shards, out_refs, held = refs[:nz], refs[nz:-1], refs[-1]
    for number in range(nz):
        held[number] = shards[number][...]
    blocks = [held[me_ref[2] ^ line].astype(F32) for line in range(nz)]
    start = 0
    for out_ref, (groups, rows) in zip(out_refs, widths):
        for group in range(groups):
            stop = start + rows
            joined = jnp.concatenate([block[start:stop] for block in blocks], axis=0).astype(out_ref.dtype)
            if groups == 1:
                out_ref[...] = joined
            else:
                out_ref[group] = joined
            start = stop


def line_in_kernel(nz, rows, me_ref, *refs):
    shards, out_ref, held = refs[:nz], refs[nz], refs[nz + 1]
    for number in range(nz):
        held[number] = shards[number][...]
    blocks = [held[me_ref[2] ^ line].astype(F32) for line in range(nz)]
    joined = [block[:rows] for block in blocks] + [block[rows : rows + 1] for block in blocks]
    left = out_ref.shape[0] - nz * (rows + 1)
    if left:
        joined.append(jnp.zeros((left, H), F32))
    out_ref[...] = jnp.concatenate(joined, axis=0).astype(BF16)


def units_kernel(me_ref, *refs):
    conv_refs, product_refs, (keep_ref, send_ref, held) = refs[:4], refs[4:8], refs[8:]

    def total(parts):
        return functools.reduce(jnp.add, [part.astype(F32) for part in parts]).astype(BF16)

    def tap(number):
        return total([ref[0, number] for ref in conv_refs[:3]] + [conv_refs[3][number]])

    product = total([ref[0] for ref in product_refs[:3]] + [product_refs[3][...]])
    units = [[tap(0), tap(1)], [tap(2)] * 2, [product[:, :H], product[:, H:]], [tap(3), tap(4)]]
    for slot in range(SLOTS):
        for unit in range(UNITS):
            held[slot ^ me_ref[3], unit] = units[slot][unit]
    for number in range(SLOTS // 2):
        keep_ref[number] = held[2 * number]
        send_ref[number] = held[2 * number + 1]


def spread(nz, me_ref, values, out_refs, held):
    natural = values[...].astype(F32)
    sizes = [H // PIECES] * UNITS + [D // PIECES]
    for line in range(nz):
        start, parts = 0, []
        for size in sizes:
            part = size // nz
            parts.append(natural[start + line * part : start + (line + 1) * part])
            start += size
        held[line] = jnp.concatenate(parts, axis=0).astype(BF16)
    for step, out_ref in enumerate(out_refs):
        out_ref[...] = held[me_ref[2] ^ step]


def spread_sums_kernel(nz, me_ref, units_ref, in_ref, *refs):
    out_refs, (held, values) = refs[:-2], refs[-2:]
    rows = units_ref.shape[1]
    for unit in range(UNITS):
        values[unit * rows : (unit + 1) * rows, :] = units_ref[unit].astype(BF16)
    values[UNITS * rows :, :] = in_ref[...].astype(BF16)
    spread(nz, me_ref, values, out_refs, held)


def spread_results_kernel(nz, me_ref, mine_ref, other_ref, *refs):
    out_refs, (held, values) = refs[:-2], refs[-2:]
    rows = H // PIECES
    for unit in range(UNITS):
        place = slice(unit * rows, (unit + 1) * rows)
        mine = (me_ref[3] == SLOT_OUT) | (me_ref[0] == unit)
        values[place, :] = jnp.where(mine, mine_ref[place, :], other_ref[0:rows, :])
    values[UNITS * rows :, :] = jnp.where(me_ref[0] == 0, mine_ref[UNITS * rows :, :], other_ref[rows:, :])
    spread(nz, me_ref, values, out_refs, held)


def rows_of(me_ref, order_ref, shards, held, part):
    for number in range(SLOTS):
        held[number] = shards[number][...]
    slots = [held[slot ^ me_ref[3]] for slot in range(SLOTS)]
    natural = [None if slot == SLOT_OUT else dot(slots[slot], order_ref[...], NT) for slot in range(SLOTS)]
    taps = [natural[slot][unit * part : (unit + 1) * part] for slot, unit in TAP_UNITS]
    products = [slots[SLOT_OUT].astype(F32)[unit * part : (unit + 1) * part] for unit in range(UNITS)]
    return natural[SLOT_IN][UNITS * part :], taps, products


def finish_sums_kernel(me_ref, order_ref, *refs):
    shards, (mom_in, mom_conv, mom_out), rest = refs[:SLOTS], refs[SLOTS : SLOTS + 3], refs[SLOTS + 3 :]
    sum_in, sum_conv, sum_out, new_in, new_conv, new_out, held = rest
    rows, taps, products = rows_of(me_ref, order_ref, shards, held, mom_out.shape[0])
    sum_in[...] = rows
    new_in[...] = MOMENTUM * mom_in[...] + rows
    for tap in range(TAPS):
        sum_conv[tap] = taps[tap]
        new_conv[tap] = MOMENTUM * mom_conv[tap] + taps[tap]
    for unit in range(UNITS):
        columns = slice(unit * H, (unit + 1) * H)
        sum_out[:, columns] = products[unit]
        new_out[:, columns] = MOMENTUM * mom_out[:, columns] + products[unit]


def finish_results_kernel(me_ref, order_ref, *refs):
    shards, (w_in, w_conv, w_out), rest = refs[:SLOTS], refs[SLOTS : SLOTS + 3], refs[SLOTS + 3 :]
    new_in, new_conv, new_out, held = rest
    rows, taps, products = rows_of(me_ref, order_ref, shards, held, w_out.shape[0])
    new_in[...] = w_in[...] - MUON_RATE * rows
    for tap in range(TAPS):
        new_conv[tap] = w_conv[tap] - MUON_RATE * taps[tap]
    for unit in range(UNITS):
        columns = slice(unit * H, (unit + 1) * H)
        new_out[:, columns] = w_out[:, columns] - MUON_RATE * products[unit]


def normalized(x_ref, low_ref):
    square = jnp.sum(x_ref[...] * x_ref[...])
    factor = 1.0 / (jnp.sqrt(square) + 1e-07)
    x_ref[...] = x_ref[...] * factor
    low_ref[...] = x_ref[...].astype(BF16)
    return square * factor * factor


def polynomial(shift, low_ref, gram_ref, poly_ref):
    size = gram_ref.shape[0]
    for start in range(0, size, 256):
        span = min(256, size - start)
        gram = dot(low_ref[...], low_ref[start : start + span, :], NT)
        row = lax.broadcasted_iota(jnp.int32, (size, span), 0)
        column = lax.broadcasted_iota(jnp.int32, (size, span), 1) + start
        gram_ref[:, start : start + span] = gram - jnp.where(row == column, shift, 0.0)
    gram_low = gram_ref[...].astype(BF16)
    linear = COEF_B + 2.0 * COEF_C * shift
    for start in range(0, size, 256):
        span = min(256, size - start)
        squared = dot(gram_low, gram_low[:, start : start + span])
        poly_ref[:, start : start + span] = (
            linear * gram_ref[:, start : start + span] + COEF_C * squared
        ).astype(BF16)
    return COEF_A + COEF_B * shift + COEF_C * shift * shift


def update(coefficient, x_ref, low_ref, poly_ref):
    square = jnp.zeros((), F32)
    for start in range(0, x_ref.shape[1], 256):
        span = min(256, x_ref.shape[1] - start)
        fresh = coefficient * x_ref[:, start : start + span] + dot(poly_ref[...], low_ref[:, start : start + span])
        square = square + jnp.sum(fresh * fresh)
        x_ref[:, start : start + span] = fresh
    low_ref[...] = x_ref[...].astype(BF16)
    return square


def newton_schulz_loop(x_ref, low_ref, gram_ref, poly_ref):
    def step(_, square):
        coefficient = polynomial(square * (1.0 / x_ref.shape[0]), low_ref, gram_ref, poly_ref)
        return update(coefficient, x_ref, low_ref, poly_ref)

    lax.fori_loop(0, NS_STEPS, step, normalized(x_ref, low_ref))


def newton_schulz(x_ref, low_ref, gram_ref, poly_ref, own):
    square = normalized(x_ref, low_ref)
    for step in range(NS_STEPS):
        coefficient = polynomial(square * (1.0 / x_ref.shape[0]), low_ref, gram_ref, poly_ref)
        if step < NS_STEPS - 1:
            square = update(coefficient, x_ref, low_ref, poly_ref)
    own(coefficient)


def orth_kernel(me_ref, *refs):
    in_pieces, unit_pieces = refs[:PAIRS], refs[PAIRS : 2 * PAIRS]
    mine_ref, other_ref = refs[2 * PAIRS : 2 * PAIRS + 2]
    held, x_ref, low_ref, wide_ref, wide_low_ref, gram_ref, poly_ref = refs[2 * PAIRS + 2 :]
    slot, core = me_ref[3], me_ref[0]
    is_in = (slot == SLOT_IN) & (core == 0)
    is_out = slot == SLOT_OUT
    places = [(pair, one) for pair in range(PAIRS) for one in range(2)]

    @pl.when(is_out)
    def _():
        rows = H // PIECES
        for number, (pair, one) in enumerate(places):
            for unit in range(UNITS):
                wide_ref[number * rows : (number + 1) * rows, unit * H : (unit + 1) * H] = unit_pieces[pair][
                    one, unit
                ].astype(F32)

    @pl.when(is_in)
    def _():
        rows = D // PIECES
        for number, (pair, one) in enumerate(places):
            held[number * rows : (number + 1) * rows, :] = in_pieces[pair][one].astype(F32)
        for start in range(0, D, 256):
            wide_ref[:, start : start + 256] = held[start : start + 256, :].T

    @pl.when(is_in | is_out)
    def _():
        def own(coefficient):
            @pl.when(is_out)
            def _():
                rows = H // PIECES
                fresh = coefficient * wide_ref[0:rows, :] + dot(poly_ref[0:rows, :], wide_low_ref[...])
                for unit in range(UNITS):
                    mine_ref[unit * rows : (unit + 1) * rows, :] = fresh[:, unit * H : (unit + 1) * H].astype(BF16)

            @pl.when(is_in)
            def _():
                rows = D // PIECES
                for out_ref, start in ((mine_ref, 0), (other_ref, PLANE * rows)):
                    columns = slice(start, start + 256)
                    fresh = coefficient * wide_ref[:, columns] + dot(poly_ref[...], wide_low_ref[:, columns])
                    out_ref[out_ref.shape[0] - rows :, :] = fresh.T[0:rows].astype(BF16)

        newton_schulz(wide_ref, wide_low_ref, gram_ref, poly_ref, own)

    @pl.when(jnp.logical_not(is_in | is_out))
    def _():
        rows = H // PIECES
        for number, (pair, one) in enumerate(places):
            x_ref[number * rows : (number + 1) * rows, :] = unit_pieces[pair][one, core].astype(F32)

        newton_schulz_loop(x_ref, low_ref, gram_ref, poly_ref)
        mine_ref[pl.ds(pl.multiple_of(core * rows, 16), rows), :] = x_ref[0:rows, :].astype(BF16)
        other_ref[0:rows, :] = x_ref[PLANE * rows : (PLANE + 1) * rows, :].astype(BF16)


class Layout:
    def __init__(self, count):
        self.count = count
        self.lines = count // PIECES
        self.part = H // count
        places = np.arange(H)
        row = places % self.part
        line = places // self.part % self.lines
        plane = places // (self.part * self.lines) % PLANE
        core = places // (self.part * self.lines * PLANE)
        self.natural = ((line * PLANE + plane) * CORES + core) * self.part + row

    def swap(self, values, mask, keep=lambda source, target: True):
        pairs = [(one, one ^ mask) for one in range(self.count)]
        pairs = [pair for pair in pairs if keep(pair[0] // PIECES % SLOTS, pair[1] // PIECES % SLOTS)]
        return lax.ppermute(values, "seq", pairs)

    def swap_line(self, values, step, keep=lambda source, target: True):
        return self.swap(values, step * PIECES, keep)

    def swap_plane(self, values, step, keep=lambda source, target: True):
        pairs = [(one, one ^ (2 if one % CORES == step else 4)) for one in range(self.count)]
        pairs = [pair for pair in pairs if keep(pair[0] // PIECES % SLOTS, pair[1] // PIECES % SLOTS)]
        return lax.ppermute(values, "seq", pairs)

    def along_line(self, values):
        return [values] + [self.swap_line(values, step) for step in range(1, self.lines)]

    def to_all(self, values, keep=lambda source, target: True):
        pair = jnp.stack([values, self.swap_plane(values, 0, keep)])
        far = self.swap_plane(pair, 1, keep)
        return [pair, far, self.swap(pair, 1, keep), self.swap(far, 1, keep)]


def add(*terms):
    return functools.reduce(jnp.add, [term.astype(F32) for term in terms])


def front_outs(rows, width):
    return [shape((rows, width), BF16)] * 3 + [shape((rows, 1), F32)]


def late_spec(rows, width):
    return pl.BlockSpec((rows, width), lambda i: (jnp.maximum(i - 2, 0), 0))


def late_out_specs(rows, width):
    return [late_spec(rows, width)] * 3 + [late_spec(rows, 1)]


def front_out_specs(rows, width):
    return [rows_spec(rows, width)] * 3 + [rows_spec(rows, 1)]


def body(
    count,
    tokens,
    cotangent,
    protein_lengths,
    w_in,
    w_conv,
    w_out,
    vectors,
    mom_in,
    mom_conv,
    mom_out,
    vec_mean,
    vec_square,
):
    lay = Layout(count)
    index = lax.axis_index("seq")
    line_index = index // PIECES
    rows = tokens.shape[0]
    me = jnp.stack(
        [index & 1, (index >> 1) & (PLANE - 1), line_index, line_index % SLOTS, index * rows]
    ).astype(jnp.int32)
    block = 256
    grid = (rows // block,)
    quarter = H // PIECES
    piece_in = D // PIECES
    to_order = jnp.asarray(np.arange(H)[:, None] == lay.natural[None, :], BF16)

    def order_low(values):
        return jnp.dot(values, to_order, preferred_element_type=F32).astype(BF16)

    row_ends = jnp.cumsum(protein_lengths, axis=1) + jnp.arange(protein_lengths.shape[0], dtype=jnp.int32)[:, None] * LEN
    mask_rows = call(
        mask_kernel, 2.0, out_shape=shape((rows, 8), F32), in_specs=[SMEM, VMEM], out_specs=VMEM
    )(me, row_ends.reshape(1, -1))

    edges = [one for one in range(count - 1) if (one + 1) * rows % LEN != 0]
    to_next = [(one, one + 1) for one in edges]
    to_previous = [(one + 1, one) for one in edges]

    part = lay.part
    line = line_index

    def join(shards, widths, outs):
        return call(
            functools.partial(line_kernel, lay.lines, widths),
            2.0,
            out_shape=outs,
            in_specs=[SMEM] + [VMEM] * lay.lines,
            out_specs=[VMEM] * len(outs),
            scratch_shapes=[pltpu.VMEM((lay.lines,) + shards[0].shape, shards[0].dtype)],
        )(me, *shards)

    in_rows = D // count
    shard_rows = UNITS * part + in_rows
    width = vectors.shape[0]
    packed_in = call(
        pack_in_kernel,
        1.0,
        out_shape=shape((-(-(in_rows + 1) // 16) * 16, H), BF16),
        in_specs=[VMEM] * 3,
        out_specs=VMEM,
    )(w_in, jnp.pad(vectors, (0, H - width)).reshape(1, H), to_order)
    line_in = lay.along_line(packed_in)
    packed = call(
        pack_rest_kernel,
        2.0,
        out_shape=shape(((TAPS + UNITS) * part, H), BF16),
        in_specs=[VMEM] * 3,
        out_specs=VMEM,
    )(w_conv, w_out, to_order)
    packed_line = lay.along_line(packed)
    mom_blocks = list(call(
        momenta_kernel,
        2.0,
        out_shape=[shape((shard_rows, H), F32)] * SLOTS,
        in_specs=[SMEM] + [VMEM] * 4,
        out_specs=[VMEM] * SLOTS,
        scratch_shapes=[pltpu.VMEM((SLOTS, shard_rows, H), F32)],
    )(me, mom_in, mom_conv, mom_out, to_order))
    in_own = call(
        functools.partial(line_in_kernel, lay.lines, in_rows),
        2.0,
        out_shape=shape((piece_in + 16, H), BF16),
        in_specs=[SMEM] + [VMEM] * lay.lines,
        out_specs=VMEM,
        scratch_shapes=[pltpu.VMEM((lay.lines,) + packed_in.shape, BF16)],
    )(me, *line_in)
    in_near = lay.swap_plane(in_own, 0)
    token_left, to_left = tie(lax.ppermute(tokens[rows - HALO :], "seq", to_next), tokens[:HALO])
    token_right = lax.ppermute(to_left, "seq", to_previous)
    in_near, mask_rows, mom_blocks[0], *packed_line[1:] = tie(in_near, mask_rows, mom_blocks[0], *packed_line[1:])
    in_pair = jnp.stack([in_own, in_near])
    in_far = lay.swap_plane(in_pair, 1)
    late_in_pair, packed_line[0] = tie(in_pair, packed_line[0])
    conv_own, out_own = join(
        packed_line,
        [(TAPS, part), (UNITS, part)],
        [shape((TAPS, quarter, H), BF16), shape((UNITS, quarter, H), BF16)],
    )
    conv_near = lay.swap_plane(conv_own, 0)
    in_far, conv_own, token_left, token_right = tie(in_far, conv_own, token_left, token_right)
    in_pieces = [late_in_pair, in_far, lay.swap(late_in_pair, 1), lay.swap(in_far, 1)]

    vec_rows = jnp.concatenate([piece[:, piece_in:] for piece in in_pieces]).reshape(-1, H)
    number = jnp.arange(vec_rows.shape[0], dtype=jnp.int32)
    from_core = me[0] ^ (number // (PLANE * 16))
    step = number // 16 % PLANE
    from_plane = me[1] ^ jnp.where(step == 1, 1 + from_core, jnp.where(step == 2, 2 - from_core, step))
    from_index = number % 16 * PIECES + from_plane * CORES + from_core
    pick = (jnp.arange(count, dtype=jnp.int32)[:, None] == from_index[None, :]).astype(BF16)
    vec_all = jnp.dot(pick, vec_rows, preferred_element_type=F32)[:, :width].reshape(-1)
    vec_d = vec_all[: 3 * D].reshape(3, D)
    vec_h = order_low(vec_all[3 * D :].reshape(6, H).astype(BF16)).astype(F32)

    one_halo = call(
        front_halo_kernel,
        5.0,
        grid=(2,),
        out_shape=shape((2 * HALO, D), BF16),
        in_specs=[whole_spec(HALO, D), whole_spec(HALO, D), whole_spec(3, D)],
        out_specs=rows_spec(HALO, D),
    )(token_left, token_right, vec_d)
    conv_near, one_halo = tie(conv_near, one_halo)
    conv_pair = jnp.stack([conv_own, conv_near])
    conv_far = lay.swap_plane(conv_pair, 1)
    late_conv_pair, late_tokens, mom_blocks[1] = tie(conv_pair, tokens, mom_blocks[1])
    mom_lines = [mom_blocks[0]] + [lay.swap_line(mom_blocks[step % SLOTS], step) for step in range(1, lay.lines)]
    one_low, normal_one, slope_one, scale_one = call(
        front_one_kernel,
        6.0,
        grid=grid,
        out_shape=front_outs(rows, D),
        in_specs=[rows_spec(block, D), whole_spec(3, D)],
        out_specs=front_out_specs(block, D),
    )(late_tokens, vec_d)
    one_low, out_own = tie(one_low, out_own)
    out_near = lay.swap_plane(out_own, 0)
    in_low, two_low, normal_two, slope_two, scale_two, two_left, two_right = call(
        functools.partial(first_kernel, lay.lines),
        11.0,
        grid=(2 + rows // block,),
        out_shape=[shape((D, H), BF16)] + front_outs(rows, H) + [shape((HALO, H), BF16)] * 2,
        in_specs=[
            SMEM,
            late_spec(block, D),
            pl.BlockSpec((HALO, D), lambda i: (jnp.minimum(i, 1), 0)),
            whole_spec(6, H),
        ]
        + [ANY] * PAIRS,
        out_specs=[whole_spec(D, H)] + late_out_specs(block, H) + [whole_spec(HALO, H)] * 2,
        scratch_shapes=[pltpu.VMEM((CORES, PLANE, piece_in, H), BF16), pltpu.SemaphoreType.DMA((PIECES,))],
    )(me, one_low, one_halo, vec_h, *in_pieces)
    conv_far, out_near, two_low, *mom_lines[1:] = tie(conv_far, out_near, two_low, *mom_lines[1:])
    conv_pieces = [late_conv_pair, conv_far, lay.swap(late_conv_pair, 1), lay.swap(conv_far, 1)]
    out_pair = jnp.stack([out_own, out_near])
    out_far = lay.swap_plane(out_pair, 1)
    conv_pieces[3], late_out_pair = tie(conv_pieces[3], out_pair)
    conv_scratch = [
        pltpu.VMEM((CORES, PLANE, TAPS, quarter, H), BF16),
        pltpu.SemaphoreType.DMA((PIECES,)),
        pltpu.VMEM((rows + 2 * HALO, H), BF16),
        pltpu.SemaphoreType.DMA((3,)),
    ]
    three_low, normal_three, slope_three, scale_three = call(
        second_kernel,
        11.0,
        grid=grid,
        out_shape=front_outs(rows, H),
        in_specs=[SMEM, rows_spec(block, 8), whole_spec(6, H)] + [ANY] * (3 + PAIRS),
        out_specs=front_out_specs(block, H),
        scratch_shapes=conv_scratch,
    )(me, mask_rows, vec_h, two_low, two_left, two_right, *conv_pieces)

    three_low, out_far = tie(three_low, out_far)
    out_pieces = [late_out_pair, out_far, lay.swap(late_out_pair, 1), lay.swap(out_far, 1)]

    keep_out, send_out, sum_cot = call(
        grad_out_kernel,
        5.0,
        grid=(D // 256,),
        out_shape=[shape((PLANE, quarter, D), BF16)] * 2 + [shape((8, D), F32)],
        in_specs=[SMEM, whole_spec(rows, H), pl.BlockSpec((rows, 256), lambda i: (0, i))],
        out_specs=[pl.BlockSpec((PLANE, quarter, 256), lambda i: (0, 0, i))] * 2 + [pl.BlockSpec((8, 256), lambda i: (0, i))],
        scratch_shapes=[pltpu.VMEM((CORES, PLANE, quarter, 256), BF16)],
    )(me, three_low, cotangent)
    late_cotangent, keep_out = tie(cotangent, keep_out)
    out_low, back_second, sums_three = call(
        back_second_kernel,
        9.0,
        grid=grid,
        out_shape=[shape((H, D), BF16), shape((rows, H), BF16), shape((8, H), F32)],
        in_specs=[SMEM, rows_spec(block, D), whole_spec(6, H), rows_spec(block, H), rows_spec(block, H), rows_spec(block, 1)]
        + [ANY] * PAIRS,
        out_specs=[whole_spec(H, D), rows_spec(block, H), whole_spec(8, H)],
        scratch_shapes=[pltpu.VMEM((CORES, PLANE, UNITS, quarter, H), BF16), pltpu.SemaphoreType.DMA((PIECES,))],
    )(me, late_cotangent, vec_h, normal_three, slope_three, scale_three, *out_pieces)
    back_left = lax.ppermute(back_second[rows - HALO :], "seq", to_next)
    back_right = lax.ppermute(back_second[:HALO], "seq", to_previous)
    other_out, late_second = tie(lay.swap(send_out, 1), back_second)
    half_out, late_second = tie(add(keep_out[2:], other_out[2:]).astype(BF16), late_second)
    near_out = lay.swap_plane(half_out, 0)
    keep_conv, send_conv = call(
        grad_conv_kernel,
        8.0,
        grid=(TAPS,),
        out_shape=[shape((PLANE, TAPS, quarter, H), BF16)] * 2,
        in_specs=[SMEM, whole_spec(rows, 8), whole_spec(rows, H)] + [ANY] * 3,
        out_specs=[pl.BlockSpec((PLANE, 1, quarter, H), lambda i: (0, i, 0, 0))] * 2,
        scratch_shapes=[
            pltpu.VMEM((CORES, PLANE, quarter, H), BF16),
            pltpu.VMEM((rows + 2 * HALO, H), BF16),
            pltpu.SemaphoreType.DMA((3,)),
        ],
    )(me, mask_rows, late_second, two_low, two_left, two_right)
    near_out, back_left, back_right, keep_conv, send_conv, late_tokens = tie(
        near_out, back_left, back_right, keep_conv, send_conv, tokens
    )
    far_out = lay.swap_plane(add(keep_out[1], other_out[1], near_out[1]).astype(BF16), 1)
    output = call(
        output_kernel,
        5.0,
        grid=grid,
        out_shape=shape((rows, D), BF16),
        in_specs=[rows_spec(block, D), rows_spec(block, H), whole_spec(H, D), whole_spec(3, D)],
        out_specs=rows_spec(block, D),
    )(late_tokens, three_low, out_low, vec_d)
    other_conv, output = tie(lay.swap(send_conv, 1), output)
    half_conv, late_second = tie(add(keep_conv[2:], other_conv[2:]).astype(BF16), late_second)
    near_conv = lay.swap_plane(half_conv, 0)
    back_first, sums_two = call(
        back_first_kernel,
        10.0,
        grid=grid,
        out_shape=[shape((rows, H), BF16), shape((8, H), F32)],
        in_specs=[SMEM, rows_spec(block, 8), whole_spec(6, H), rows_spec(block, H), rows_spec(block, H), rows_spec(block, 1)]
        + [ANY] * (3 + PAIRS),
        out_specs=[rows_spec(block, H), whole_spec(8, H)],
        scratch_shapes=conv_scratch,
    )(
        me,
        mask_rows,
        vec_h,
        normal_two,
        slope_two,
        scale_two,
        late_second,
        back_left,
        back_right,
        *conv_pieces,
    )
    back_first, mom_lines[0] = tie(back_first, mom_lines[0])
    mom_unit_pieces, mom_in_piece = join(
        mom_lines,
        [(UNITS, part), (1, in_rows)],
        [shape((UNITS, quarter, H), F32), shape((piece_in, H), F32)],
    )
    near_conv, far_out, back_first, mom_unit_pieces = tie(near_conv, far_out, back_first, mom_unit_pieces)
    piece_conv, back_first = tie(add(keep_conv[1], other_conv[1], near_conv[1]).astype(BF16), back_first)
    far_conv = lay.swap_plane(piece_conv, 1)
    keep_in, send_in = call(
        functools.partial(grad_in_kernel, lay.lines),
        6.0,
        out_shape=[shape((PLANE, piece_in, H), BF16)] * 2,
        in_specs=[SMEM, VMEM, VMEM],
        out_specs=[VMEM] * 2,
        scratch_shapes=[pltpu.VMEM((D, H), F32), pltpu.VMEM((CORES, PLANE, piece_in, H), BF16)],
    )(me, one_low, back_first)
    far_conv, keep_in, send_in = tie(far_conv, keep_in, send_in)
    other_in = lay.swap(send_in, 1)
    lines = lay.lines
    conv_block, out_block = whole_spec(1, TAPS, quarter, H), whole_spec(1, quarter, D)
    unit_keep, unit_send = call(
        units_kernel,
        3.0,
        grid=(1,),
        out_shape=[shape((SLOTS // 2, UNITS, quarter, H), BF16)] * 2,
        in_specs=[SMEM] + [conv_block] * 3 + [whole_spec(TAPS, quarter, H)] + [out_block] * 3 + [whole_spec(quarter, D)],
        out_specs=[whole_spec(SLOTS // 2, UNITS, quarter, H)] * 2,
        scratch_shapes=[pltpu.VMEM((SLOTS, UNITS, quarter, H), BF16)],
    )(me, keep_conv, other_conv, near_conv, far_conv, keep_out, other_out, near_out, far_out)
    unit_near = lay.swap_line(unit_send, 1)
    other_in, unit_keep = tie(other_in, unit_keep)
    half_in, late_first = tie(add(keep_in[2:], other_in[2:]).astype(BF16), back_first)
    near_in = lay.swap_plane(half_in, 0)
    input_grad, sums_one = call(
        input_grad_kernel,
        8.0,
        grid=grid,
        out_shape=[shape((rows, D), BF16), shape((8, D), F32)],
        in_specs=[
            rows_spec(block, H),
            whole_spec(D, H),
            whole_spec(3, D),
            rows_spec(block, D),
            rows_spec(block, D),
            rows_spec(block, 1),
            rows_spec(block, D),
        ],
        out_specs=[rows_spec(block, D), whole_spec(8, D)],
    )(late_first, in_low, vec_d, normal_one, slope_one, scale_one, cotangent)
    near_in, input_grad = tie(near_in, input_grad)
    piece_in_sum, sums_one = tie(add(keep_in[1], other_in[1], near_in[1]).astype(BF16), sums_one)
    far_in = lay.swap_plane(piece_in_sum, 1)
    vec_terms = call(
        vec_kernel,
        1.0,
        out_shape=shape((6 + 6, H), F32),
        in_specs=[VMEM] * 5,
        out_specs=VMEM,
    )(to_order, sums_one, sum_cot, sums_two, sums_three)
    unit_half = add(unit_keep, unit_near)
    for step in range(SLOTS, lines):
        if step & (step - 1) == 0:
            unit_half = add(unit_half, lay.swap_line(unit_half.astype(BF16), step))
    far_in, vec_terms, unit_low = tie(far_in, vec_terms, unit_half[1].astype(BF16))
    unit_far = lay.swap_line(unit_low, 2)
    in_sum = add(keep_in[0], other_in[0], near_in[0], far_in)
    for step in range(SLOTS, lines):
        if step & (step - 1) == 0:
            in_sum = add(in_sum, lay.swap_line(in_sum.astype(BF16), step))
    in_slot = lambda source, target: target == SLOT_IN
    in_parts = [lay.swap_line(in_sum.astype(BF16), step, in_slot) for step in range(1, SLOTS)]
    in_sum = add(in_sum, *in_parts)
    in_moment = (MOMENTUM * mom_in_piece + in_sum).astype(BF16)
    vec_sums = vec_terms + lay.swap(vec_terms, 1)
    vec_sums = vec_sums + lay.swap_plane(vec_sums, 0)
    unit_far, vec_sums = tie(unit_far, vec_sums)
    unit_sum = add(unit_half[0], unit_far)
    unit_moment = (MOMENTUM * mom_unit_pieces + unit_sum).astype(BF16)

    def orth_scratch(width):
        return [pltpu.VMEM((H, width), F32), pltpu.VMEM((H, width), BF16)]

    vec_sums = vec_sums + lay.swap_plane(vec_sums, 1)
    near, vec_sums = tie(lay.swap_plane(unit_moment, 0), vec_sums)
    unit_pair = jnp.stack([unit_moment, near])
    in_pieces_m = lay.to_all(in_moment, in_slot)
    line_scratch = [
        pltpu.VMEM((lines, shard_rows, H), BF16),
        pltpu.VMEM((UNITS * quarter + piece_in, H), BF16),
    ]

    def spread_line(kernel, *values):
        blocks = call(
            functools.partial(kernel, lines),
            3.0,
            out_shape=[shape((shard_rows, H), BF16)] * SLOTS,
            in_specs=[SMEM] + [VMEM] * len(values),
            out_specs=[VMEM] * SLOTS,
            scratch_shapes=line_scratch,
        )(me, *values)
        return blocks

    def to_line(blocks):
        return [blocks[0]] + [lay.swap_line(blocks[step], step) for step in range(1, SLOTS)]

    sum_shards = to_line(spread_line(spread_sums_kernel, unit_sum, in_sum))
    vec_sums = vec_sums + lay.swap_line(vec_sums, 1)
    unit_far, vec_sums, *sum_shards[1:] = tie(lay.swap_plane(unit_pair, 1), vec_sums, *sum_shards[1:])
    unit_pieces_m = [unit_pair, unit_far, lay.swap(unit_pair, 1), lay.swap(unit_far, 1)]
    mine, other = call(
        orth_kernel,
        21.0,
        out_shape=[shape((UNITS * quarter + piece_in, H), BF16), shape((quarter + piece_in, H), BF16)],
        in_specs=[SMEM] + [VMEM] * (2 * PAIRS),
        out_specs=[VMEM] * 2,
        scratch_shapes=[pltpu.VMEM((D, H), F32)]
        + orth_scratch(H)
        + orth_scratch(D)
        + [pltpu.VMEM((H, H), F32), pltpu.VMEM((H, H), BF16)],
    )(me, *in_pieces_m, *unit_pieces_m)
    orth_blocks = spread_line(spread_results_kernel, mine, lay.swap(other, 1))
    orth_blocks = list(orth_blocks)
    orth_blocks[0], vec_sums = tie(orth_blocks[0], vec_sums)
    step = 2
    while step < lines:
        vec_sums = vec_sums + lay.swap_line(vec_sums, step)
        step *= 2
    orth_shards = to_line(orth_blocks)
    orth_shards[0], sum_shards[0] = tie(orth_shards[0], sum_shards[0])
    orth_shards[1], vec_sums = tie(orth_shards[1], vec_sums)
    sum_vec = lax.dynamic_slice_in_dim(vec_sums.reshape(-1), index * width, width)

    def finish(kernel, shards, *values, outs):
        return call(
            kernel,
            2.0,
            out_shape=[shape(one.shape, F32) for one in values] * outs,
            in_specs=[SMEM] + [VMEM] * (SLOTS + 4),
            out_specs=[VMEM] * (3 * outs),
            scratch_shapes=[pltpu.VMEM((SLOTS, shard_rows, H), BF16)],
        )(me, to_order, *shards, *values)

    sum_in, sum_conv, sum_out, moment_in, moment_conv, moment_out = finish(
        finish_sums_kernel, sum_shards, mom_in, mom_conv, mom_out, outs=2
    )
    new_in, new_conv, new_out = finish(finish_results_kernel, orth_shards, w_in, w_conv, w_out, outs=1)

    vec_mean_new = BETA_ONE * vec_mean + (1.0 - BETA_ONE) * sum_vec
    vec_square_new = BETA_TWO * vec_square + (1.0 - BETA_TWO) * sum_vec * sum_vec
    corrected_mean = vec_mean_new / (1.0 - BETA_ONE**STEP)
    corrected_square = vec_square_new / (1.0 - BETA_TWO**STEP)
    vec_new = vectors - ADAM_RATE * corrected_mean / (jnp.sqrt(corrected_square) + ADAM_EPS)
    return (
        output,
        input_grad,
        sum_in,
        sum_conv,
        sum_out,
        moment_in,
        moment_conv,
        moment_out,
        new_in,
        new_conv,
        new_out,
        sum_vec,
        vec_mean_new,
        vec_square_new,
        vec_new,
    )


def solution(mesh):
    matrix, taps, vector = P("seq", None), P(None, "seq", None), P("seq")
    return jax.shard_map(
        functools.partial(body, mesh.shape["seq"]),
        mesh=mesh,
        in_specs=(matrix, matrix, P(), matrix, taps, matrix, vector, matrix, taps, matrix, vector, vector),
        out_specs=(
            matrix,
            matrix,
            matrix,
            taps,
            matrix,
            matrix,
            taps,
            matrix,
            matrix,
            taps,
            matrix,
            vector,
            vector,
            vector,
            vector,
        ),
        check_vma=False,
    )
```

```python
import functools

import jax
import jax.numpy as jnp
import numpy as np
from jax import lax
from jax.experimental import pallas as pl
from jax.experimental.pallas import tpu as pltpu
from jax.sharding import PartitionSpec as P

D = 1280
H = 640
TAPS = 5
DILATION = 128
LEN = 1024
NS_STEPS = 5
STEP = 10
HALO = (TAPS // 2) * DILATION
CORES = 2
PLANE = 4
PIECES = CORES * PLANE
PAIRS = PIECES // 2
UNITS = 2
SLOTS = 4
SLOT_IN = 1
SLOT_OUT = 2
TAP_UNITS = ((0, 0), (0, 1), (1, 1), (3, 0), (3, 1))

EPS = 1e-05
COEF_A = 3.4445
COEF_B = -4.775
COEF_C = 2.0315
MOMENTUM = 0.95
MUON_RATE = 0.5
BETA_ONE = 0.9
BETA_TWO = 0.95
ADAM_RATE = 0.2
ADAM_EPS = 1e-08

F32 = jnp.float32
BF16 = jnp.bfloat16
NN = (((1,), (0,)), ((), ()))
NT = (((1,), (1,)), ((), ()))
TN = (((0,), (0,)), ((), ()))
INV_SQRT2 = 0.7071067811865476
INV_SQRT2PI = 0.3989422804014327
VMEM_LIMIT = 20 << 20
RELATIVE = 0.05

ANY = pl.BlockSpec(memory_space=pl.ANY)
VMEM = pl.BlockSpec(memory_space=pltpu.VMEM)
SMEM = pl.BlockSpec(memory_space=pltpu.SMEM)


def dot(left, right, dims=NN):
    return lax.dot_general(left, right, dims, preferred_element_type=F32)


def call(kernel, micros, **kwargs):
    return pl.pallas_call(
        kernel,
        name=getattr(kernel, "func", kernel).__name__,
        cost_estimate=pl.CostEstimate(flops=int(micros * RELATIVE * 1e9), bytes_accessed=int(micros * RELATIVE * 1e6), transcendentals=0),
        compiler_params=pltpu.CompilerParams(vmem_limit_bytes=VMEM_LIMIT),
        **kwargs,
    )


def tie(*values):
    return lax.optimization_barrier(values)


def shape(dims, dtype):
    return jax.ShapeDtypeStruct(dims, dtype)


def rows_spec(rows, width):
    return pl.BlockSpec((rows, width), lambda i: (i, 0))


def whole_spec(*dims):
    return pl.BlockSpec(dims, lambda i: (0,) * len(dims))


def front(values, gain, shift):
    average = jnp.mean(values, axis=-1, keepdims=True)
    centered = values - average
    scale = lax.rsqrt(jnp.mean(centered * centered, axis=-1, keepdims=True) + EPS)
    normal = centered * scale
    arg = normal * gain + shift
    below = 0.5 + 0.5 * lax.erf(arg * INV_SQRT2)
    slope = below + arg * (jnp.exp(-0.5 * arg * arg) * INV_SQRT2PI)
    return arg * below, normal, slope, scale


def front_back(incoming, gain, normal, slope, scale):
    d_arg = incoming * slope
    d_normal = d_arg * gain
    mean_one = jnp.mean(d_normal, axis=-1, keepdims=True)
    mean_two = jnp.mean(d_normal * normal, axis=-1, keepdims=True)
    grad = (d_normal - mean_one - normal * mean_two) * scale
    gain_grad = jnp.sum(d_arg * normal, axis=0, keepdims=True)
    shift_grad = jnp.sum(d_arg, axis=0, keepdims=True)
    return grad, gain_grad, shift_grad


def load_pieces(me_ref, pieces, held, sems):
    copies = []
    for other in range(CORES):
        core = me_ref[0] ^ other
        for number in range(PLANE):
            place = (0, 1 + core, 2 - core, 3)[number]
            copies.append(
                pltpu.make_async_copy(
                    pieces[2 * other + number // 2].at[number % 2, pl.ds(0, held.shape[2])],
                    held.at[core, me_ref[1] ^ place],
                    sems.at[other * PLANE + number],
                )
            )
    for copy in copies:
        copy.start()
    return copies


def front_one_kernel(tokens_ref, vec_ref, hidden_ref, normal_ref, slope_ref, scale_ref):
    hidden, normal, slope, scale = front(tokens_ref[...].astype(F32), vec_ref[0:1, :], vec_ref[1:2, :])
    hidden_ref[...] = hidden.astype(BF16)
    normal_ref[...] = normal.astype(BF16)
    slope_ref[...] = slope.astype(BF16)
    scale_ref[...] = scale


def front_halo_kernel(left_ref, right_ref, vec_ref, hidden_ref):
    values = jnp.where(pl.program_id(0) == 0, left_ref[...], right_ref[...])
    hidden_ref[...] = front(values.astype(F32), vec_ref[0:1, :], vec_ref[1:2, :])[0].astype(BF16)


def first_kernel(nz, me_ref, hidden_ref, halo_ref, vec_ref, *refs):
    pieces, outs, (held, sems) = refs[:PAIRS], refs[PAIRS:-2], refs[-2:]
    weight_ref, two_ref, normal_ref, slope_ref, scale_ref, left_ref, right_ref = outs
    part = D // PIECES // nz
    step = pl.program_id(0)

    @pl.when(step == 0)
    def _():
        for copy in load_pieces(me_ref, pieces, held, sems):
            copy.wait()
        blocks = [
            [held[core, place].astype(F32) for core in range(CORES)] for place in range(PLANE)
        ]
        for line in range(nz):
            rows = []
            for place in range(PLANE):
                for core in range(CORES):
                    rows.append(blocks[place][core][line * part : (line + 1) * part])
            length = part * PIECES
            weight_ref[line * length : (line + 1) * length, :] = jnp.concatenate(rows, axis=0).astype(BF16)

    values = jnp.where(step < 2, halo_ref[...], hidden_ref[...])
    first = dot(values, weight_ref[...]) + vec_ref[0:1, :]
    hidden, normal, slope, scale = front(first, vec_ref[1:2, :], vec_ref[2:3, :])
    two_ref[...] = hidden.astype(BF16)
    normal_ref[...] = normal.astype(BF16)
    slope_ref[...] = slope.astype(BF16)
    scale_ref[...] = scale

    @pl.when(step == 0)
    def _():
        left_ref[...] = hidden.astype(BF16)

    @pl.when(step == 1)
    def _():
        right_ref[...] = hidden.astype(BF16)


def mask_kernel(me_ref, ends_ref, mask_ref):
    rows = mask_ref.shape[0]
    first = me_ref[4] - HALO
    place = lax.broadcasted_iota(jnp.int32, (rows + 2 * HALO, 1), 0) + first
    ids = jnp.sum((place >= ends_ref[...]).astype(F32), axis=1, keepdims=True)
    ids = jnp.where(place < 0, -1.0, ids)
    column = lax.broadcasted_iota(jnp.int32, mask_ref.shape, 1)
    mask = jnp.zeros(mask_ref.shape, F32)
    for tap in range(TAPS):
        same = ids[tap * DILATION : tap * DILATION + rows] == ids[HALO : HALO + rows]
        mask = mask + jnp.where((column == tap) & same, 1.0, 0.0)
    mask_ref[...] = mask


def masked_tap(mask_ref, ext, start, rows, tap):
    values = ext[pl.ds(pl.multiple_of(start, DILATION), rows), :]
    if tap == TAPS // 2:
        return values
    return values * mask_ref[:, tap : tap + 1].astype(BF16)


def fill_ext(ext, local_ref, left_ref, right_ref, sems):
    rows = local_ref.shape[0]
    copies = [
        pltpu.make_async_copy(left_ref, ext.at[pl.ds(0, HALO)], sems.at[0]),
        pltpu.make_async_copy(local_ref, ext.at[pl.ds(HALO, rows)], sems.at[1]),
        pltpu.make_async_copy(right_ref, ext.at[pl.ds(HALO + rows, HALO)], sems.at[2]),
    ]
    for copy in copies:
        copy.start()
    return copies


def start_conv(me_ref, pieces, held, sems, ext, local_ref, left_ref, right_ref, ext_sems):
    @pl.when(pl.program_id(0) == 0)
    def _():
        copies = load_pieces(me_ref, pieces, held, sems)
        copies += fill_ext(ext, local_ref, left_ref, right_ref, ext_sems)
        for copy in copies:
            copy.wait()


def tap_weight(held, tap):
    return held[:, :, tap].reshape(H, H)


def second_kernel(me_ref, mask_ref, vec_ref, local_ref, left_ref, right_ref, *refs):
    pieces, outs, (held, sems, ext, ext_sems) = refs[:PAIRS], refs[PAIRS:-4], refs[-4:]
    three_ref, normal_ref, slope_ref, scale_ref = outs
    start_conv(me_ref, pieces, held, sems, ext, local_ref, left_ref, right_ref, ext_sems)
    rows = mask_ref.shape[0]
    total = vec_ref[3:4, :]
    for tap in range(TAPS):
        start = pl.program_id(0) * rows + tap * DILATION
        total = total + dot(masked_tap(mask_ref, ext, start, rows, tap), tap_weight(held, tap))
    second = total.astype(BF16).astype(F32)
    hidden, normal, slope, scale = front(second, vec_ref[4:5, :], vec_ref[5:6, :])
    three_ref[...] = hidden.astype(BF16)
    normal_ref[...] = normal.astype(BF16)
    slope_ref[...] = slope.astype(BF16)
    scale_ref[...] = scale


def back_second_kernel(me_ref, cot_ref, vec_ref, normal_ref, slope_ref, scale_ref, *refs):
    pieces, outs, (held, sems) = refs[:PAIRS], refs[PAIRS:-2], refs[-2:]
    weight_ref, back_ref, sums_ref = outs

    @pl.when(pl.program_id(0) == 0)
    def _():
        for copy in load_pieces(me_ref, pieces, held, sems):
            copy.wait()
        for unit in range(UNITS):
            weight_ref[:, unit * H : (unit + 1) * H] = held[:, :, unit].reshape(H, H)
        sums_ref[...] = jnp.zeros_like(sums_ref)

    back_three = dot(cot_ref[...], weight_ref[...], NT)
    grad, gain_grad, shift_grad = front_back(
        back_three, vec_ref[4:5, :], normal_ref[...].astype(F32), slope_ref[...].astype(F32), scale_ref[...]
    )
    back = grad.astype(BF16)
    back_ref[...] = back
    sums_ref[0:1, :] += gain_grad
    sums_ref[1:2, :] += shift_grad
    sums_ref[2:3, :] += jnp.sum(back.astype(F32), axis=0, keepdims=True)


def output_kernel(tokens_ref, three_ref, weight_ref, vec_ref, output_ref):
    product = dot(three_ref[...], weight_ref[...])
    output_ref[...] = (tokens_ref[...].astype(F32) + product + vec_ref[2:3, :]).astype(BF16)


def place_rows(me_ref, held, tiles):
    for core in range(CORES):
        for place in range(PLANE):
            step = me_ref[1] ^ place
            number = step if core else 2 * (step & 1) + (step >> 1)
            held[me_ref[0] ^ core, number] = tiles[core][place]


def grad_out_kernel(me_ref, three_ref, cot_ref, keep_ref, send_ref, sum_ref, held):
    cot = cot_ref[...]
    grad = dot(three_ref[...], cot, TN).astype(BF16)
    quarter = H // PIECES
    tiles = [
        [grad[(core * PLANE + place) * quarter : (core * PLANE + place + 1) * quarter] for place in range(PLANE)]
        for core in range(CORES)
    ]
    place_rows(me_ref, held, tiles)
    keep_ref[...] = held[0]
    send_ref[...] = held[1]
    sum_ref[...] = jnp.broadcast_to(jnp.sum(cot.astype(F32), axis=0, keepdims=True), sum_ref.shape)


def back_first_kernel(
    me_ref, mask_ref, vec_ref, normal_ref, slope_ref, scale_ref, local_ref, left_ref, right_ref, *refs
):
    pieces, outs, (held, sems, ext, ext_sems) = refs[:PAIRS], refs[PAIRS:-4], refs[-4:]
    back_ref, sums_ref = outs
    start_conv(me_ref, pieces, held, sems, ext, local_ref, left_ref, right_ref, ext_sems)

    @pl.when(pl.program_id(0) == 0)
    def _():
        sums_ref[...] = jnp.zeros_like(sums_ref)

    rows = mask_ref.shape[0]
    total = None
    for tap in range(TAPS):
        start = pl.program_id(0) * rows + tap * DILATION
        term = dot(masked_tap(mask_ref, ext, start, rows, tap), tap_weight(held, TAPS - 1 - tap), NT)
        total = term if total is None else total + term
    back_two = total.astype(BF16).astype(F32)
    grad, gain_grad, shift_grad = front_back(
        back_two, vec_ref[1:2, :], normal_ref[...].astype(F32), slope_ref[...].astype(F32), scale_ref[...]
    )
    back = grad.astype(BF16)
    back_ref[...] = back
    sums_ref[0:1, :] += gain_grad
    sums_ref[1:2, :] += shift_grad
    sums_ref[2:3, :] += jnp.sum(back.astype(F32), axis=0, keepdims=True)


def grad_in_kernel(nz, me_ref, one_ref, back_ref, keep_ref, send_ref, grad_ref, held):
    for start in range(0, H, 256):
        width = min(256, H - start)
        grad_ref[:, start : start + width] = dot(one_ref[...], back_ref[:, start : start + width], TN)
    part = D // PIECES // nz
    tiles = []
    for core in range(CORES):
        tiles.append([])
        for place in range(PLANE):
            rows = []
            for line in range(nz):
                first = ((line * PLANE + place) * CORES + core) * part
                rows.append(grad_ref[first : first + part, :])
            tiles[core].append(jnp.concatenate(rows, axis=0).astype(BF16))
    place_rows(me_ref, held, tiles)
    keep_ref[...] = held[0]
    send_ref[...] = held[1]


def grad_conv_kernel(me_ref, mask_ref, back_ref, local_ref, left_ref, right_ref, keep_ref, send_ref, held, ext, ext_sems):
    tap = pl.program_id(0)

    @pl.when(tap == 0)
    def _():
        for copy in fill_ext(ext, local_ref, left_ref, right_ref, ext_sems):
            copy.wait()

    rows = back_ref.shape[0]
    values = ext[pl.ds(pl.multiple_of(tap * DILATION, DILATION), rows), :]
    column = lax.broadcasted_iota(jnp.int32, mask_ref.shape, 1)
    mask = jnp.sum(jnp.where(column == tap, mask_ref[...], 0.0), axis=1, keepdims=True)
    values = values * mask.astype(BF16)
    grad = dot(values, back_ref[...], TN).astype(BF16)
    quarter = H // PIECES
    tiles = [
        [grad[(core * PLANE + place) * quarter : (core * PLANE + place + 1) * quarter] for place in range(PLANE)]
        for core in range(CORES)
    ]
    place_rows(me_ref, held, tiles)
    keep_ref[:, 0] = held[0]
    send_ref[:, 0] = held[1]


def vec_kernel(order_ref, one_ref, cot_ref, two_ref, three_ref, out_ref):
    for number, row in enumerate([one_ref[0:1, :], one_ref[1:2, :], cot_ref[0:1, :]]):
        out_ref[2 * number : 2 * number + 1, :] = row[:, :H]
        out_ref[2 * number + 1 : 2 * number + 2, :] = row[:, H:]
    hidden = jnp.concatenate([two_ref[...], three_ref[...]], axis=0)
    natural = exact_dot(hidden, order_ref[...], NT)
    for number, row in enumerate([2, 0, 1, 10, 8, 9]):
        out_ref[6 + number : 7 + number, :] = natural[row : row + 1, :]


def input_grad_kernel(back_ref, weight_ref, vec_ref, normal_ref, slope_ref, scale_ref, cot_ref, grad_ref, sums_ref):
    @pl.when(pl.program_id(0) == 0)
    def _():
        sums_ref[...] = jnp.zeros_like(sums_ref)

    back_one = dot(back_ref[...], weight_ref[...], NT)
    grad, gain_grad, shift_grad = front_back(
        back_one, vec_ref[0:1, :], normal_ref[...].astype(F32), slope_ref[...].astype(F32), scale_ref[...]
    )
    grad_ref[...] = (cot_ref[...].astype(F32) + grad).astype(BF16)
    sums_ref[0:1, :] += gain_grad
    sums_ref[1:2, :] += shift_grad


def exact_dot(values, order, dims):
    result = 0.0
    for _ in range(3):
        low = values.astype(BF16)
        result = result + dot(low, order, dims)
        values = values - low.astype(F32)
    return result


def pack_in_kernel(w_in_ref, vec_ref, order_ref, packed_ref):
    rows = [dot(w_in_ref[...].astype(BF16), order_ref[...]), vec_ref[...]]
    left = packed_ref.shape[0] - sum(one.shape[0] for one in rows)
    packed_ref[...] = jnp.concatenate(rows + [jnp.zeros((left, H), F32)], axis=0).astype(BF16)


def pack_rest_kernel(w_conv_ref, w_out_ref, order_ref, packed_ref):
    taps = jnp.concatenate([w_conv_ref[tap] for tap in range(TAPS)], axis=0)
    products = [w_out_ref[:, unit * H : (unit + 1) * H] for unit in range(UNITS)]
    packed_ref[...] = jnp.concatenate([dot(taps.astype(BF16), order_ref[...])] + products, axis=0).astype(BF16)


def momenta_kernel(me_ref, mom_in_ref, mom_conv_ref, mom_out_ref, order_ref, *refs):
    out_refs, held = refs[:-1], refs[-1]
    ordered = jnp.concatenate([mom_in_ref[...]] + [mom_conv_ref[tap] for tap in range(TAPS)], axis=0)
    ordered = exact_dot(ordered, order_ref[...], NN)
    rows, part = mom_in_ref.shape[0], mom_conv_ref.shape[1]
    taps = [ordered[rows + tap * part : rows + (tap + 1) * part] for tap in range(TAPS)]
    products = [mom_out_ref[:, unit * H : (unit + 1) * H] for unit in range(UNITS)]
    units = [taps[0:2], [taps[2]] * 2, products, taps[3:5]]
    for slot in range(SLOTS):
        held[slot ^ me_ref[3]] = jnp.concatenate(units[slot] + [ordered[:rows]], axis=0)
    for step, out_ref in enumerate(out_refs):
        out_ref[...] = held[step]


def line_kernel(nz, widths, me_ref, *refs):
    shards, out_refs, held = refs[:nz], refs[nz:-1], refs[-1]
    for number in range(nz):
        held[number] = shards[number][...]
    blocks = [held[me_ref[2] ^ line].astype(F32) for line in range(nz)]
    start = 0
    for out_ref, (groups, rows) in zip(out_refs, widths):
        for group in range(groups):
            stop = start + rows
            joined = jnp.concatenate([block[start:stop] for block in blocks], axis=0).astype(out_ref.dtype)
            if groups == 1:
                out_ref[...] = joined
            else:
                out_ref[group] = joined
            start = stop


def line_in_kernel(nz, rows, me_ref, *refs):
    shards, out_ref, held = refs[:nz], refs[nz], refs[nz + 1]
    for number in range(nz):
        held[number] = shards[number][...]
    blocks = [held[me_ref[2] ^ line].astype(F32) for line in range(nz)]
    joined = [block[:rows] for block in blocks] + [block[rows : rows + 1] for block in blocks]
    left = out_ref.shape[0] - nz * (rows + 1)
    if left:
        joined.append(jnp.zeros((left, H), F32))
    out_ref[...] = jnp.concatenate(joined, axis=0).astype(BF16)


def units_kernel(me_ref, *refs):
    conv_refs, product_refs, (keep_ref, send_ref, held) = refs[:4], refs[4:8], refs[8:]

    def total(parts):
        return functools.reduce(jnp.add, [part.astype(F32) for part in parts]).astype(BF16)

    def tap(number):
        return total([ref[0, number] for ref in conv_refs[:3]] + [conv_refs[3][number]])

    product = total([ref[0] for ref in product_refs[:3]] + [product_refs[3][...]])
    units = [[tap(0), tap(1)], [tap(2)] * 2, [product[:, :H], product[:, H:]], [tap(3), tap(4)]]
    for slot in range(SLOTS):
        for unit in range(UNITS):
            held[slot ^ me_ref[3], unit] = units[slot][unit]
    for number in range(SLOTS // 2):
        keep_ref[number] = held[2 * number]
        send_ref[number] = held[2 * number + 1]


def spread(nz, me_ref, values, out_refs, held):
    natural = values[...].astype(F32)
    sizes = [H // PIECES] * UNITS + [D // PIECES]
    for line in range(nz):
        start, parts = 0, []
        for size in sizes:
            part = size // nz
            parts.append(natural[start + line * part : start + (line + 1) * part])
            start += size
        held[line] = jnp.concatenate(parts, axis=0).astype(BF16)
    for step, out_ref in enumerate(out_refs):
        out_ref[...] = held[me_ref[2] ^ step]


def spread_sums_kernel(nz, me_ref, units_ref, in_ref, *refs):
    out_refs, (held, values) = refs[:-2], refs[-2:]
    rows = units_ref.shape[1]
    for unit in range(UNITS):
        values[unit * rows : (unit + 1) * rows, :] = units_ref[unit].astype(BF16)
    values[UNITS * rows :, :] = in_ref[...].astype(BF16)
    spread(nz, me_ref, values, out_refs, held)


def spread_results_kernel(nz, me_ref, mine_ref, other_ref, *refs):
    out_refs, (held, values) = refs[:-2], refs[-2:]
    rows = H // PIECES
    for unit in range(UNITS):
        place = slice(unit * rows, (unit + 1) * rows)
        mine = (me_ref[3] == SLOT_OUT) | (me_ref[0] == unit)
        values[place, :] = jnp.where(mine, mine_ref[place, :], other_ref[0:rows, :])
    values[UNITS * rows :, :] = jnp.where(me_ref[0] == 0, mine_ref[UNITS * rows :, :], other_ref[rows:, :])
    spread(nz, me_ref, values, out_refs, held)


def rows_of(me_ref, order_ref, shards, held, part):
    for number in range(SLOTS):
        held[number] = shards[number][...]
    slots = [held[slot ^ me_ref[3]] for slot in range(SLOTS)]
    natural = [None if slot == SLOT_OUT else dot(slots[slot], order_ref[...], NT) for slot in range(SLOTS)]
    taps = [natural[slot][unit * part : (unit + 1) * part] for slot, unit in TAP_UNITS]
    products = [slots[SLOT_OUT].astype(F32)[unit * part : (unit + 1) * part] for unit in range(UNITS)]
    return natural[SLOT_IN][UNITS * part :], taps, products


def finish_sums_kernel(me_ref, order_ref, *refs):
    shards, (mom_in, mom_conv, mom_out), rest = refs[:SLOTS], refs[SLOTS : SLOTS + 3], refs[SLOTS + 3 :]
    sum_in, sum_conv, sum_out, new_in, new_conv, new_out, held = rest
    rows, taps, products = rows_of(me_ref, order_ref, shards, held, mom_out.shape[0])
    sum_in[...] = rows
    new_in[...] = MOMENTUM * mom_in[...] + rows
    for tap in range(TAPS):
        sum_conv[tap] = taps[tap]
        new_conv[tap] = MOMENTUM * mom_conv[tap] + taps[tap]
    for unit in range(UNITS):
        columns = slice(unit * H, (unit + 1) * H)
        sum_out[:, columns] = products[unit]
        new_out[:, columns] = MOMENTUM * mom_out[:, columns] + products[unit]


def finish_results_kernel(me_ref, order_ref, *refs):
    shards, (w_in, w_conv, w_out), rest = refs[:SLOTS], refs[SLOTS : SLOTS + 3], refs[SLOTS + 3 :]
    new_in, new_conv, new_out, held = rest
    rows, taps, products = rows_of(me_ref, order_ref, shards, held, w_out.shape[0])
    new_in[...] = w_in[...] - MUON_RATE * rows
    for tap in range(TAPS):
        new_conv[tap] = w_conv[tap] - MUON_RATE * taps[tap]
    for unit in range(UNITS):
        columns = slice(unit * H, (unit + 1) * H)
        new_out[:, columns] = w_out[:, columns] - MUON_RATE * products[unit]


def normalized(x_ref, low_ref):
    square = jnp.sum(x_ref[...] * x_ref[...])
    factor = 1.0 / (jnp.sqrt(square) + 1e-07)
    x_ref[...] = x_ref[...] * factor
    low_ref[...] = x_ref[...].astype(BF16)
    return square * factor * factor


def polynomial(shift, low_ref, gram_ref, poly_ref):
    size = gram_ref.shape[0]
    for start in range(0, size, 256):
        span = min(256, size - start)
        gram = dot(low_ref[...], low_ref[start : start + span, :], NT)
        row = lax.broadcasted_iota(jnp.int32, (size, span), 0)
        column = lax.broadcasted_iota(jnp.int32, (size, span), 1) + start
        gram_ref[:, start : start + span] = gram - jnp.where(row == column, shift, 0.0)
    gram_low = gram_ref[...].astype(BF16)
    linear = COEF_B + 2.0 * COEF_C * shift
    for start in range(0, size, 256):
        span = min(256, size - start)
        squared = dot(gram_low, gram_low[:, start : start + span])
        poly_ref[:, start : start + span] = (
            linear * gram_ref[:, start : start + span] + COEF_C * squared
        ).astype(BF16)
    return COEF_A + COEF_B * shift + COEF_C * shift * shift


def update(coefficient, x_ref, low_ref, poly_ref):
    square = jnp.zeros((), F32)
    for start in range(0, x_ref.shape[1], 256):
        span = min(256, x_ref.shape[1] - start)
        fresh = coefficient * x_ref[:, start : start + span] + dot(poly_ref[...], low_ref[:, start : start + span])
        square = square + jnp.sum(fresh * fresh)
        x_ref[:, start : start + span] = fresh
    low_ref[...] = x_ref[...].astype(BF16)
    return square


def newton_schulz_loop(x_ref, low_ref, gram_ref, poly_ref):
    def step(_, square):
        coefficient = polynomial(square * (1.0 / x_ref.shape[0]), low_ref, gram_ref, poly_ref)
        return update(coefficient, x_ref, low_ref, poly_ref)

    lax.fori_loop(0, NS_STEPS, step, normalized(x_ref, low_ref))


def newton_schulz(x_ref, low_ref, gram_ref, poly_ref, own):
    square = normalized(x_ref, low_ref)
    for step in range(NS_STEPS):
        coefficient = polynomial(square * (1.0 / x_ref.shape[0]), low_ref, gram_ref, poly_ref)
        if step < NS_STEPS - 1:
            square = update(coefficient, x_ref, low_ref, poly_ref)
    own(coefficient)


def orth_kernel(me_ref, *refs):
    in_pieces, unit_pieces = refs[:PAIRS], refs[PAIRS : 2 * PAIRS]
    mine_ref, other_ref = refs[2 * PAIRS : 2 * PAIRS + 2]
    held, x_ref, low_ref, wide_ref, wide_low_ref, gram_ref, poly_ref = refs[2 * PAIRS + 2 :]
    slot, core = me_ref[3], me_ref[0]
    is_in = (slot == SLOT_IN) & (core == 0)
    is_out = slot == SLOT_OUT
    places = [(pair, one) for pair in range(PAIRS) for one in range(2)]

    @pl.when(is_out)
    def _():
        rows = H // PIECES
        for number, (pair, one) in enumerate(places):
            for unit in range(UNITS):
                wide_ref[number * rows : (number + 1) * rows, unit * H : (unit + 1) * H] = unit_pieces[pair][
                    one, unit
                ].astype(F32)

    @pl.when(is_in)
    def _():
        rows = D // PIECES
        for number, (pair, one) in enumerate(places):
            held[number * rows : (number + 1) * rows, :] = in_pieces[pair][one].astype(F32)
        for start in range(0, D, 256):
            wide_ref[:, start : start + 256] = held[start : start + 256, :].T

    @pl.when(is_in | is_out)
    def _():
        def own(coefficient):
            @pl.when(is_out)
            def _():
                rows = H // PIECES
                fresh = coefficient * wide_ref[0:rows, :] + dot(poly_ref[0:rows, :], wide_low_ref[...])
                for unit in range(UNITS):
                    mine_ref[unit * rows : (unit + 1) * rows, :] = fresh[:, unit * H : (unit + 1) * H].astype(BF16)

            @pl.when(is_in)
            def _():
                rows = D // PIECES
                for out_ref, start in ((mine_ref, 0), (other_ref, PLANE * rows)):
                    columns = slice(start, start + 256)
                    fresh = coefficient * wide_ref[:, columns] + dot(poly_ref[...], wide_low_ref[:, columns])
                    out_ref[out_ref.shape[0] - rows :, :] = fresh.T[0:rows].astype(BF16)

        newton_schulz(wide_ref, wide_low_ref, gram_ref, poly_ref, own)

    @pl.when(jnp.logical_not(is_in | is_out))
    def _():
        rows = H // PIECES
        for number, (pair, one) in enumerate(places):
            x_ref[number * rows : (number + 1) * rows, :] = unit_pieces[pair][one, core].astype(F32)

        newton_schulz_loop(x_ref, low_ref, gram_ref, poly_ref)
        mine_ref[pl.ds(pl.multiple_of(core * rows, 16), rows), :] = x_ref[0:rows, :].astype(BF16)
        other_ref[0:rows, :] = x_ref[PLANE * rows : (PLANE + 1) * rows, :].astype(BF16)


class Layout:
    def __init__(self, count):
        self.count = count
        self.lines = count // PIECES
        self.part = H // count
        places = np.arange(H)
        row = places % self.part
        line = places // self.part % self.lines
        plane = places // (self.part * self.lines) % PLANE
        core = places // (self.part * self.lines * PLANE)
        self.natural = ((line * PLANE + plane) * CORES + core) * self.part + row

    def swap(self, values, mask, keep=lambda source, target: True):
        pairs = [(one, one ^ mask) for one in range(self.count)]
        pairs = [pair for pair in pairs if keep(pair[0] // PIECES % SLOTS, pair[1] // PIECES % SLOTS)]
        return lax.ppermute(values, "seq", pairs)

    def swap_line(self, values, step, keep=lambda source, target: True):
        return self.swap(values, step * PIECES, keep)

    def swap_plane(self, values, step, keep=lambda source, target: True):
        pairs = [(one, one ^ (2 if one % CORES == step else 4)) for one in range(self.count)]
        pairs = [pair for pair in pairs if keep(pair[0] // PIECES % SLOTS, pair[1] // PIECES % SLOTS)]
        return lax.ppermute(values, "seq", pairs)

    def along_line(self, values):
        return [values] + [self.swap_line(values, step) for step in range(1, self.lines)]

    def to_all(self, values, keep=lambda source, target: True):
        pair = jnp.stack([values, self.swap_plane(values, 0, keep)])
        far = self.swap_plane(pair, 1, keep)
        return [pair, far, self.swap(pair, 1, keep), self.swap(far, 1, keep)]


def add(*terms):
    return functools.reduce(jnp.add, [term.astype(F32) for term in terms])


def front_outs(rows, width):
    return [shape((rows, width), BF16)] * 3 + [shape((rows, 1), F32)]


def late_spec(rows, width):
    return pl.BlockSpec((rows, width), lambda i: (jnp.maximum(i - 2, 0), 0))


def late_out_specs(rows, width):
    return [late_spec(rows, width)] * 3 + [late_spec(rows, 1)]


def front_out_specs(rows, width):
    return [rows_spec(rows, width)] * 3 + [rows_spec(rows, 1)]


def body(
    count,
    tokens,
    cotangent,
    protein_lengths,
    w_in,
    w_conv,
    w_out,
    vectors,
    mom_in,
    mom_conv,
    mom_out,
    vec_mean,
    vec_square,
):
    lay = Layout(count)
    index = lax.axis_index("seq")
    line_index = index // PIECES
    rows = tokens.shape[0]
    me = jnp.stack(
        [index & 1, (index >> 1) & (PLANE - 1), line_index, line_index % SLOTS, index * rows]
    ).astype(jnp.int32)
    block = 256
    grid = (rows // block,)
    quarter = H // PIECES
    piece_in = D // PIECES
    to_order = jnp.asarray(np.arange(H)[:, None] == lay.natural[None, :], BF16)

    def order_low(values):
        return jnp.dot(values, to_order, preferred_element_type=F32).astype(BF16)

    row_ends = jnp.cumsum(protein_lengths, axis=1) + jnp.arange(protein_lengths.shape[0], dtype=jnp.int32)[:, None] * LEN
    mask_rows = call(
        mask_kernel, 2.0, out_shape=shape((rows, 8), F32), in_specs=[SMEM, VMEM], out_specs=VMEM
    )(me, row_ends.reshape(1, -1))

    edges = [one for one in range(count - 1) if (one + 1) * rows % LEN != 0]
    to_next = [(one, one + 1) for one in edges]
    to_previous = [(one + 1, one) for one in edges]

    part = lay.part
    line = line_index

    def join(shards, widths, outs):
        return call(
            functools.partial(line_kernel, lay.lines, widths),
            2.0,
            out_shape=outs,
            in_specs=[SMEM] + [VMEM] * lay.lines,
            out_specs=[VMEM] * len(outs),
            scratch_shapes=[pltpu.VMEM((lay.lines,) + shards[0].shape, shards[0].dtype)],
        )(me, *shards)

    in_rows = D // count
    shard_rows = UNITS * part + in_rows
    width = vectors.shape[0]
    packed_in = call(
        pack_in_kernel,
        1.0,
        out_shape=shape((-(-(in_rows + 1) // 16) * 16, H), BF16),
        in_specs=[VMEM] * 3,
        out_specs=VMEM,
    )(w_in, jnp.pad(vectors, (0, H - width)).reshape(1, H), to_order)
    packed_in, to_right = tie(packed_in, tokens[rows - HALO :])
    line_in = lay.along_line(packed_in)
    packed = call(
        pack_rest_kernel,
        2.0,
        out_shape=shape(((TAPS + UNITS) * part, H), BF16),
        in_specs=[VMEM] * 3,
        out_specs=VMEM,
    )(w_conv, w_out, to_order)
    packed_line = lay.along_line(packed)
    mom_blocks = list(call(
        momenta_kernel,
        2.0,
        out_shape=[shape((shard_rows, H), F32)] * SLOTS,
        in_specs=[SMEM] + [VMEM] * 4,
        out_specs=[VMEM] * SLOTS,
        scratch_shapes=[pltpu.VMEM((SLOTS, shard_rows, H), F32)],
    )(me, mom_in, mom_conv, mom_out, to_order))
    in_own = call(
        functools.partial(line_in_kernel, lay.lines, in_rows),
        2.0,
        out_shape=shape((piece_in + 16, H), BF16),
        in_specs=[SMEM] + [VMEM] * lay.lines,
        out_specs=VMEM,
        scratch_shapes=[pltpu.VMEM((lay.lines,) + packed_in.shape, BF16)],
    )(me, *line_in)
    in_near = lay.swap_plane(in_own, 0)
    token_left, to_left = tie(lax.ppermute(to_right, "seq", to_next), tokens[:HALO])
    token_right = lax.ppermute(to_left, "seq", to_previous)
    in_near, mask_rows, mom_blocks[0], *packed_line[1:] = tie(in_near, mask_rows, mom_blocks[0], *packed_line[1:])
    in_pair = jnp.stack([in_own, in_near])
    in_far = lay.swap_plane(in_pair, 1)
    late_in_pair, packed_line[0] = tie(in_pair, packed_line[0])
    conv_own, out_own = join(
        packed_line,
        [(TAPS, part), (UNITS, part)],
        [shape((TAPS, quarter, H), BF16), shape((UNITS, quarter, H), BF16)],
    )
    conv_near = lay.swap_plane(conv_own, 0)
    in_far, conv_own, token_left, token_right = tie(in_far, conv_own, token_left, token_right)
    in_pieces = [late_in_pair, in_far, lay.swap(late_in_pair, 1), lay.swap(in_far, 1)]

    vec_rows = jnp.concatenate([piece[:, piece_in:] for piece in in_pieces]).reshape(-1, H)
    number = jnp.arange(vec_rows.shape[0], dtype=jnp.int32)
    from_core = me[0] ^ (number // (PLANE * 16))
    step = number // 16 % PLANE
    from_plane = me[1] ^ jnp.where(step == 1, 1 + from_core, jnp.where(step == 2, 2 - from_core, step))
    from_index = number % 16 * PIECES + from_plane * CORES + from_core
    pick = (jnp.arange(count, dtype=jnp.int32)[:, None] == from_index[None, :]).astype(BF16)
    vec_all = jnp.dot(pick, vec_rows, preferred_element_type=F32)[:, :width].reshape(-1)
    vec_d = vec_all[: 3 * D].reshape(3, D)
    vec_h = order_low(vec_all[3 * D :].reshape(6, H).astype(BF16)).astype(F32)

    one_halo = call(
        front_halo_kernel,
        5.0,
        grid=(2,),
        out_shape=shape((2 * HALO, D), BF16),
        in_specs=[whole_spec(HALO, D), whole_spec(HALO, D), whole_spec(3, D)],
        out_specs=rows_spec(HALO, D),
    )(token_left, token_right, vec_d)
    conv_near, one_halo = tie(conv_near, one_halo)
    conv_pair = jnp.stack([conv_own, conv_near])
    conv_far = lay.swap_plane(conv_pair, 1)
    late_conv_pair, late_tokens, mom_blocks[1] = tie(conv_pair, tokens, mom_blocks[1])
    mom_lines = [mom_blocks[0]] + [lay.swap_line(mom_blocks[step % SLOTS], step) for step in range(1, lay.lines)]
    one_low, normal_one, slope_one, scale_one = call(
        front_one_kernel,
        6.0,
        grid=grid,
        out_shape=front_outs(rows, D),
        in_specs=[rows_spec(block, D), whole_spec(3, D)],
        out_specs=front_out_specs(block, D),
    )(late_tokens, vec_d)
    one_low, out_own = tie(one_low, out_own)
    out_near = lay.swap_plane(out_own, 0)
    in_low, two_low, normal_two, slope_two, scale_two, two_left, two_right = call(
        functools.partial(first_kernel, lay.lines),
        11.0,
        grid=(2 + rows // block,),
        out_shape=[shape((D, H), BF16)] + front_outs(rows, H) + [shape((HALO, H), BF16)] * 2,
        in_specs=[
            SMEM,
            late_spec(block, D),
            pl.BlockSpec((HALO, D), lambda i: (jnp.minimum(i, 1), 0)),
            whole_spec(6, H),
        ]
        + [ANY] * PAIRS,
        out_specs=[whole_spec(D, H)] + late_out_specs(block, H) + [whole_spec(HALO, H)] * 2,
        scratch_shapes=[pltpu.VMEM((CORES, PLANE, piece_in, H), BF16), pltpu.SemaphoreType.DMA((PIECES,))],
    )(me, one_low, one_halo, vec_h, *in_pieces)
    conv_far, out_near, two_low, *mom_lines[1:] = tie(conv_far, out_near, two_low, *mom_lines[1:])
    conv_pieces = [late_conv_pair, conv_far, lay.swap(late_conv_pair, 1), lay.swap(conv_far, 1)]
    out_pair = jnp.stack([out_own, out_near])
    out_far = lay.swap_plane(out_pair, 1)
    conv_pieces[3], late_out_pair = tie(conv_pieces[3], out_pair)
    conv_scratch = [
        pltpu.VMEM((CORES, PLANE, TAPS, quarter, H), BF16),
        pltpu.SemaphoreType.DMA((PIECES,)),
        pltpu.VMEM((rows + 2 * HALO, H), BF16),
        pltpu.SemaphoreType.DMA((3,)),
    ]
    three_low, normal_three, slope_three, scale_three = call(
        second_kernel,
        11.0,
        grid=grid,
        out_shape=front_outs(rows, H),
        in_specs=[SMEM, rows_spec(block, 8), whole_spec(6, H)] + [ANY] * (3 + PAIRS),
        out_specs=front_out_specs(block, H),
        scratch_shapes=conv_scratch,
    )(me, mask_rows, vec_h, two_low, two_left, two_right, *conv_pieces)

    three_low, out_far = tie(three_low, out_far)
    out_pieces = [late_out_pair, out_far, lay.swap(late_out_pair, 1), lay.swap(out_far, 1)]

    keep_out, send_out, sum_cot = call(
        grad_out_kernel,
        5.0,
        grid=(D // 256,),
        out_shape=[shape((PLANE, quarter, D), BF16)] * 2 + [shape((8, D), F32)],
        in_specs=[SMEM, whole_spec(rows, H), pl.BlockSpec((rows, 256), lambda i: (0, i))],
        out_specs=[pl.BlockSpec((PLANE, quarter, 256), lambda i: (0, 0, i))] * 2 + [pl.BlockSpec((8, 256), lambda i: (0, i))],
        scratch_shapes=[pltpu.VMEM((CORES, PLANE, quarter, 256), BF16)],
    )(me, three_low, cotangent)
    late_cotangent, keep_out = tie(cotangent, keep_out)
    out_low, back_second, sums_three = call(
        back_second_kernel,
        9.0,
        grid=grid,
        out_shape=[shape((H, D), BF16), shape((rows, H), BF16), shape((8, H), F32)],
        in_specs=[SMEM, rows_spec(block, D), whole_spec(6, H), rows_spec(block, H), rows_spec(block, H), rows_spec(block, 1)]
        + [ANY] * PAIRS,
        out_specs=[whole_spec(H, D), rows_spec(block, H), whole_spec(8, H)],
        scratch_shapes=[pltpu.VMEM((CORES, PLANE, UNITS, quarter, H), BF16), pltpu.SemaphoreType.DMA((PIECES,))],
    )(me, late_cotangent, vec_h, normal_three, slope_three, scale_three, *out_pieces)
    back_left = lax.ppermute(back_second[rows - HALO :], "seq", to_next)
    back_right = lax.ppermute(back_second[:HALO], "seq", to_previous)
    other_out, late_second = tie(lay.swap(send_out, 1), back_second)
    half_out, late_second = tie(add(keep_out[2:], other_out[2:]).astype(BF16), late_second)
    near_out = lay.swap_plane(half_out, 0)
    keep_conv, send_conv = call(
        grad_conv_kernel,
        8.0,
        grid=(TAPS,),
        out_shape=[shape((PLANE, TAPS, quarter, H), BF16)] * 2,
        in_specs=[SMEM, whole_spec(rows, 8), whole_spec(rows, H)] + [ANY] * 3,
        out_specs=[pl.BlockSpec((PLANE, 1, quarter, H), lambda i: (0, i, 0, 0))] * 2,
        scratch_shapes=[
            pltpu.VMEM((CORES, PLANE, quarter, H), BF16),
            pltpu.VMEM((rows + 2 * HALO, H), BF16),
            pltpu.SemaphoreType.DMA((3,)),
        ],
    )(me, mask_rows, late_second, two_low, two_left, two_right)
    near_out, back_left, back_right, keep_conv, send_conv, late_tokens = tie(
        near_out, back_left, back_right, keep_conv, send_conv, tokens
    )
    far_out = lay.swap_plane(add(keep_out[1], other_out[1], near_out[1]).astype(BF16), 1)
    output = call(
        output_kernel,
        5.0,
        grid=grid,
        out_shape=shape((rows, D), BF16),
        in_specs=[rows_spec(block, D), rows_spec(block, H), whole_spec(H, D), whole_spec(3, D)],
        out_specs=rows_spec(block, D),
    )(late_tokens, three_low, out_low, vec_d)
    other_conv, output = tie(lay.swap(send_conv, 1), output)
    half_conv, late_second = tie(add(keep_conv[2:], other_conv[2:]).astype(BF16), late_second)
    near_conv = lay.swap_plane(half_conv, 0)
    back_first, sums_two = call(
        back_first_kernel,
        10.0,
        grid=grid,
        out_shape=[shape((rows, H), BF16), shape((8, H), F32)],
        in_specs=[SMEM, rows_spec(block, 8), whole_spec(6, H), rows_spec(block, H), rows_spec(block, H), rows_spec(block, 1)]
        + [ANY] * (3 + PAIRS),
        out_specs=[rows_spec(block, H), whole_spec(8, H)],
        scratch_shapes=conv_scratch,
    )(
        me,
        mask_rows,
        vec_h,
        normal_two,
        slope_two,
        scale_two,
        late_second,
        back_left,
        back_right,
        *conv_pieces,
    )
    back_first, mom_lines[0] = tie(back_first, mom_lines[0])
    mom_unit_pieces, mom_in_piece = join(
        mom_lines,
        [(UNITS, part), (1, in_rows)],
        [shape((UNITS, quarter, H), F32), shape((piece_in, H), F32)],
    )
    near_conv, far_out, back_first, mom_unit_pieces = tie(near_conv, far_out, back_first, mom_unit_pieces)
    piece_conv, back_first = tie(add(keep_conv[1], other_conv[1], near_conv[1]).astype(BF16), back_first)
    far_conv = lay.swap_plane(piece_conv, 1)
    keep_in, send_in = call(
        functools.partial(grad_in_kernel, lay.lines),
        6.0,
        out_shape=[shape((PLANE, piece_in, H), BF16)] * 2,
        in_specs=[SMEM, VMEM, VMEM],
        out_specs=[VMEM] * 2,
        scratch_shapes=[pltpu.VMEM((D, H), F32), pltpu.VMEM((CORES, PLANE, piece_in, H), BF16)],
    )(me, one_low, back_first)
    far_conv, keep_in, send_in = tie(far_conv, keep_in, send_in)
    other_in = lay.swap(send_in, 1)
    lines = lay.lines
    conv_block, out_block = whole_spec(1, TAPS, quarter, H), whole_spec(1, quarter, D)
    unit_keep, unit_send = call(
        units_kernel,
        3.0,
        grid=(1,),
        out_shape=[shape((SLOTS // 2, UNITS, quarter, H), BF16)] * 2,
        in_specs=[SMEM] + [conv_block] * 3 + [whole_spec(TAPS, quarter, H)] + [out_block] * 3 + [whole_spec(quarter, D)],
        out_specs=[whole_spec(SLOTS // 2, UNITS, quarter, H)] * 2,
        scratch_shapes=[pltpu.VMEM((SLOTS, UNITS, quarter, H), BF16)],
    )(me, keep_conv, other_conv, near_conv, far_conv, keep_out, other_out, near_out, far_out)
    unit_near = lay.swap_line(unit_send, 1)
    other_in, unit_keep = tie(other_in, unit_keep)
    half_in, late_first = tie(add(keep_in[2:], other_in[2:]).astype(BF16), back_first)
    near_in = lay.swap_plane(half_in, 0)
    input_grad, sums_one = call(
        input_grad_kernel,
        8.0,
        grid=grid,
        out_shape=[shape((rows, D), BF16), shape((8, D), F32)],
        in_specs=[
            rows_spec(block, H),
            whole_spec(D, H),
            whole_spec(3, D),
            rows_spec(block, D),
            rows_spec(block, D),
            rows_spec(block, 1),
            rows_spec(block, D),
        ],
        out_specs=[rows_spec(block, D), whole_spec(8, D)],
    )(late_first, in_low, vec_d, normal_one, slope_one, scale_one, cotangent)
    near_in, input_grad = tie(near_in, input_grad)
    piece_in_sum, sums_one = tie(add(keep_in[1], other_in[1], near_in[1]).astype(BF16), sums_one)
    far_in = lay.swap_plane(piece_in_sum, 1)
    vec_terms = call(
        vec_kernel,
        1.0,
        out_shape=shape((6 + 6, H), F32),
        in_specs=[VMEM] * 5,
        out_specs=VMEM,
    )(to_order, sums_one, sum_cot, sums_two, sums_three)
    unit_half = add(unit_keep, unit_near)
    for step in range(SLOTS, lines):
        if step & (step - 1) == 0:
            unit_half = add(unit_half, lay.swap_line(unit_half.astype(BF16), step))
    far_in, vec_terms, unit_low = tie(far_in, vec_terms, unit_half[1].astype(BF16))
    unit_far = lay.swap_line(unit_low, 2)
    in_sum = add(keep_in[0], other_in[0], near_in[0], far_in)
    for step in range(SLOTS, lines):
        if step & (step - 1) == 0:
            in_sum = add(in_sum, lay.swap_line(in_sum.astype(BF16), step))
    in_slot = lambda source, target: target == SLOT_IN
    in_parts = [lay.swap_line(in_sum.astype(BF16), step, in_slot) for step in range(1, SLOTS)]
    in_sum = add(in_sum, *in_parts)
    in_moment = (MOMENTUM * mom_in_piece + in_sum).astype(BF16)
    vec_sums = vec_terms + lay.swap(vec_terms, 1)
    vec_sums = vec_sums + lay.swap_plane(vec_sums, 0)
    unit_far, vec_sums = tie(unit_far, vec_sums)
    unit_sum = add(unit_half[0], unit_far)
    unit_moment = (MOMENTUM * mom_unit_pieces + unit_sum).astype(BF16)

    def orth_scratch(width):
        return [pltpu.VMEM((H, width), F32), pltpu.VMEM((H, width), BF16)]

    vec_sums = vec_sums + lay.swap_plane(vec_sums, 1)
    near, vec_sums = tie(lay.swap_plane(unit_moment, 0), vec_sums)
    unit_pair = jnp.stack([unit_moment, near])
    in_pieces_m = lay.to_all(in_moment, in_slot)
    line_scratch = [
        pltpu.VMEM((lines, shard_rows, H), BF16),
        pltpu.VMEM((UNITS * quarter + piece_in, H), BF16),
    ]

    def spread_line(kernel, *values):
        blocks = call(
            functools.partial(kernel, lines),
            3.0,
            out_shape=[shape((shard_rows, H), BF16)] * SLOTS,
            in_specs=[SMEM] + [VMEM] * len(values),
            out_specs=[VMEM] * SLOTS,
            scratch_shapes=line_scratch,
        )(me, *values)
        return blocks

    def to_line(blocks):
        return [blocks[0]] + [lay.swap_line(blocks[step], step) for step in range(1, SLOTS)]

    sum_shards = to_line(spread_line(spread_sums_kernel, unit_sum, in_sum))
    vec_sums = vec_sums + lay.swap_line(vec_sums, 1)
    unit_far, vec_sums, *sum_shards[1:] = tie(lay.swap_plane(unit_pair, 1), vec_sums, *sum_shards[1:])
    unit_pieces_m = [unit_pair, unit_far, lay.swap(unit_pair, 1), lay.swap(unit_far, 1)]
    mine, other = call(
        orth_kernel,
        21.0,
        out_shape=[shape((UNITS * quarter + piece_in, H), BF16), shape((quarter + piece_in, H), BF16)],
        in_specs=[SMEM] + [VMEM] * (2 * PAIRS),
        out_specs=[VMEM] * 2,
        scratch_shapes=[pltpu.VMEM((D, H), F32)]
        + orth_scratch(H)
        + orth_scratch(D)
        + [pltpu.VMEM((H, H), F32), pltpu.VMEM((H, H), BF16)],
    )(me, *in_pieces_m, *unit_pieces_m)
    orth_blocks = spread_line(spread_results_kernel, mine, lay.swap(other, 1))
    orth_blocks = list(orth_blocks)
    orth_blocks[0], vec_sums = tie(orth_blocks[0], vec_sums)
    step = 2
    while step < lines:
        vec_sums = vec_sums + lay.swap_line(vec_sums, step)
        step *= 2
    orth_shards = to_line(orth_blocks)
    orth_shards[0], sum_shards[0] = tie(orth_shards[0], sum_shards[0])
    orth_shards[1], vec_sums = tie(orth_shards[1], vec_sums)
    sum_vec = lax.dynamic_slice_in_dim(vec_sums.reshape(-1), index * width, width)

    def finish(kernel, shards, *values, outs):
        return call(
            kernel,
            2.0,
            out_shape=[shape(one.shape, F32) for one in values] * outs,
            in_specs=[SMEM] + [VMEM] * (SLOTS + 4),
            out_specs=[VMEM] * (3 * outs),
            scratch_shapes=[pltpu.VMEM((SLOTS, shard_rows, H), BF16)],
        )(me, to_order, *shards, *values)

    sum_in, sum_conv, sum_out, moment_in, moment_conv, moment_out = finish(
        finish_sums_kernel, sum_shards, mom_in, mom_conv, mom_out, outs=2
    )
    new_in, new_conv, new_out = finish(finish_results_kernel, orth_shards, w_in, w_conv, w_out, outs=1)

    vec_mean_new = BETA_ONE * vec_mean + (1.0 - BETA_ONE) * sum_vec
    vec_square_new = BETA_TWO * vec_square + (1.0 - BETA_TWO) * sum_vec * sum_vec
    corrected_mean = vec_mean_new / (1.0 - BETA_ONE**STEP)
    corrected_square = vec_square_new / (1.0 - BETA_TWO**STEP)
    vec_new = vectors - ADAM_RATE * corrected_mean / (jnp.sqrt(corrected_square) + ADAM_EPS)
    return (
        output,
        input_grad,
        sum_in,
        sum_conv,
        sum_out,
        moment_in,
        moment_conv,
        moment_out,
        new_in,
        new_conv,
        new_out,
        sum_vec,
        vec_mean_new,
        vec_square_new,
        vec_new,
    )


def solution(mesh):
    matrix, taps, vector = P("seq", None), P(None, "seq", None), P("seq")
    return jax.shard_map(
        functools.partial(body, mesh.shape["seq"]),
        mesh=mesh,
        in_specs=(matrix, matrix, P(), matrix, taps, matrix, vector, matrix, taps, matrix, vector, vector),
        out_specs=(
            matrix,
            matrix,
            matrix,
            taps,
            matrix,
            matrix,
            taps,
            matrix,
            matrix,
            taps,
            matrix,
            vector,
            vector,
            vector,
            vector,
        ),
        check_vma=False,
    )
```
